32 devices in a mesh: row: 8 (over z, y), col: 4 (over x, core).
Axes of the slice: x: 2, y: 2, z: 4, core: 2. Of those that a mesh axis runs over, the one named last changes fastest.
Arguments:
- activations: bfloat16 [8192, 4096], P(('row', 'col')), may hold values from -6 to 6
- out_grads: bfloat16 [8192, 4096], P(('row', 'col')), may hold values from -6 to 6
- proj_in: bfloat16 [4096, 128], replicated, may hold values from -0.09375 to 0.09375
- proj_out: bfloat16 [4096, 128], replicated, may hold values from -0.09375 to 0.09375
- lengths: int32 [256], P(('row', 'col')), may hold values from 1 to 32, 6144 in all
- gram_old: float32 [16384, 16384], P('row', 'col'), as said below
- queries: float32 [16384, 256], P('row'), may hold values from -96 to 96
Outputs:
- gram_new: float32 [16384, 16384], P('row', 'col')
- solution: float32 [16384, 256], P('row')
The draws below stay inside these ranges and needn't reach their ends.
Inputs may be any that keep to these rules, and one draw needn't show every extreme that they name: `gram_old`: symmetric and positive definite. Example e's token slots from lengths[e] on are padding.
All inputs are finite; a program needn't handle non-finite values. No bound on the sum of `lengths` on one device may be relied on, other than what follows from the above.
Results may differ from the reference program's by a relative error of at most 0.0055.
Values may be sent and summed in bfloat16 or wider, within the bound.
No kernel may reach another device: no remote copies, remote signals or barrier semaphores. Data moves between devices by JAX's collectives and lax.ppermute only.
A program may use at most 192 MiB of HBM per device.

```python
import math
import jax
import jax.numpy as jnp
import numpy as np
from jax import lax

D = 4096
R = 128
SEQ = 32
ITERS = 2
NQ = 256
EXAMPLES = 256
TOKENS = 8192
FEAT = 16384


def draw_gram_old(key, part):
    order_size = R * R
    factor_count = R
    key_noise, key_levels, key_factor = jax.random.split(key, 3)
    entries = jax.random.normal(key_noise, (order_size, order_size), jnp.float32)
    levels = jnp.exp(jax.random.uniform(key_levels, (order_size,), jnp.float32, math.log(4.0), math.log(16.0)))
    factor = jax.random.normal(key_factor, (order_size, factor_count), jnp.float32)
    factor = factor * math.sqrt(8.0 / factor_count)
    coupled = jnp.dot(factor, factor.T, precision=lax.Precision.HIGHEST)
    coupled = 0.5 * (coupled + coupled.T)
    shared = (entries + entries.T) * 0.5 ** 0.5 / math.sqrt(order_size)
    return shared + coupled + jnp.diag(levels)


def level_of(stream_key, dims, cuts, least, top_value):
    loudness = 1.0
    for axis_at, parts in cuts:
        steps = jax.random.uniform(jax.random.fold_in(jax.random.fold_in(stream_key, 6), axis_at), (parts,), jnp.float32, least / len(cuts), top_value / len(cuts))
        loudness = loudness * jnp.repeat(jnp.exp(steps), dims[axis_at] // parts).reshape((-1,) + (1,) * (len(dims) - 1 - axis_at))
    return loudness


def length_profile(amount, total, bound, lean):
    loads = [(1 << 20) // math.isqrt(standing ** lean) + 1 for standing in range(2, amount + 1)]
    surplus, holding = total - bound - (amount - 1), [1] * (amount - 1)
    while surplus > 0:
        movable = [i for i in range(amount - 1) if holding[i] < bound]
        whole, budget = sum([loads[i] for i in movable]), surplus
        for i in movable:
            more = min(bound - holding[i], max(1, budget * loads[i] // whole), surplus)
            holding[i] = holding[i] + more
            surplus = surplus - more
    return np.array([bound] + holding)


def uneven_parts(key, amount, total, bound, slope):
    if amount == 2:
        one = jax.random.randint(key, (), max(1, total - bound), min(bound, total - 1) + 1)
        return jnp.stack([one, total - one])
    sizes = jnp.asarray(length_profile(amount, total, bound, slope), jnp.int32)
    twos = (amount - 1) // 2
    giver, taker = sizes[1:1 + 2 * twos:2], sizes[2:2 + 2 * twos:2]
    room = jnp.minimum(giver - 1, bound - taker)
    passed = jax.random.randint(jax.random.fold_in(key, 1), (twos,), 0, 1 << 20) % (room + 1)
    sizes = sizes.at[1:1 + 2 * twos:2].set(giver - passed).at[2:2 + 2 * twos:2].set(taker + passed)
    return sizes[jax.random.permutation(jax.random.fold_in(key, 2), amount)]


def scatter_about(key, dims, scale, bound, pieces=(), held_as=jnp.bfloat16):
    values = jax.random.normal(key, dims, jnp.float32) * scale
    if len(pieces) > 0:
        values = level_of(key, dims, pieces, -0.22, 0.18) * values
    return jnp.clip(values, min=-bound, max=bound).astype(held_as)


def setup_inputs(seed: int = 0) -> dict:
    streams_of = jax.random.split(jax.random.key(seed), 8)
    activations = scatter_about(streams_of[0], (TOKENS, D), 1.0, 6.0, ((0, 32),))
    out_grads = scatter_about(streams_of[1], (TOKENS, D), 1.0, 6.0, ((0, 32),))
    proj_in = scatter_about(streams_of[2], (D, R), D ** -0.5, 0.09375)
    proj_out = scatter_about(streams_of[3], (D, R), D ** -0.5, 0.09375)
    lengths = uneven_parts(streams_of[4], EXAMPLES, EXAMPLES * 24, SEQ, 1).astype(jnp.int32)
    gram_old = draw_gram_old(jax.random.fold_in(streams_of[7], 71), 0)
    queries = scatter_about(streams_of[6], (FEAT, NQ), 16.0, 96.0, ((0, 8),), jnp.float32)
    return dict(activations=activations, out_grads=out_grads, proj_in=proj_in, proj_out=proj_out, lengths=lengths, gram_old=gram_old, queries=queries)


decay_rate = 0.5
damping = 1.0


def reference(activations, out_grads, proj_in, proj_out, lengths, gram_old, queries):
    low_in = jnp.dot(activations, proj_in, preferred_element_type=jnp.float32).astype(jnp.bfloat16)
    low_out = jnp.dot(out_grads, proj_out, preferred_element_type=jnp.float32).astype(jnp.bfloat16)
    low_in = low_in.reshape(EXAMPLES, SEQ, R)
    low_out = low_out.reshape(EXAMPLES, SEQ, R)
    valid_mask = jnp.arange(SEQ)[None, :] < lengths[:, None]
    low_out = jnp.where(valid_mask[:, :, None], low_out, jnp.zeros((), jnp.bfloat16))
    grads = jnp.einsum("eto,eti->eoi", low_out.astype(jnp.float32), low_in.astype(jnp.float32))
    grads = grads.reshape(EXAMPLES, FEAT).astype(jnp.bfloat16)
    product = lax.dot_general(grads, grads, (((0,), (0,)), ((), ())), preferred_element_type=jnp.float32)
    gram_new = decay_rate * gram_old + ((1.0 - decay_rate) / EXAMPLES) * product
    diag_index = jnp.arange(FEAT)
    gram_new = gram_new.at[diag_index, diag_index].add(damping)
    solution = jnp.zeros_like(queries)
    residual = queries
    direction = queries
    norm_now = jnp.sum(residual * residual, axis=0)
    for sweep in range(ITERS):
        mapped = jnp.dot(gram_new, direction, precision=lax.Precision.HIGHEST)
        step_size = norm_now / jnp.sum(direction * mapped, axis=0)
        solution = solution + step_size * direction
        if sweep + 1 < ITERS:
            residual = residual - step_size * mapped
            norm_next = jnp.sum(residual * residual, axis=0)
            direction = residual + (norm_next / norm_now) * direction
            norm_now = norm_next
    return gram_new, solution
```

```python
import functools

import jax
import jax.numpy as jnp
from jax import lax
from jax.experimental import pallas as pl
from jax.experimental.pallas import tpu as pltpu
from jax.sharding import PartitionSpec as P

SEQ = 32

decay_rate = 0.5
damping = 1.0

BF = jnp.bfloat16
F32 = jnp.float32
VMEM_BYTES = 40 * 1024 * 1024


def dot(a, b, dims=((1,), (0,))):
    return lax.dot_general(a, b, (dims, ((), ())), preferred_element_type=F32)


def grads_kernel(chunks, outs, sel_ref, low_in_ref, out_ref):
    tokens = low_in_ref.shape[1]
    rank = low_in_ref.shape[2]
    slots = tokens // SEQ
    halves = sel_ref.shape[1]
    width = sel_ref.shape[3]
    example = lax.broadcasted_iota(jnp.int32, (slots, width), 0)
    token = lax.broadcasted_iota(jnp.int32, (slots, width), 1)
    pieces = []
    for j in range(chunks):
        left = []
        for h in range(halves):
            mask = ((token + h * width) // SEQ == example).astype(F32)
            rows = sel_ref[j, h]
            spread = rows[:, None, :] * mask[None, :, :]
            left.append(spread.reshape(outs * slots, width).astype(BF))
        left = jnp.concatenate(left, axis=1)
        pieces.append(dot(left, low_in_ref[j]).reshape(outs, slots, rank))
    both = jnp.concatenate(pieces, axis=1).astype(BF)
    for o in range(outs):
        out_ref[:, o * rank : (o + 1) * rank] = both[o]


def build_grads(sel, low_in):
    count, halves, outs, width = sel.shape
    _, tokens, rank = low_in.shape
    chunks = 2
    slots = tokens // SEQ
    return pl.pallas_call(
        functools.partial(grads_kernel, chunks, outs),
        grid=(count // chunks,),
        in_specs=[
            pl.BlockSpec((chunks, halves, outs, width), lambda i: (i, 0, 0, 0)),
            pl.BlockSpec((chunks, tokens, rank), lambda i: (i, 0, 0)),
        ],
        out_specs=pl.BlockSpec((chunks * slots, outs * rank), lambda i: (i, 0)),
        out_shape=jax.ShapeDtypeStruct((count * slots, outs * rank), BF),
        compiler_params=pltpu.CompilerParams(vmem_limit_bytes=VMEM_BYTES),
        cost_estimate=pl.CostEstimate(
            flops=2 * count * outs * slots * tokens * rank,
            bytes_accessed=count * (slots * outs * rank * 2 + tokens * rank * 4),
            transcendentals=0,
        ),
        name="build_grads",
    )(sel, low_in)


def old_product_kernel(first, half_ref, gram_ref, vec_ref, *rest):
    out_ref = rest[-1]
    block = gram_ref[...]
    high = block.astype(BF)
    low = (block - high.astype(F32)).astype(BF)
    vec = vec_ref[...]
    total = dot(high, vec) + dot(low, vec)
    if first:
        out_ref[...] = decay_rate * total
    else:
        out_ref[...] = rest[0][...] + decay_rate * total


def old_product(half, gram, vec, before=None):
    rows, cols = gram.shape
    depth, queries = vec.shape
    block = min(256, rows)
    in_specs = [
        pl.BlockSpec((block, depth), lambda i, half_ref: (i, half_ref[0])),
        pl.BlockSpec((depth, queries), lambda i, half_ref: (0, 0)),
    ]
    args = [gram, vec]
    if before is not None:
        in_specs.append(pl.BlockSpec((block, queries), lambda i, half_ref: (i, 0)))
        args.append(before)
    return pl.pallas_call(
        functools.partial(old_product_kernel, before is None),
        grid_spec=pltpu.PrefetchScalarGridSpec(
            num_scalar_prefetch=1,
            grid=(rows // block,),
            in_specs=in_specs,
            out_specs=pl.BlockSpec((block, queries), lambda i, half_ref: (i, 0)),
        ),
        out_shape=jax.ShapeDtypeStruct((rows, queries), F32),
        compiler_params=pltpu.CompilerParams(vmem_limit_bytes=VMEM_BYTES),
        cost_estimate=pl.CostEstimate(
            flops=4 * rows * depth * queries,
            bytes_accessed=4 * rows * depth + 2 * depth * queries + 4 * rows * queries,
            transcendentals=0,
        ),
        name="old_product",
    )(half, *args)


def gram_kernel(scale, block, strip, at_ref, gram_ref, left_ref, right_ref, out_ref):
    cols = gram_ref.shape[1]
    left = left_ref[...]
    offset = at_ref[0] + pl.program_id(0) * block
    ahead = lax.broadcasted_iota(jnp.int32, (block, strip), 0)
    ahead = ahead - lax.broadcasted_iota(jnp.int32, (block, strip), 1)
    for s in range(cols // strip):
        part = slice(s * strip, (s + 1) * strip)
        product = dot(left, right_ref[:, part], ((0,), (0,)))
        value = decay_rate * gram_ref[:, part] + scale * product
        out_ref[:, part] = value + jnp.where(ahead == s * strip - offset, damping, 0.0)


def update_gram(at, gram, grads, scale):
    rows, cols = gram.shape
    examples = grads.shape[0]
    block = min(256, rows)
    strip = min(1024, cols)
    return pl.pallas_call(
        functools.partial(gram_kernel, scale, block, strip),
        grid_spec=pltpu.PrefetchScalarGridSpec(
            num_scalar_prefetch=1,
            grid=(rows // block,),
            in_specs=[
                pl.BlockSpec((block, cols), lambda i, at_ref: (i, 0)),
                pl.BlockSpec((examples, block), lambda i, at_ref: (0, cols // block + i)),
                pl.BlockSpec((examples, cols), lambda i, at_ref: (0, 0)),
            ],
            out_specs=pl.BlockSpec((block, cols), lambda i, at_ref: (i, 0)),
        ),
        out_shape=jax.ShapeDtypeStruct((rows, cols), F32),
        compiler_params=pltpu.CompilerParams(vmem_limit_bytes=VMEM_BYTES),
        cost_estimate=pl.CostEstimate(
            flops=2 * rows * cols * examples,
            bytes_accessed=8 * rows * cols + 2 * examples * (rows + cols),
            transcendentals=0,
        ),
        name="update_gram",
    )(at, gram, grads, grads)


def moment_kernel(plan_ref, gram_ref, vec_ref, other_ref, left_ref, out_ref):
    part = pl.program_id(0)
    step = pl.program_id(1)

    @pl.when((part == 0) & (step == 0))
    def _():
        out_ref[...] = jnp.zeros_like(out_ref)

    def add(vec, weight):
        mapped = dot(gram_ref[...].astype(BF), vec) * left_ref[...]
        rows, queries = mapped.shape
        out_ref[...] += weight * jnp.sum(mapped.reshape(rows // 8, 8, queries), axis=0)

    @pl.when(part == 0)
    def _():
        add(vec_ref[...], plan_ref[2].astype(F32))

    @pl.when((part == 1) & (plan_ref[1] == 1))
    def _():
        add(other_ref[...], 1.0)


def moment(plan, gram, vec, other, left):
    rows, cols = gram.shape
    depth, queries = vec.shape
    block = min(256, rows)
    last = rows // block - 1

    def gram_at(p, i, plan_ref):
        skip = (p == 1) & (plan_ref[1] == 0)
        half = jnp.where((p == 1) & (plan_ref[1] == 1), 1 - plan_ref[0], plan_ref[0])
        return (jnp.where(skip, last, i), half)

    def left_at(p, i, plan_ref):
        return (jnp.where((p == 1) & (plan_ref[1] == 0), last, i), 0)

    return pl.pallas_call(
        moment_kernel,
        grid_spec=pltpu.PrefetchScalarGridSpec(
            num_scalar_prefetch=1,
            grid=(2, rows // block),
            in_specs=[
                pl.BlockSpec((block, depth), gram_at),
                pl.BlockSpec((depth, queries), lambda p, i, plan_ref: (0, 0)),
                pl.BlockSpec((depth, queries), lambda p, i, plan_ref: (0, 0)),
                pl.BlockSpec((block, queries), left_at),
            ],
            out_specs=pl.BlockSpec((8, queries), lambda p, i, plan_ref: (0, 0)),
        ),
        out_shape=jax.ShapeDtypeStruct((8, queries), F32),
        compiler_params=pltpu.CompilerParams(vmem_limit_bytes=VMEM_BYTES),
        cost_estimate=pl.CostEstimate(
            flops=2 * rows * cols * queries,
            bytes_accessed=4 * rows * cols + 8 * rows * queries,
            transcendentals=0,
        ),
        name="moment",
    )(plan, gram, vec, other, left)


def turn(value, position, axis):
    count = value.shape[axis]
    slots = [
        lax.dynamic_index_in_dim(value, (position - i) % count, axis, keepdims=True)
        for i in range(count)
    ]
    return jnp.concatenate(slots, axis)


def shards(activations, out_grads, proj_in, proj_out, lengths, gram_old, queries):
    local_count = lengths.shape[0]
    rank = proj_in.shape[1]
    row_count = lax.axis_size("row")
    col_count = lax.axis_size("col")
    rows, cols = gram_old.shape
    tokens = local_count * SEQ
    half_tokens = tokens // 2
    tiers = row_count // 2
    files = col_count // 2
    row = lax.axis_index("row")
    col = lax.axis_index("col")
    z, y = row // 2, row % 2
    x, core = col // 2, col % 2
    total_examples = local_count * row_count * col_count
    scale = (1.0 - decay_rate) / total_examples

    def move(value, goes):
        pairs = []
        for r in range(row_count):
            for c in range(col_count):
                to = goes(r // 2, r % 2, c // 2, c % 2)
                if to is not None:
                    pairs.append((r * col_count + c, (to[0] * 2 + to[1]) * col_count + to[2] * 2 + to[3]))
        return lax.ppermute(value, ("row", "col"), pairs)

    def swap_y(value):
        return move(value, lambda z, y, x, k: (z, 1 - y, x, k))

    def swap_core(value):
        return move(value, lambda z, y, x, k: (z, y, x, 1 - k))

    def ring_z(value):
        return move(value, lambda z, y, x, k: ((z + 1) % tiers, y, x, k))

    def ring_x(value):
        return move(value, lambda z, y, x, k: (z, y, (x + 1) % files, k))

    def flip_x(value, bit):
        return move(value, lambda z, y, x, k: (z, y, x ^ bit, k))

    def flip_z(value, bit):
        return move(value, lambda z, y, x, k: (z ^ bit, y, x, k))

    def chain(value, sign):
        got = []
        for s in range(1, tiers):

            def goes(z, y, x, k, s=s):
                source = x * 2 + k
                if z == source + sign * (s - 1) and 0 <= z + sign < tiers:
                    return (z + sign, y, x, k)
                return None

            value = move(value, goes)
            got.append(value)
        return got

    def ring(value, step, count):
        got = [value]
        for _ in range(count - 1):
            value = step(value)
            got.append(value)
        return got

    away = z - col
    sent = queries.astype(BF)
    ups, downs = chain(sent, 1), chain(sent, -1)
    mine = sent
    for s in range(1, tiers):
        mine = jnp.where(away == s, ups[s - 1], mine)
        mine = jnp.where(away == -s, downs[s - 1], mine)
    theirs = swap_y(mine)

    low_in = dot(activations, proj_in).astype(BF)
    low_out = dot(proj_out, out_grads, ((0,), (1,))).astype(BF)
    slot = jnp.arange(tokens, dtype=jnp.int32)
    valid_mask = slot % SEQ < jnp.repeat(lengths, SEQ)
    low_out = jnp.where(valid_mask[None, :], low_out, jnp.zeros((), BF))
    low_out = low_out.reshape(rank, 2, half_tokens).transpose(1, 0, 2)

    ins = jnp.stack(ring(low_in, ring_z, tiers))
    outs = jnp.stack(ring(low_out, ring_z, tiers))
    ins = jnp.stack([ins, swap_y(ins)])
    outs = jnp.stack(ring(outs, ring_x, files))
    ins = jnp.stack(ring(ins, ring_x, files))
    outs = jnp.stack([outs, swap_y(outs)])
    outs = jnp.swapaxes(outs, 0, 1)
    ins = jnp.stack([ins, swap_core(ins)])
    outs = jnp.stack([outs, swap_core(outs)])
    chunks = 2 * files * 2 * tiers
    ins = ins.reshape(chunks, tokens, rank)
    outs = outs.reshape(chunks, 2, rank, half_tokens)
    outs_col = cols // rank
    outs_row = rows // rank
    sel = jnp.concatenate(
        [
            lax.dynamic_slice_in_dim(outs, col * outs_col, outs_col, 2),
            lax.dynamic_slice_in_dim(outs, row * outs_row, outs_row, 2),
        ],
        axis=2,
    ).astype(F32)
    grads = build_grads(sel, ins)

    half = y.reshape(1).astype(jnp.int32)
    partial_value = old_product(half, gram_old, mine)
    partial_value = old_product(1 - half, gram_old, theirs, partial_value)
    halved = rows // 2
    give = lax.dynamic_slice_in_dim(partial_value, (1 - core) * halved, halved, 0)
    keep = lax.dynamic_slice_in_dim(partial_value, core * halved, halved, 0)
    keep = keep + swap_core(give)
    bit = 1
    while bit < files:
        short = keep.astype(BF)
        keep = short.astype(F32) + flip_x(short, bit).astype(F32)
        bit *= 2
    other = swap_core(keep)
    mapped = jnp.where(
        core == 0, jnp.concatenate([keep, other], 0), jnp.concatenate([other, keep], 0)
    )

    first = jnp.where(y == 0, mine, theirs)
    second = jnp.where(y == 0, theirs, mine)
    depth = rows
    inner = dot(grads[:, :depth], first) + dot(grads[:, depth:cols], second)
    count = inner.shape[1]
    inner = inner.reshape(2, files, -1, count)
    inner = turn(turn(inner, core, 0), x, 1)
    inner = inner + swap_core(inner)
    bit = 1
    while bit < files:
        inner = inner + flip_x(inner, bit)
        bit *= 2
    inner = turn(turn(inner, core, 0), x, 1).reshape(-1, count).astype(BF)
    mapped = mapped + scale * dot(grads[:, cols:], inner, ((0,), (0,))) + damping * queries

    at = (row * rows - col * cols).reshape(1).astype(jnp.int32)
    gram_new = update_gram(at, gram_old, grads, scale)

    short = mapped.astype(BF)

    def cross_at_source(z, y, x, k):
        return (z, 1 - y, x, k) if z == x * 2 + k else None

    cross = move(short, cross_at_source)
    ups, downs = chain(cross, 1), chain(short, -1)
    vec = short
    for s in range(1, tiers):
        vec = jnp.where(away == s, ups[s - 1], vec)
        vec = jnp.where(away == -s, downs[s - 1], vec)
    plan = jnp.stack(
        [
            jnp.where(away > 0, 1 - y, y),
            jnp.where(away == 0, 1, 0),
            jnp.where(away == 0, 1, 2),
        ]
    ).astype(jnp.int32)
    curve = jnp.sum(moment(plan, gram_new, vec, cross, mapped), axis=0)

    even = 1.0 / col_count
    sums = jnp.stack(
        [
            jnp.sum(queries * queries, axis=0) * even,
            jnp.sum(queries * mapped, axis=0) * even,
            jnp.sum(mapped * mapped, axis=0) * even,
            curve,
        ]
    )
    sums = sums + swap_core(sums)
    bit = 1
    while bit < files:
        sums = sums + flip_x(sums, bit)
        bit *= 2
    sums = sums + swap_y(sums)
    bit = 1
    while bit < tiers:
        sums = sums + flip_z(sums, bit)
        bit *= 2
    norm_now, along, square, curve = sums[0], sums[1], sums[2], sums[3]
    step = norm_now / along
    norm_next = step * step * square - norm_now
    momentum = norm_next / norm_now
    curvature = along - 2.0 * step * square + step * step * curve
    step_next = norm_next / (curvature - momentum * norm_next / step)
    solution = (step + step_next * (1.0 + momentum)) * queries - (step_next * step) * mapped
    return (gram_new, solution)


def solution(mesh):
    in_specs = (
        P(("row", "col"), None),
        P(("row", "col"), None),
        P(),
        P(),
        P(("row", "col")),
        P("row", "col"),
        P("row", None),
    )
    out_specs = (P("row", "col"), P("row", None))
    return jax.shard_map(shards, mesh=mesh, in_specs=in_specs, out_specs=out_specs, check_vma=False)
```

```python
import functools

import jax
import jax.numpy as jnp
from jax import lax
from jax.experimental import pallas as pl
from jax.experimental.pallas import tpu as pltpu
from jax.sharding import PartitionSpec as P

SEQ = 32

decay_rate = 0.5
damping = 1.0

BF = jnp.bfloat16
F32 = jnp.float32
VMEM_BYTES = 40 * 1024 * 1024


def dot(a, b, dims=((1,), (0,))):
    return lax.dot_general(a, b, (dims, ((), ())), preferred_element_type=F32)


def params():
    return pltpu.CompilerParams(vmem_limit_bytes=VMEM_BYTES)


def cost(flops, moved):
    return pl.CostEstimate(flops=flops, bytes_accessed=moved, transcendentals=0)


def grads_kernel(parts, chunks, outs_col, outs_row, at_ref, *refs):
    factor_refs = refs[:parts]
    col_ref, row_ref, rows_ref = refs[parts:]
    rank = factor_refs[0].shape[2]
    tokens = factor_refs[0].shape[1] // 2
    slots = tokens // SEQ
    halves = tokens // rank
    outs = outs_col + outs_row
    example = lax.broadcasted_iota(jnp.int32, (slots, rank), 0)
    token = lax.broadcasted_iota(jnp.int32, (slots, rank), 1)
    col_at = pl.multiple_of(at_ref[1] * outs_col, outs_col)
    row_at = pl.multiple_of(at_ref[0] * outs_row, outs_row)

    def build(factor_ref):
        pieces = []
        for j in range(chunks):
            rows_ref[...] = factor_ref[j, tokens:, :].astype(F32)
            left = []
            for h in range(halves):
                mask = ((token + h * rank) // SEQ == example).astype(F32)
                rows = jnp.concatenate(
                    [
                        rows_ref[pl.ds(h * rank + col_at, outs_col), :],
                        rows_ref[pl.ds(h * rank + row_at, outs_row), :],
                    ],
                    axis=0,
                )
                spread = rows[:, None, :] * mask[None, :, :]
                left.append(spread.reshape(outs * slots, rank).astype(BF))
            left = jnp.concatenate(left, axis=1)
            pieces.append(dot(left, factor_ref[j, :tokens, :]).reshape(outs, slots, rank))
        both = jnp.concatenate(pieces, axis=1).astype(BF)
        for o in range(outs_col):
            col_ref[:, o * rank : (o + 1) * rank] = both[o]
        for o in range(outs_row):
            row_ref[:, o * rank : (o + 1) * rank] = both[outs_col + o]

    for part in range(parts):
        pl.when(pl.program_id(0) == part)(functools.partial(build, factor_refs[part]))


def build_grads(place, factors, rows, cols):
    parts = len(factors)
    count, depth, rank = factors[0].shape
    tokens = depth // 2
    chunks = 2
    slots = tokens // SEQ
    steps = count // chunks
    total = parts * count * slots

    files = parts // 2

    def grads_at(p, i, at_ref):
        x, core = at_ref[1] // 2, at_ref[1] % 2
        source = 2 * lax.rem(x - p % files + files, files) + (core ^ (p // files))
        return (source * steps + i, 0)

    def factor_at(part, p, i, at_ref):
        return (jnp.where(p == part, i, jnp.where(p < part, 0, steps - 1)), 0, 0)

    return pl.pallas_call(
        functools.partial(grads_kernel, parts, chunks, cols // rank, rows // rank),
        grid_spec=pltpu.PrefetchScalarGridSpec(
            num_scalar_prefetch=1,
            grid=(parts, steps),
            in_specs=[
                pl.BlockSpec((chunks, depth, rank), functools.partial(factor_at, part))
                for part in range(parts)
            ],
            out_specs=[
                pl.BlockSpec((chunks * slots, cols), grads_at),
                pl.BlockSpec((chunks * slots, rows), grads_at),
            ],
            scratch_shapes=[pltpu.VMEM((tokens, rank), F32)],
        ),
        out_shape=[
            jax.ShapeDtypeStruct((total, cols), BF),
            jax.ShapeDtypeStruct((total, rows), BF),
        ],
        compiler_params=params(),
        cost_estimate=cost(2 * total * (rows + cols) * tokens, 2 * total * (rows + cols)),
        name="build_grads",
    )(place, *factors)


def back_kernel(streams, plan_ref, *refs):
    vec_ref, gram_refs, out_ref = refs[0], refs[1 : 1 + streams], refs[-1]
    depth = gram_refs[0].shape[0]
    total = None
    for s in range(streams):
        block = gram_refs[s][...]
        high = block.astype(BF)
        low = (block - high.astype(F32)).astype(BF)
        vec = vec_ref[:, s * depth : (s + 1) * depth]
        value = dot(vec, high) + dot(vec, low)
        total = value if total is None else total + value
    total = decay_rate * total.T
    if len(refs) > streams + 2:
        own = jnp.where(plan_ref[1] == 1, damping, 0.0)
        total = total + own * refs[-2][...]
    out_ref[...] = total.astype(out_ref.dtype)


def back_product(plan, vec, gram, queries=None):
    count, rows = vec.shape
    width = gram.shape[1] // 2
    block = min(512, width)
    steps = width // block
    streams = 2
    depth = rows // streams

    def gram_at(s, i, plan_ref):
        return (s, plan_ref[0] * steps + i)

    in_specs = [pl.BlockSpec((count, rows), lambda i, plan_ref: (0, 0))]
    for s in range(streams):
        in_specs.append(pl.BlockSpec((depth, block), functools.partial(gram_at, s)))
    args = [vec] + [gram] * streams
    kind = BF
    if queries is not None:
        in_specs.append(pl.BlockSpec((block, count), lambda i, plan_ref: (i, 0)))
        args.append(queries)
        kind = F32
    return pl.pallas_call(
        functools.partial(back_kernel, streams),
        grid_spec=pltpu.PrefetchScalarGridSpec(
            num_scalar_prefetch=1,
            grid=(steps,),
            in_specs=in_specs,
            out_specs=pl.BlockSpec((block, count), lambda i, plan_ref: (i, 0)),
        ),
        out_shape=jax.ShapeDtypeStruct((width, count), kind),
        compiler_params=params(),
        cost_estimate=cost(4 * rows * width * count, 4 * rows * width + 4 * width * count),
        name="back_product",
    )(plan, *args)


def gram_kernel(scale, block, strip, first, at_ref, gram_ref, left_ref, right_ref, *rest):
    out_ref = rest[-1]
    cols = gram_ref.shape[1]
    left = left_ref[...]
    offset = at_ref[0] + (first + pl.program_id(0)) * block
    ahead = lax.broadcasted_iota(jnp.int32, (block, strip), 0)
    ahead = ahead - lax.broadcasted_iota(jnp.int32, (block, strip), 1)
    for s in range(cols // strip):
        part = slice(s * strip, (s + 1) * strip)
        product = dot(left, right_ref[:, part], ((0,), (0,)))
        value = decay_rate * gram_ref[:, part] + scale * product
        out_ref[:, part] = value + jnp.where(ahead == s * strip - offset, damping, 0.0)


def update_gram(at, gram, left, right, scale, first, count, block, before):
    rows, cols = gram.shape
    examples = left.shape[0]
    strip = min(1024, cols)
    in_specs = [
        pl.BlockSpec((block, cols), lambda i, at_ref: (first + i, 0)),
        pl.BlockSpec((examples, block), lambda i, at_ref: (0, first + i)),
        pl.BlockSpec((examples, cols), lambda i, at_ref: (0, 0)),
    ]
    args = [gram, left, right]
    alias = {}
    if before is not None:
        in_specs.append(pl.BlockSpec(memory_space=pl.ANY))
        args.append(before)
        alias = {4: 0}
    return pl.pallas_call(
        functools.partial(gram_kernel, scale, block, strip, first),
        grid_spec=pltpu.PrefetchScalarGridSpec(
            num_scalar_prefetch=1,
            grid=(count,),
            in_specs=in_specs,
            out_specs=pl.BlockSpec((block, cols), lambda i, at_ref: (first + i, 0)),
        ),
        out_shape=jax.ShapeDtypeStruct((rows, cols), F32),
        input_output_aliases=alias,
        compiler_params=params(),
        cost_estimate=cost(2 * count * block * cols * examples, 8 * count * block * cols),
        name="update_gram",
    )(at, *args)


def finish_kernel(with_sums, plan_ref, old_ref, grad_ref, inner_ref, *refs):
    value = old_ref[0].astype(F32) + dot(grad_ref[...], inner_ref[...], ((0,), (0,)))
    refs[-1 - with_sums][...] = value.astype(refs[-1 - with_sums].dtype)
    if with_sums:
        query = refs[0][...]
        sums_ref = refs[-1]

        @pl.when(pl.program_id(0) == 0)
        def _():
            sums_ref[...] = jnp.zeros_like(sums_ref)

        rows, count = value.shape
        for k, product in enumerate((query * query, query * value, value * value)):
            sums_ref[k] += jnp.sum(product.reshape(rows // 8, 8, count), axis=0)


def finish(plan, old, grads, inner, kind, queries=None):
    tiers, piece, count = old.shape
    examples = grads.shape[0]

    def piece_of(i, plan_ref):
        return lax.rem(plan_ref[0] - i + tiers, tiers)

    in_specs = [
        pl.BlockSpec((1, piece, count), lambda i, plan_ref: (i, 0, 0)),
        pl.BlockSpec(
            (examples, piece), lambda i, plan_ref: (0, plan_ref[1] * tiers + piece_of(i, plan_ref))
        ),
        pl.BlockSpec((examples, count), lambda i, plan_ref: (0, 0)),
    ]
    args = [old, grads, inner]
    out_specs = [pl.BlockSpec((piece, count), lambda i, plan_ref: (piece_of(i, plan_ref), 0))]
    out_shape = [jax.ShapeDtypeStruct((tiers * piece, count), kind)]
    with_sums = queries is not None
    if with_sums:
        in_specs.append(
            pl.BlockSpec((piece, count), lambda i, plan_ref: (piece_of(i, plan_ref), 0))
        )
        args.append(queries)
        out_specs.append(pl.BlockSpec((3, 8, count), lambda i, plan_ref: (0, 0, 0)))
        out_shape.append(jax.ShapeDtypeStruct((3, 8, count), F32))
    return pl.pallas_call(
        functools.partial(finish_kernel, int(with_sums)),
        grid_spec=pltpu.PrefetchScalarGridSpec(
            num_scalar_prefetch=1, grid=(tiers,), in_specs=in_specs, out_specs=out_specs
        ),
        out_shape=out_shape,
        compiler_params=params(),
        cost_estimate=cost(
            2 * tiers * piece * count * examples, 2 * tiers * piece * (examples + 3 * count)
        ),
        name="finish",
    )(plan, *args)


def curve_kernel(steps, plan_ref, same_ref, other_ref, extra_ref, vec_ref, next_ref, out_ref):
    i = pl.program_id(0)
    upper = (i >= steps // 2).astype(jnp.int32)
    width = same_ref.shape[1]

    def take(ref, quadrant):
        return ref[pl.ds(pl.multiple_of(quadrant * width, width), width), :]

    weight = plan_ref[3].astype(F32)
    total = weight * dot(same_ref[...].astype(BF), take(vec_ref, upper ^ plan_ref[1]))
    out_ref[...] = total + 2.0 * dot(
        other_ref[...].astype(BF), take(next_ref, upper ^ plan_ref[2])
    )

    @pl.when((plan_ref[4] == 1) & (i < steps // 2))
    def _():
        out_ref[...] += 2.0 * dot(extra_ref[...].astype(BF), vec_ref[width:, :])


def curve_product(plan, gram, vec, other):
    rows = gram.shape[0]
    depth, count = vec.shape
    block = min(256, rows // 2)
    steps = rows // block
    width = depth // 2

    def upper(i):
        return jnp.where(i >= steps // 2, 1, 0)

    def same_at(i, plan_ref):
        return (i, plan_ref[0] * 2 + (upper(i) ^ plan_ref[1]))

    def other_at(i, plan_ref):
        return (i, (1 - plan_ref[0]) * 2 + (upper(i) ^ plan_ref[2]))

    def extra_at(i, plan_ref):
        live = jnp.where(plan_ref[4] == 1, jnp.minimum(i, steps // 2 - 1), 0)
        return (live, plan_ref[0] * 2 + 1)

    return pl.pallas_call(
        functools.partial(curve_kernel, steps),
        grid_spec=pltpu.PrefetchScalarGridSpec(
            num_scalar_prefetch=1,
            grid=(steps,),
            in_specs=[
                pl.BlockSpec((block, width), same_at),
                pl.BlockSpec((block, width), other_at),
                pl.BlockSpec((block, width), extra_at),
                pl.BlockSpec((depth, count), lambda i, plan_ref: (0, 0)),
                pl.BlockSpec((depth, count), lambda i, plan_ref: (0, 0)),
            ],
            out_specs=pl.BlockSpec((block, count), lambda i, plan_ref: (i, 0)),
        ),
        out_shape=jax.ShapeDtypeStruct((rows, count), F32),
        compiler_params=params(),
        cost_estimate=cost(2 * rows * depth * count, 4 * rows * depth),
        name="curve_product",
    )(plan, gram, gram, gram, vec, other)


def after(value, *others):
    return lax.optimization_barrier((value,) + others)[0]


def integers(*values):
    return jnp.stack([jnp.asarray(v).astype(jnp.int32) for v in values])


def shards(activations, out_grads, proj_in, proj_out, lengths, gram_old, queries):
    local_count = lengths.shape[0]
    rank = proj_in.shape[1]
    row_count = lax.axis_size("row")
    col_count = lax.axis_size("col")
    rows, cols = gram_old.shape
    count = queries.shape[1]
    tokens = local_count * SEQ
    tiers = row_count // 2
    files = col_count // 2
    piece = rows // tiers
    row = lax.axis_index("row")
    col = lax.axis_index("col")
    z, y = row // 2, row % 2
    x, core = col // 2, col % 2
    total_examples = local_count * row_count * col_count
    scale = (1.0 - decay_rate) / total_examples

    def move(value, goes):
        pairs = []
        for r in range(row_count):
            for c in range(col_count):
                to = goes(r // 2, r % 2, c // 2, c % 2)
                if to is not None:
                    pairs.append((r * col_count + c, (to[0] * 2 + to[1]) * col_count + to[2] * 2 + to[3]))
        return lax.ppermute(value, ("row", "col"), pairs)

    def swap_y(value):
        return move(value, lambda z, y, x, k: (z, 1 - y, x, k))

    def swap_core(value):
        return move(value, lambda z, y, x, k: (z, y, x, 1 - k))

    def ring_z(value, by=1):
        return move(value, lambda z, y, x, k: ((z + by) % tiers, y, x, k))

    def ring_x(value):
        return move(value, lambda z, y, x, k: (z, y, (x + 1) % files, k))

    def flip_x(value, bit):
        return move(value, lambda z, y, x, k: (z, y, x ^ bit, k))

    low_in = dot(activations, proj_in).astype(BF)
    low_out = dot(proj_out, out_grads, ((0,), (1,))).astype(BF)
    slot = jnp.arange(tokens, dtype=jnp.int32)
    valid_mask = slot % SEQ < jnp.repeat(lengths, SEQ)
    low_out = jnp.where(valid_mask[None, :], low_out, jnp.zeros((), BF))
    low_out = low_out.reshape(rank, tokens // rank, rank).transpose(1, 0, 2).reshape(tokens, rank)
    local = jnp.concatenate([low_in, low_out], axis=0)
    factors = lax.all_gather(local, "row")
    parts = [factors]
    for _ in range(files - 1):
        parts.append(ring_x(parts[-1]))
    parts = parts + [swap_core(part) for part in parts]

    vec = queries.astype(BF).T
    away = back_product(integers(1 - y, 0), vec, gram_old)
    here = back_product(after(integers(y, z == col), local), vec, gram_old, queries)
    come = swap_y(away)
    here = here.reshape(tiers, piece, count)
    come = come.reshape(tiers, piece, count)

    def own(turn):
        at = (z - 1 - turn) % tiers
        one = lax.dynamic_index_in_dim(here, at, 0, keepdims=False)
        two = lax.dynamic_index_in_dim(come, at, 0, keepdims=False)
        return one + two.astype(F32)

    total = own(0)
    for turn in range(tiers - 1):
        total = ring_z(total.astype(BF)).astype(F32) + own(turn + 1)

    place = integers(row, col)
    grads_col, grads_row = build_grads(place, parts, rows, cols)
    inner = lax.psum(dot(grads_row, queries.astype(BF)), "row")
    inner = (scale * inner).astype(BF)

    block = min(128, rows)
    blocks = rows // block
    cuts = [blocks * k // (tiers - 1) for k in range(tiers)]
    at = integers(row * rows - col * cols).reshape(1)
    gram_new = None
    short = total.astype(BF)
    same, other = [short], [swap_y(short)]
    for turn in range(tiers - 1):
        got = ring_z(short)
        if cuts[turn + 1] > cuts[turn]:
            gram_new = update_gram(
                after(at, short), gram_old, grads_row, grads_col, scale,
                cuts[turn], cuts[turn + 1] - cuts[turn], block, gram_new,
            )
        short = got
        same.append(short)
        other.append(swap_y(short))
    same = jnp.stack(same)
    other = jnp.stack(other)

    mate = swap_core(same)
    mine = jnp.where(core == z % 2, same, mate)
    cut = tiers // 2
    send = lax.dynamic_slice_in_dim(mine, core * cut, cut, 0)
    found = mine
    for s in range(1, files):
        send = ring_x(send)
        rest = swap_core(send)
        both = jnp.where(
            core == 0, jnp.concatenate([send, rest], 0), jnp.concatenate([rest, send], 0)
        )
        found = jnp.where((x - s) % files == z // 2, both, found)

    (vec_same,) = finish(integers(z, y), same, grads_col, inner, BF)
    (vec_other,) = finish(integers(z, 1 - y), other, grads_col, inner, BF)
    plan = integers(
        y, row > 2 * col + y, row > 2 * col + 1 - y, jnp.where(z == col, 1, 2), z == col
    )
    product = curve_product(plan, gram_new, vec_same, vec_other)
    mapped, sums = finish(integers(z, 0), found, grads_row, inner, F32, queries)
    sums = jnp.sum(sums, axis=1) * (1.0 / col_count)
    sums = jnp.concatenate([sums, jnp.sum(product * mapped, axis=0)[None]], axis=0)
    sums = sums + swap_core(sums)
    bit = 1
    while bit < files:
        sums = sums + flip_x(sums, bit)
        bit *= 2
    sums = sums + swap_y(sums)
    around = jnp.stack([sums] + [ring_z(sums, by) for by in range(1, tiers)])
    sums = sum(
        lax.dynamic_index_in_dim(around, (z - k) % tiers, 0, keepdims=False) for k in range(tiers)
    )
    norm_now, along, square, curve = sums[0], sums[1], sums[2], sums[3]
    step = norm_now / along
    norm_next = step * step * square - norm_now
    momentum = norm_next / norm_now
    curvature = along - 2.0 * step * square + step * step * curve
    step_next = norm_next / (curvature - momentum * norm_next / step)
    solution = (step + step_next * (1.0 + momentum)) * queries - (step_next * step) * mapped
    return (gram_new, solution)


def solution(mesh):
    in_specs = (
        P(("row", "col"), None),
        P(("row", "col"), None),
        P(),
        P(),
        P(("row", "col")),
        P("row", "col"),
        P("row", None),
    )
    out_specs = (P("row", "col"), P("row", None))
    return jax.shard_map(shards, mesh=mesh, in_specs=in_specs, out_specs=out_specs, check_vma=False)
```

```python
import functools

import jax
import jax.numpy as jnp
from jax import lax
from jax.experimental import pallas as pl
from jax.experimental.pallas import tpu as pltpu
from jax.sharding import PartitionSpec as P

SEQ = 32

decay_rate = 0.5
damping = 1.0

BF = jnp.bfloat16
F32 = jnp.float32
VMEM_BYTES = 40 * 1024 * 1024


def dot(a, b, dims=((1,), (0,))):
    return lax.dot_general(a, b, (dims, ((), ())), preferred_element_type=F32)


def params():
    return pltpu.CompilerParams(vmem_limit_bytes=VMEM_BYTES)


def cost(flops, moved):
    return pl.CostEstimate(flops=flops, bytes_accessed=moved, transcendentals=0)


def grads_kernel(outs_col, outs_row, at_ref, *refs):
    factor_refs = refs[:4]
    col_ref, row_ref, rows_ref = refs[4:]
    rank = factor_refs[0].shape[2]
    tokens = factor_refs[0].shape[1] // 2
    slots = tokens // SEQ
    halves = tokens // rank
    outs = outs_col + outs_row
    example = lax.broadcasted_iota(jnp.int32, (slots, rank), 0)
    token = lax.broadcasted_iota(jnp.int32, (slots, rank), 1)
    col_at = pl.multiple_of(at_ref[1] * outs_col, outs_col)
    row_at = pl.multiple_of(at_ref[0] * outs_row, outs_row)

    def build(factor_ref):
        rows_ref[...] = factor_ref[0, tokens:, :].astype(F32)
        left = []
        for h in range(halves):
            mask = ((token + h * rank) // SEQ == example).astype(F32)
            rows = jnp.concatenate(
                [
                    rows_ref[pl.ds(h * rank + col_at, outs_col), :],
                    rows_ref[pl.ds(h * rank + row_at, outs_row), :],
                ],
                axis=0,
            )
            spread = rows[:, None, :] * mask[None, :, :]
            left.append(spread.reshape(outs * slots, rank).astype(BF))
        left = jnp.concatenate(left, axis=1)
        return dot(left, factor_ref[0, :tokens, :]).reshape(outs, slots, rank)

    def pair(own_ref, mate_ref):
        own, mate = build(own_ref), build(mate_ref)
        even = at_ref[1] % 2 == 0
        both = [jnp.where(even, own, mate), jnp.where(even, mate, own)]
        both = jnp.concatenate(both, axis=1).astype(BF)
        for o in range(outs_col):
            col_ref[:, o * rank : (o + 1) * rank] = both[o]
        for o in range(outs_row):
            row_ref[:, o * rank : (o + 1) * rank] = both[outs_col + o]

    for part in range(2):
        pl.when(pl.program_id(0) == part)(
            functools.partial(pair, factor_refs[part], factor_refs[2 + part])
        )


def build_grads(place, factors, tiers, rows, cols):
    count, depth, rank = factors[0].shape
    tokens = depth // 2
    slots = tokens // SEQ
    files = count // tiers
    total = 4 * count * slots

    def grads_at(p, i, at_ref):
        z, y, x = at_ref[0] // 2, at_ref[0] % 2, at_ref[1] // 2
        from_x = lax.rem(x - i // tiers + files, files)
        from_z = lax.rem(z - i % tiers + tiers, tiers)
        return ((from_x * tiers + from_z) * 2 + (y ^ p), 0)

    def factor_at(part, p, i, at_ref):
        return (jnp.where(p == part, i, jnp.where(p < part, 0, count - 1)), 0, 0)

    return pl.pallas_call(
        functools.partial(grads_kernel, cols // rank, rows // rank),
        grid_spec=pltpu.PrefetchScalarGridSpec(
            num_scalar_prefetch=1,
            grid=(2, count),
            in_specs=[
                pl.BlockSpec((1, depth, rank), functools.partial(factor_at, part % 2))
                for part in range(4)
            ],
            out_specs=[
                pl.BlockSpec((2 * slots, cols), grads_at),
                pl.BlockSpec((2 * slots, rows), grads_at),
            ],
            scratch_shapes=[pltpu.VMEM((tokens, rank), F32)],
        ),
        out_shape=[
            jax.ShapeDtypeStruct((total, cols), BF),
            jax.ShapeDtypeStruct((total, rows), BF),
        ],
        compiler_params=params(),
        cost_estimate=cost(2 * total * (rows + cols) * tokens, 2 * total * (rows + cols)),
        name="build_grads",
    )(place, *factors)


def back_kernel(streams, plan_ref, *refs):
    vec_ref, gram_refs, out_ref = refs[0], refs[1 : 1 + streams], refs[-1]
    depth = gram_refs[0].shape[0]
    total = None
    for s in range(streams):
        vec = vec_ref[:, s * depth : (s + 1) * depth]
        value = dot(vec, gram_refs[s][...].astype(BF))
        total = value if total is None else total + value
    total = decay_rate * total.T
    if len(refs) > streams + 2:
        own = jnp.where(plan_ref[1] == 1, damping, 0.0)
        total = total + own * refs[-2][...]
    out_ref[...] = total.astype(out_ref.dtype)


def back_product(plan, vec, gram, queries=None):
    count, rows = vec.shape
    width = gram.shape[1] // 2
    block = min(512, width)
    steps = width // block
    streams = 2
    depth = rows // streams

    def gram_at(s, i, plan_ref):
        return (s, plan_ref[0] * steps + i)

    in_specs = [pl.BlockSpec((count, rows), lambda i, plan_ref: (0, 0))]
    for s in range(streams):
        in_specs.append(pl.BlockSpec((depth, block), functools.partial(gram_at, s)))
    args = [vec] + [gram] * streams
    kind = BF
    if queries is not None:
        in_specs.append(pl.BlockSpec((block, count), lambda i, plan_ref: (i, 0)))
        args.append(queries)
        kind = F32
    return pl.pallas_call(
        functools.partial(back_kernel, streams),
        grid_spec=pltpu.PrefetchScalarGridSpec(
            num_scalar_prefetch=1,
            grid=(steps,),
            in_specs=in_specs,
            out_specs=pl.BlockSpec((block, count), lambda i, plan_ref: (i, 0)),
        ),
        out_shape=jax.ShapeDtypeStruct((width, count), kind),
        compiler_params=params(),
        cost_estimate=cost(2 * rows * width * count, 4 * rows * width + 4 * width * count),
        name="back_product",
    )(plan, *args)


def gram_kernel(scale, block, strip, first, at_ref, gram_ref, left_ref, right_ref, *rest):
    out_ref = rest[-1]
    cols = gram_ref.shape[1]
    left = left_ref[...]
    offset = at_ref[0] + (first + pl.program_id(0)) * block
    ahead = lax.broadcasted_iota(jnp.int32, (block, strip), 0)
    ahead = ahead - lax.broadcasted_iota(jnp.int32, (block, strip), 1)
    for s in range(cols // strip):
        part = slice(s * strip, (s + 1) * strip)
        product = dot(left, right_ref[:, part], ((0,), (0,)))
        value = decay_rate * gram_ref[:, part] + scale * product
        out_ref[:, part] = value + jnp.where(ahead == s * strip - offset, damping, 0.0)


def update_gram(at, gram, left, right, scale, first, count, block, before):
    rows, cols = gram.shape
    examples = left.shape[0]
    strip = min(1024, cols)
    in_specs = [
        pl.BlockSpec((block, cols), lambda i, at_ref: (first + i, 0)),
        pl.BlockSpec((examples, block), lambda i, at_ref: (0, first + i)),
        pl.BlockSpec((examples, cols), lambda i, at_ref: (0, 0)),
    ]
    args = [gram, left, right]
    alias = {}
    if before is not None:
        in_specs.append(pl.BlockSpec(memory_space=pl.ANY))
        args.append(before)
        alias = {4: 0}
    return pl.pallas_call(
        functools.partial(gram_kernel, scale, block, strip, first),
        grid_spec=pltpu.PrefetchScalarGridSpec(
            num_scalar_prefetch=1,
            grid=(count,),
            in_specs=in_specs,
            out_specs=pl.BlockSpec((block, cols), lambda i, at_ref: (first + i, 0)),
        ),
        out_shape=jax.ShapeDtypeStruct((rows, cols), F32),
        input_output_aliases=alias,
        compiler_params=params(),
        cost_estimate=cost(2 * count * block * cols * examples, 8 * count * block * cols),
        name="update_gram",
    )(at, *args)


def finish_kernel(with_sums, plan_ref, old_ref, grad_ref, inner_ref, *refs):
    value = old_ref[0].astype(F32) + dot(grad_ref[...], inner_ref[...], ((0,), (0,)))
    refs[-1 - with_sums][...] = value.astype(refs[-1 - with_sums].dtype)
    if with_sums:
        query = refs[0][...]
        sums_ref = refs[-1]

        @pl.when(pl.program_id(0) == 0)
        def _():
            sums_ref[...] = jnp.zeros_like(sums_ref)

        rows, count = value.shape
        for k, product in enumerate((query * query, query * value, value * value)):
            sums_ref[k] += jnp.sum(product.reshape(rows // 8, 8, count), axis=0)


def finish(plan, old, grads, inner, kind, queries=None):
    tiers, piece, count = old.shape
    examples = grads.shape[0]

    def piece_of(i, plan_ref):
        return lax.rem(plan_ref[0] - i + tiers, tiers)

    in_specs = [
        pl.BlockSpec((1, piece, count), lambda i, plan_ref: (i, 0, 0)),
        pl.BlockSpec(
            (examples, piece), lambda i, plan_ref: (0, plan_ref[1] * tiers + piece_of(i, plan_ref))
        ),
        pl.BlockSpec((examples, count), lambda i, plan_ref: (0, 0)),
    ]
    args = [old, grads, inner]
    out_specs = [pl.BlockSpec((piece, count), lambda i, plan_ref: (piece_of(i, plan_ref), 0))]
    out_shape = [jax.ShapeDtypeStruct((tiers * piece, count), kind)]
    with_sums = queries is not None
    if with_sums:
        in_specs.append(
            pl.BlockSpec((piece, count), lambda i, plan_ref: (piece_of(i, plan_ref), 0))
        )
        args.append(queries)
        out_specs.append(pl.BlockSpec((3, 8, count), lambda i, plan_ref: (0, 0, 0)))
        out_shape.append(jax.ShapeDtypeStruct((3, 8, count), F32))
    return pl.pallas_call(
        functools.partial(finish_kernel, int(with_sums)),
        grid_spec=pltpu.PrefetchScalarGridSpec(
            num_scalar_prefetch=1, grid=(tiers,), in_specs=in_specs, out_specs=out_specs
        ),
        out_shape=out_shape,
        compiler_params=params(),
        cost_estimate=cost(
            2 * tiers * piece * count * examples, 2 * tiers * piece * (examples + 3 * count)
        ),
        name="finish",
    )(plan, *args)


def curve_kernel(streams, plan_ref, *refs):
    gram_refs = refs[:streams]
    same_ref, other_ref, left_ref, out_ref = refs[streams:]
    i = pl.program_id(0)
    upper = i % 2
    block, width = gram_refs[0].shape

    @pl.when(i == 0)
    def _():
        out_ref[...] = jnp.zeros_like(out_ref)

    def add(vec_ref, quadrant, upper, weight):
        vec = vec_ref[pl.ds(pl.multiple_of(quadrant * width, width), width), :]
        for s in range(streams):
            mapped = dot(gram_refs[s][...].astype(BF), vec)
            start = pl.multiple_of((upper * streams + s) * block, block)
            mapped = mapped * left_ref[pl.ds(start, block), :]
            mapped = jnp.sum(mapped.reshape(block // 8, 8, mapped.shape[1]), axis=0)
            out_ref[...] += weight * mapped

    @pl.when(i < 2)
    def _():
        add(same_ref, upper ^ plan_ref[1], upper, plan_ref[3].astype(F32))

    @pl.when((i >= 2) & (i < 4))
    def _():
        add(other_ref, upper ^ plan_ref[2], upper, 2.0)

    @pl.when((i == 4) & (plan_ref[4] == 1))
    def _():
        add(same_ref, 1, 0, 2.0)


def curve_product(plan, gram, same, other, left):
    rows = gram.shape[0]
    depth, count = same.shape
    width = depth // 2
    streams = 2
    block = width // streams

    def gram_at(s, i, plan_ref):
        skip = (i == 4) & (plan_ref[4] == 0)
        step = jnp.where(skip, 3, i)
        upper = jnp.where(step == 4, 0, step % 2)
        half = jnp.where((step == 2) | (step == 3), 1 - plan_ref[0], plan_ref[0])
        flag = jnp.where(step < 2, plan_ref[1], jnp.where(step < 4, plan_ref[2], 1))
        return (upper * streams + s, half * 2 + (upper ^ flag))

    def whole(i, plan_ref):
        return (0, 0)

    return pl.pallas_call(
        functools.partial(curve_kernel, streams),
        grid_spec=pltpu.PrefetchScalarGridSpec(
            num_scalar_prefetch=1,
            grid=(5,),
            in_specs=[
                pl.BlockSpec((block, width), functools.partial(gram_at, s)) for s in range(streams)
            ]
            + [
                pl.BlockSpec((depth, count), whole),
                pl.BlockSpec((depth, count), whole),
                pl.BlockSpec((rows, count), whole),
            ],
            out_specs=pl.BlockSpec((8, count), whole),
        ),
        out_shape=jax.ShapeDtypeStruct((8, count), F32),
        compiler_params=params(),
        cost_estimate=cost(2 * rows * depth * count, 4 * rows * depth),
        name="curve_product",
    )(plan, *([gram] * streams), same, other, left)


def after(value, *others):
    return lax.optimization_barrier((value,) + others)[0]


def integers(*values):
    return jnp.stack([jnp.asarray(v).astype(jnp.int32) for v in values])


def shards(activations, out_grads, proj_in, proj_out, lengths, gram_old, queries):
    local_count = lengths.shape[0]
    rank = proj_in.shape[1]
    row_count = lax.axis_size("row")
    col_count = lax.axis_size("col")
    rows, cols = gram_old.shape
    count = queries.shape[1]
    tokens = local_count * SEQ
    tiers = row_count // 2
    files = col_count // 2
    piece = rows // tiers
    row = lax.axis_index("row")
    col = lax.axis_index("col")
    z, y = row // 2, row % 2
    x, core = col // 2, col % 2
    total_examples = local_count * row_count * col_count
    scale = (1.0 - decay_rate) / total_examples

    def move(value, goes):
        pairs = []
        for r in range(row_count):
            for c in range(col_count):
                to = goes(r // 2, r % 2, c // 2, c % 2)
                if to is not None:
                    pairs.append((r * col_count + c, (to[0] * 2 + to[1]) * col_count + to[2] * 2 + to[3]))
        return lax.ppermute(value, ("row", "col"), pairs)

    def swap_y(value):
        return move(value, lambda z, y, x, k: (z, 1 - y, x, k))

    def swap_core(value):
        return move(value, lambda z, y, x, k: (z, y, x, 1 - k))

    def ring_z(value, by=1):
        return move(value, lambda z, y, x, k: ((z + by) % tiers, y, x, k))

    def ring_x(value):
        return move(value, lambda z, y, x, k: (z, y, (x + 1) % files, k))

    def flip_x(value, bit):
        return move(value, lambda z, y, x, k: (z, y, x ^ bit, k))

    def spread_z(value):
        return [value] + [ring_z(value, by) for by in range(1, tiers)]

    vec = queries.astype(BF).T
    away = back_product(integers(1 - y, 0), vec, gram_old)
    come = swap_y(away)

    low_in = dot(activations, proj_in).astype(BF)
    low_out = dot(proj_out, out_grads, ((0,), (1,))).astype(BF)
    slot = jnp.arange(tokens, dtype=jnp.int32)
    valid_mask = slot % SEQ < jnp.repeat(lengths, SEQ)
    low_out = jnp.where(valid_mask[None, :], low_out, jnp.zeros((), BF))
    low_out = low_out.reshape(rank, tokens // rank, rank).transpose(1, 0, 2).reshape(tokens, rank)
    local = after(jnp.concatenate([low_in, low_out], axis=0), away)
    factors = [jnp.stack(spread_z(local))]

    here = back_product(after(integers(y, z == col), local), vec, gram_old, queries)
    here = here.reshape(tiers, piece, count)
    come = come.reshape(tiers, piece, count)

    def piece_for(by):
        at = (z + by) % tiers
        one = lax.dynamic_index_in_dim(here, at, 0, keepdims=False)
        two = lax.dynamic_index_in_dim(come, at, 0, keepdims=False)
        return one + two.astype(F32)

    parts = [ring_z(piece_for(by).astype(BF), by) for by in range(1, tiers)]
    total = piece_for(0)

    factors = [after(factors[0], here)]
    for _ in range(files - 1):
        factors.append(ring_x(factors[-1]))
    factors = after(jnp.concatenate(factors, axis=0), come)
    factors = [factors, swap_y(factors)]

    for part in parts:
        total = total + part.astype(F32)
    short = total.astype(BF)
    factors = factors + [swap_core(factors[0]), swap_core(after(factors[1], short))]

    same = spread_z(short)
    other = [swap_y(short)]

    place = integers(row, col)
    grads_col, grads_row = build_grads(place, factors, tiers, rows, cols)
    partial = dot(grads_row, queries.astype(BF))
    inner = partial + swap_y(partial.astype(BF)).astype(F32)
    inner = inner.astype(BF)
    inner = sum(v.astype(F32) for v in reversed(spread_z(inner)))
    inner = (scale * inner).astype(BF)

    block = min(256, rows)
    blocks = rows // block
    at = integers(row * rows - col * cols).reshape(1)
    gram_new = update_gram(
        after(at, partial, other[0]), gram_old, grads_row, grads_col, scale, 0, blocks // 2, block, None
    )
    same = lax.optimization_barrier((*same, gram_new))[:-1]
    same = jnp.stack(same)
    crossed = swap_y(after(same[1:], other[0]))
    other = jnp.concatenate([other[0][None], crossed], axis=0)

    mate = swap_core(same)
    mine = jnp.where(core == z % 2, same, mate)
    cut = tiers // 2
    send = lax.dynamic_slice_in_dim(mine, core * cut, cut, 0)
    found = mine
    for s in range(1, files):
        send = ring_x(send)
        rest = swap_core(send)
        both = jnp.where(
            core == 0, jnp.concatenate([send, rest], 0), jnp.concatenate([rest, send], 0)
        )
        found = jnp.where((x - s) % files == z // 2, both, found)

    gram_new = update_gram(
        after(at, same), gram_old, grads_row, grads_col, scale,
        blocks // 2, blocks - blocks // 2, block, gram_new,
    )
    (vec_same,) = finish(integers(z, y), same, grads_col, inner, BF)
    mapped, sums = finish(integers(z, 0), found, grads_row, inner, F32, queries)
    (vec_other,) = finish(integers(z, 1 - y), other, grads_col, inner, BF)
    plan = integers(
        y, row > 2 * col + y, row > 2 * col + 1 - y, jnp.where(z == col, 1, 2), z == col
    )
    curve = curve_product(plan, gram_new, vec_same, vec_other, mapped)
    sums = jnp.concatenate([sums * (1.0 / col_count), curve[None]], axis=0).sum(axis=1)
    sums = sums + swap_core(sums)
    bit = 1
    while bit < files:
        sums = sums + flip_x(sums, bit)
        bit *= 2
    sums = sums + swap_y(sums)
    around = jnp.stack(spread_z(sums))
    sums = sum(
        lax.dynamic_index_in_dim(around, (z - k) % tiers, 0, keepdims=False) for k in range(tiers)
    )
    norm_now, along, square, curve = sums[0], sums[1], sums[2], sums[3]
    step = norm_now / along
    norm_next = step * step * square - norm_now
    momentum = norm_next / norm_now
    curvature = along - 2.0 * step * square + step * step * curve
    step_next = norm_next / (curvature - momentum * norm_next / step)
    solution = (step + step_next * (1.0 + momentum)) * queries - (step_next * step) * mapped
    return (gram_new, solution)


def solution(mesh):
    in_specs = (
        P(("row", "col"), None),
        P(("row", "col"), None),
        P(),
        P(),
        P(("row", "col")),
        P("row", "col"),
        P("row", None),
    )
    out_specs = (P("row", "col"), P("row", None))
    return jax.shard_map(shards, mesh=mesh, in_specs=in_specs, out_specs=out_specs, check_vma=False)
```

```python
import functools

import jax
import jax.numpy as jnp
from jax import lax
from jax.experimental import pallas as pl
from jax.experimental.pallas import tpu as pltpu
from jax.sharding import PartitionSpec as P

SEQ = 32

decay_rate = 0.5
damping = 1.0

BF = jnp.bfloat16
F32 = jnp.float32
VMEM_BYTES = 40 * 1024 * 1024


def dot(a, b, dims=((1,), (0,))):
    return lax.dot_general(a, b, (dims, ((), ())), preferred_element_type=F32)


def params(mebibytes=24):
    return pltpu.CompilerParams(vmem_limit_bytes=mebibytes * 1024 * 1024)


def cost(flops, moved):
    return pl.CostEstimate(flops=flops, bytes_accessed=moved, transcendentals=0)


def grads_kernel(outs_col, outs_row, at_ref, *refs):
    in_refs, out_refs = refs[:4], refs[4:8]
    col_ref, row_ref, rows_ref = refs[8:]
    _, tokens, rank = in_refs[0].shape
    slots = tokens // SEQ
    halves = tokens // rank
    outs = outs_col + outs_row
    example = lax.broadcasted_iota(jnp.int32, (slots, rank), 0)
    token = lax.broadcasted_iota(jnp.int32, (slots, rank), 1)
    col_at = pl.multiple_of(at_ref[1] * outs_col, outs_col)
    row_at = pl.multiple_of(at_ref[0] * outs_row, outs_row)

    def build(in_ref, k):
        left = []
        for h in range(halves):
            mask = ((token + h * rank) // SEQ == example).astype(F32)
            rows = jnp.concatenate(
                [
                    rows_ref[k, pl.ds(h * rank + col_at, outs_col), :],
                    rows_ref[k, pl.ds(h * rank + row_at, outs_row), :],
                ],
                axis=0,
            )
            spread = rows[:, None, :] * mask[None, :, :]
            left.append(spread.reshape(outs * slots, rank).astype(BF))
        left = jnp.concatenate(left, axis=1)
        return dot(left, in_ref[0]).reshape(outs, slots, rank)

    def pair(part):
        rows_ref[0] = out_refs[part][0].astype(F32)
        rows_ref[1] = out_refs[2 + part][0].astype(F32)
        own, mate = build(in_refs[part], 0), build(in_refs[2 + part], 1)
        even = at_ref[1] % 2 == 0
        both = [jnp.where(even, own, mate), jnp.where(even, mate, own)]
        both = jnp.concatenate(both, axis=1).astype(BF)
        for o in range(outs_col):
            col_ref[:, o * rank : (o + 1) * rank] = both[o]
        for o in range(outs_row):
            row_ref[:, o * rank : (o + 1) * rank] = both[outs_col + o]

    for part in range(2):
        pl.when(pl.program_id(0) == part)(functools.partial(pair, part))


def build_grads(place, ins, outs, tiers, rows, cols):
    count, tokens, rank = ins[0].shape
    slots = tokens // SEQ
    files = count // tiers
    total = 4 * count * slots

    def grads_at(p, i, at_ref):
        z, y, x = at_ref[0] // 2, at_ref[0] % 2, at_ref[1] // 2
        from_x = lax.rem(x - i // tiers + files, files)
        from_z = lax.rem(z - i % tiers + tiers, tiers)
        return ((from_x * tiers + from_z) * 2 + (y ^ p), 0)

    def factor_at(part, p, i, at_ref):
        return (jnp.where(p == part, i, jnp.where(p < part, 0, count - 1)), 0, 0)

    return pl.pallas_call(
        functools.partial(grads_kernel, cols // rank, rows // rank),
        grid_spec=pltpu.PrefetchScalarGridSpec(
            num_scalar_prefetch=1,
            grid=(2, count),
            in_specs=[
                pl.BlockSpec((1, tokens, rank), functools.partial(factor_at, part % 2))
                for part in range(8)
            ],
            out_specs=[
                pl.BlockSpec((2 * slots, cols), grads_at),
                pl.BlockSpec((2 * slots, rows), grads_at),
            ],
            scratch_shapes=[pltpu.VMEM((2, tokens, rank), F32)],
        ),
        out_shape=[
            jax.ShapeDtypeStruct((total, cols), BF),
            jax.ShapeDtypeStruct((total, rows), BF),
        ],
        compiler_params=params(),
        cost_estimate=cost(0, total * (rows + cols)),
        name="build_grads",
    )(place, *ins, *outs)


def back_kernel(streams, plan_ref, *refs):
    vec_ref, gram_refs, out_ref = refs[0], refs[1 : 1 + streams], refs[-1]
    depth = gram_refs[0].shape[0]
    total = None
    for s in range(streams):
        vec = vec_ref[:, s * depth : (s + 1) * depth]
        value = dot(vec, gram_refs[s][...].astype(BF))
        total = value if total is None else total + value
    total = decay_rate * total.T
    if len(refs) > streams + 2:
        own = jnp.where(plan_ref[1] == 1, damping, 0.0)
        total = total + own * refs[streams + 1][...]
    out_ref[...] = total.astype(out_ref.dtype)


def back_product(plan, vec, gram, queries=None, cut=None, before=None):
    count, rows = vec.shape
    width = gram.shape[1] // 2
    block = min(512, width)
    steps = width // block
    streams = 2
    depth = rows // streams
    first, last = (0, steps) if cut is None else (cut * steps // 2, (cut + 1) * steps // 2)

    def gram_at(s, i, plan_ref):
        return (s, plan_ref[0] * steps + first + i)

    in_specs = [pl.BlockSpec((count, rows), lambda i, plan_ref: (0, 0))]
    for s in range(streams):
        in_specs.append(pl.BlockSpec((depth, block), functools.partial(gram_at, s)))
    args = [vec] + [gram] * streams
    kind = BF
    if queries is not None:
        in_specs.append(pl.BlockSpec((block, count), lambda i, plan_ref: (first + i, 0)))
        args.append(queries)
        kind = F32
    alias = {}
    if before is not None:
        in_specs.append(pl.BlockSpec(memory_space=pl.ANY))
        args.append(before)
        alias = {len(args): 0}
    return pl.pallas_call(
        functools.partial(back_kernel, streams),
        grid_spec=pltpu.PrefetchScalarGridSpec(
            num_scalar_prefetch=1,
            grid=(last - first,),
            in_specs=in_specs,
            out_specs=pl.BlockSpec((block, count), lambda i, plan_ref: (first + i, 0)),
        ),
        out_shape=jax.ShapeDtypeStruct((width, count), kind),
        input_output_aliases=alias,
        compiler_params=params(),
        cost_estimate=cost(2 * rows * width * count, 4 * rows * width + 4 * width * count),
        name="back_product",
    )(plan, *args)


def gram_kernel(scale, block, first, at_ref, gram_ref, left_ref, right_ref, *rest):
    out_ref, copy_ref = rest[-2:]
    strip = copy_ref.shape[1] // 3
    left = left_ref[...]
    offset = at_ref[0] + (first + pl.program_id(0)) * block
    ahead = lax.broadcasted_iota(jnp.int32, (block, strip), 0)
    ahead = ahead - lax.broadcasted_iota(jnp.int32, (block, strip), 1)
    for s in range(gram_ref.shape[1] // strip):
        part = slice(s * strip, (s + 1) * strip)
        product = dot(left, right_ref[:, part], ((0,), (0,)))
        value = decay_rate * gram_ref[:, part] + scale * product
        value = value + jnp.where(ahead == s * strip - offset, damping, 0.0)
        out_ref[:, part] = value
        short = value.astype(BF)
        for k in range(3):

            @pl.when(at_ref[1 + k] == s)
            def _(k=k, short=short):
                copy_ref[:, k * strip : (k + 1) * strip] = short


def update_gram(at, gram, left, right, scale, first, count, block, before):
    rows, cols = gram.shape
    examples = left.shape[0]
    width = 3 * (cols // 4)
    in_specs = [
        pl.BlockSpec((block, cols), lambda i, at_ref: (first + i, 0)),
        pl.BlockSpec((examples, block), lambda i, at_ref: (0, first + i)),
        pl.BlockSpec((examples, cols), lambda i, at_ref: (0, 0)),
    ]
    args = [gram, left, right]
    alias = {}
    if before is not None:
        in_specs.append(pl.BlockSpec(memory_space=pl.ANY))
        args.append(before)
        alias = {4: 0}
    return pl.pallas_call(
        functools.partial(gram_kernel, scale, block, first),
        grid_spec=pltpu.PrefetchScalarGridSpec(
            num_scalar_prefetch=1,
            grid=(count,),
            in_specs=in_specs,
            out_specs=[
                pl.BlockSpec((block, cols), lambda i, at_ref: (first + i, 0)),
                pl.BlockSpec((block, width), lambda i, at_ref: (i, 0)),
            ],
        ),
        out_shape=[
            jax.ShapeDtypeStruct((rows, cols), F32),
            jax.ShapeDtypeStruct((count * block, width), BF),
        ],
        input_output_aliases=alias,
        compiler_params=params(30),
        cost_estimate=cost(0, count * block * cols),
        name="update_gram",
    )(at, *args)


def finish_kernel(with_sums, plan_ref, old_ref, grad_ref, inner_ref, *refs):
    value = old_ref[0].astype(F32) + dot(grad_ref[...], inner_ref[...], ((0,), (0,)))
    refs[-1 - with_sums][...] = value.astype(refs[-1 - with_sums].dtype)
    if with_sums:
        query = refs[0][...]
        sums_ref = refs[-1]

        @pl.when(pl.program_id(0) == 0)
        def _():
            sums_ref[...] = jnp.zeros_like(sums_ref)

        rows, count = value.shape
        for k, product in enumerate((query * query, query * value, value * value)):
            sums_ref[k] += jnp.sum(product.reshape(rows // 8, 8, count), axis=0)


def finish(plan, old, grads, inner, kind, queries=None):
    tiers, piece, count = old.shape
    examples = grads.shape[0]

    def piece_of(i, plan_ref):
        return lax.rem(plan_ref[0] - i + tiers, tiers)

    in_specs = [
        pl.BlockSpec((1, piece, count), lambda i, plan_ref: (i, 0, 0)),
        pl.BlockSpec(
            (examples, piece), lambda i, plan_ref: (0, plan_ref[1] * tiers + piece_of(i, plan_ref))
        ),
        pl.BlockSpec((examples, count), lambda i, plan_ref: (0, 0)),
    ]
    args = [old, grads, inner]
    out_specs = [pl.BlockSpec((piece, count), lambda i, plan_ref: (piece_of(i, plan_ref), 0))]
    out_shape = [jax.ShapeDtypeStruct((tiers * piece, count), kind)]
    with_sums = queries is not None
    if with_sums:
        in_specs.append(
            pl.BlockSpec((piece, count), lambda i, plan_ref: (piece_of(i, plan_ref), 0))
        )
        args.append(queries)
        out_specs.append(pl.BlockSpec((3, 8, count), lambda i, plan_ref: (0, 0, 0)))
        out_shape.append(jax.ShapeDtypeStruct((3, 8, count), F32))
    return pl.pallas_call(
        functools.partial(finish_kernel, int(with_sums)),
        grid_spec=pltpu.PrefetchScalarGridSpec(
            num_scalar_prefetch=1, grid=(tiers,), in_specs=in_specs, out_specs=out_specs
        ),
        out_shape=out_shape,
        compiler_params=params(),
        cost_estimate=cost(
            2 * tiers * piece * count * examples, 2 * tiers * piece * (examples + 3 * count)
        ),
        name="finish",
    )(plan, *args)


def curve_kernel(pieces, plan_ref, *refs):
    copy_refs = refs[:pieces]
    same_ref, other_ref, left_ref, out_ref = refs[pieces:]
    block = copy_refs[0].shape[0]
    width = same_ref.shape[0] // 2
    weight = plan_ref[2].astype(F32)
    out_ref[...] = jnp.zeros_like(out_ref)

    def take(ref, quadrant):
        return ref[pl.ds(pl.multiple_of(quadrant * width, width), width), :]

    def add(k, mapped):
        mapped = mapped * left_ref[k * block : (k + 1) * block, :]
        out_ref[...] += jnp.sum(mapped.reshape(block // 8, 8, mapped.shape[1]), axis=0)

    for k in range(pieces):
        upper = k * 2 // pieces
        mapped = weight * dot(copy_refs[k][:, :width], take(same_ref, upper ^ plan_ref[0]))
        mapped = mapped + 2.0 * dot(
            copy_refs[k][:, width : 2 * width], take(other_ref, upper ^ plan_ref[1])
        )
        add(k, mapped)

    @pl.when(plan_ref[3] == 1)
    def _():
        for k in range(pieces // 2):
            add(k, 2.0 * dot(copy_refs[k][:, 2 * width :], same_ref[width:, :]))


def curve_product(plan, copies, same, other, left):
    depth, count = same.shape
    rows = left.shape[0]
    return pl.pallas_call(
        functools.partial(curve_kernel, len(copies)),
        in_specs=[pl.BlockSpec(memory_space=pltpu.SMEM)]
        + [pl.BlockSpec(memory_space=pltpu.VMEM)] * (len(copies) + 3),
        out_specs=pl.BlockSpec(memory_space=pltpu.VMEM),
        out_shape=jax.ShapeDtypeStruct((8, count), F32),
        compiler_params=params(32),
        cost_estimate=cost(2 * rows * depth * count, 2 * rows * depth),
        name="curve_product",
    )(plan, *copies, same, other, left)


def combine_kernel(sums_ref, query_ref, mapped_ref, out_ref):
    norm_now, along = sums_ref[0:1, :], sums_ref[1:2, :]
    square, curve = sums_ref[2:3, :], sums_ref[3:4, :]
    step = norm_now / along
    norm_next = step * step * square - norm_now
    momentum = norm_next / norm_now
    curvature = along - 2.0 * step * square + step * step * curve
    step_next = norm_next / (curvature - momentum * norm_next / step)
    here = step + step_next * (1.0 + momentum)
    out_ref[...] = here * query_ref[...] - (step_next * step) * mapped_ref[...]


def combine(sums, queries, mapped):
    rows, count = queries.shape
    block = rows // 4
    return pl.pallas_call(
        combine_kernel,
        grid=(rows // block,),
        in_specs=[
            pl.BlockSpec(sums.shape, lambda i: (0, 0)),
            pl.BlockSpec((block, count), lambda i: (i, 0)),
            pl.BlockSpec((block, count), lambda i: (i, 0)),
        ],
        out_specs=pl.BlockSpec((block, count), lambda i: (i, 0)),
        out_shape=jax.ShapeDtypeStruct((rows, count), F32),
        compiler_params=params(),
        cost_estimate=cost(3 * rows * count, 12 * rows * count),
        name="combine",
    )(sums, queries, mapped)


def after(value, *others):
    return lax.optimization_barrier((value,) + others)[0]


def integers(*values):
    return jnp.stack([jnp.asarray(v).astype(jnp.int32) for v in values])


def shards(activations, out_grads, proj_in, proj_out, lengths, gram_old, queries):
    local_count = lengths.shape[0]
    rank = proj_in.shape[1]
    row_count = lax.axis_size("row")
    col_count = lax.axis_size("col")
    rows, cols = gram_old.shape
    count = queries.shape[1]
    tokens = local_count * SEQ
    tiers = row_count // 2
    files = col_count // 2
    piece = rows // tiers
    row = lax.axis_index("row")
    col = lax.axis_index("col")
    z, y = row // 2, row % 2
    x, core = col // 2, col % 2
    total_examples = local_count * row_count * col_count
    scale = (1.0 - decay_rate) / total_examples

    def move(value, goes):
        pairs = []
        for r in range(row_count):
            for c in range(col_count):
                to = goes(r // 2, r % 2, c // 2, c % 2)
                if to is not None:
                    pairs.append((r * col_count + c, (to[0] * 2 + to[1]) * col_count + to[2] * 2 + to[3]))
        return lax.ppermute(value, ("row", "col"), pairs)

    def swap_y(value):
        return move(value, lambda z, y, x, k: (z, 1 - y, x, k))

    def swap_core(value):
        return move(value, lambda z, y, x, k: (z, y, x, 1 - k))

    def ring_z(value, by=1):
        return move(value, lambda z, y, x, k: ((z + by) % tiers, y, x, k))

    def ring_x(value):
        return move(value, lambda z, y, x, k: (z, y, (x + 1) % files, k))

    def flip_x(value, bit):
        return move(value, lambda z, y, x, k: (z, y, x ^ bit, k))

    def spread_z(value):
        return [value] + [ring_z(value, by) for by in range(1, tiers)]

    vec = queries.astype(BF).T
    away = back_product(integers(1 - y, 0), vec, gram_old)
    come = swap_y(away)

    proj_in, proj_out, _ = lax.optimization_barrier((proj_in, proj_out, away))
    low_in = dot(activations, proj_in).astype(BF)
    low_out = dot(proj_out, out_grads, ((0,), (1,))).astype(BF)
    slot = jnp.arange(tokens, dtype=jnp.int32)
    valid_mask = slot % SEQ < jnp.repeat(lengths, SEQ)
    low_out = jnp.where(valid_mask[None, :], low_out, jnp.zeros((), BF))
    low_out = low_out.reshape(rank, tokens // rank, rank).transpose(1, 0, 2).reshape(tokens, rank)
    local = jnp.concatenate([low_in, low_out], axis=0)

    plan = after(integers(y, z == col), local)
    here = back_product(plan, vec, gram_old, queries, 0)
    factors = spread_z(after(local, here))
    here = back_product(plan, vec, gram_old, queries, 1, here)
    here = here.reshape(tiers, piece, count)
    come = come.reshape(tiers, piece, count)

    def piece_for(by):
        at = (z + by) % tiers
        one = lax.dynamic_index_in_dim(here, at, 0, keepdims=False)
        two = lax.dynamic_index_in_dim(come, at, 0, keepdims=False)
        return one + two.astype(F32)

    sends = [piece_for(by).astype(BF) for by in range(1, tiers)]
    parts = [ring_z(sends[by - 1], by) for by in range(1, tiers)]
    total = piece_for(0)

    def ring(value):
        got = [value]
        for _ in range(files - 1):
            got.append(ring_x(got[-1]))
        return got

    factors = lax.optimization_barrier((*factors, *sends))[:tiers]
    ins = jnp.stack([f[:tokens] for f in factors])
    outs = jnp.stack([f[tokens:] for f in factors])
    ins = ring(ins)
    outs = [outs, swap_y(outs)]
    held = lax.optimization_barrier((*ins, *outs, parts[0]))
    ins = jnp.concatenate(held[:files], axis=0)
    outs = jnp.stack(held[files : files + 2])
    ins = [ins, swap_y(ins)]
    outs = ring(outs)
    outs = [jnp.concatenate([o[p] for o in outs], axis=0) for p in range(2)]

    for part in parts:
        total = total + part.astype(F32)
    short = total.astype(BF)
    ins = ins + [swap_core(f) for f in ins]
    outs = outs + [swap_core(f) for f in outs]

    same = spread_z(short)
    other = [swap_y(after(short, ins[3]))]

    place = integers(row, col)
    grads_col, grads_row = build_grads(place, ins, outs, tiers, rows, cols)
    partial = dot(grads_row, queries.astype(BF))
    inner = partial + swap_y(partial.astype(BF)).astype(F32)
    inner = inner.astype(BF)
    inner = sum(v.astype(F32) for v in reversed(spread_z(inner)))
    inner = (scale * inner).astype(BF)

    flags = integers(row > 2 * col + y, row > 2 * col + 1 - y)
    block = min(256, rows // 4)
    blocks = rows // block // 4
    gram_new = None
    copies = []

    def update(k, wait):
        upper = k // 2
        at = integers(
            row * rows - col * cols,
            2 * y + (upper ^ flags[0]),
            2 * (1 - y) + (upper ^ flags[1]),
            jnp.where(z == col, 2 * y + 1, -1) if upper == 0 else -1,
        )
        gram, copy = update_gram(
            after(at, *wait), gram_old, grads_row, grads_col, scale, k * blocks, blocks, block, gram_new
        )
        copies.append(copy)
        return gram

    gram_new = update(0, (partial,))
    gram_new = update(1, (other[0],))
    same = lax.optimization_barrier((*same, gram_new))[:-1]
    same = jnp.stack(same)
    crossed = swap_y(after(same[1:], other[0]))

    mate = swap_core(same)
    mine = jnp.where(core == z % 2, same, mate)
    cut = tiers // 2
    send = lax.dynamic_slice_in_dim(mine, core * cut, cut, 0)
    found = mine
    for s in range(1, files):
        send = ring_x(send)
        rest = swap_core(send)
        both = jnp.where(
            core == 0, jnp.concatenate([send, rest], 0), jnp.concatenate([rest, send], 0)
        )
        found = jnp.where((x - s) % files == z // 2, both, found)

    gram_new = update(2, (same,))
    gram_new = update(3, (mine,))
    crossed = after(crossed, copies[3])
    other = jnp.concatenate([other[0][None], crossed], axis=0)
    (vec_same,) = finish(integers(z, y), same, grads_col, inner, BF)
    mapped, sums = finish(integers(z, 0), found, grads_row, inner, F32, queries)
    (vec_other,) = finish(integers(z, 1 - y), other, grads_col, inner, BF)
    plan = jnp.concatenate([flags, integers(jnp.where(z == col, 1, 2), z == col)])
    curve = curve_product(plan, copies, vec_same, vec_other, mapped)
    sums = jnp.concatenate([sums * (1.0 / col_count), curve[None]], axis=0).sum(axis=1)
    sums = sums + swap_core(sums)
    bit = 1
    while bit < files:
        sums = sums + flip_x(sums, bit)
        bit *= 2
    sums = sums + swap_y(sums)
    around = jnp.stack(spread_z(sums))
    sums = sum(
        lax.dynamic_index_in_dim(around, (z - k) % tiers, 0, keepdims=False) for k in range(tiers)
    )
    solution = combine(sums, queries, mapped)
    return (gram_new, solution)


def solution(mesh):
    in_specs = (
        P(("row", "col"), None),
        P(("row", "col"), None),
        P(),
        P(),
        P(("row", "col")),
        P("row", "col"),
        P("row", None),
    )
    out_specs = (P("row", "col"), P("row", None))
    return jax.shard_map(shards, mesh=mesh, in_specs=in_specs, out_specs=out_specs, check_vma=False)
```

```python
import functools

import jax
import jax.numpy as jnp
from jax import lax
from jax.experimental import pallas as pl
from jax.experimental.pallas import tpu as pltpu
from jax.sharding import PartitionSpec as P

SEQ = 32

decay_rate = 0.5
damping = 1.0

BF = jnp.bfloat16
F32 = jnp.float32
VMEM_BYTES = 40 * 1024 * 1024


def dot(a, b, dims=((1,), (0,))):
    return lax.dot_general(a, b, (dims, ((), ())), preferred_element_type=F32)


def params(mebibytes=24):
    return pltpu.CompilerParams(vmem_limit_bytes=mebibytes * 1024 * 1024)


def cost(flops, moved):
    return pl.CostEstimate(flops=flops, bytes_accessed=moved, transcendentals=0)


def grads_kernel(parts, outs_col, outs_row, at_ref, *refs):
    factor_refs = refs[: 2 * parts]
    col_ref, row_ref, rows_ref = refs[2 * parts :]
    rank = factor_refs[0].shape[2]
    tokens = factor_refs[0].shape[1] // 2
    slots = tokens // SEQ
    halves = tokens // rank
    outs = outs_col + outs_row
    example = lax.broadcasted_iota(jnp.int32, (slots, rank), 0)
    token = lax.broadcasted_iota(jnp.int32, (slots, rank), 1)
    col_at = pl.multiple_of(at_ref[1] * outs_col, outs_col)
    row_at = pl.multiple_of(at_ref[0] * outs_row, outs_row)

    def build(factor_ref, k):
        left = []
        for h in range(halves):
            mask = ((token + h * rank) // SEQ == example).astype(F32)
            rows = jnp.concatenate(
                [
                    rows_ref[k, pl.ds(h * rank + col_at, outs_col), :],
                    rows_ref[k, pl.ds(h * rank + row_at, outs_row), :],
                ],
                axis=0,
            )
            spread = rows[:, None, :] * mask[None, :, :]
            left.append(spread.reshape(outs * slots, rank).astype(BF))
        left = jnp.concatenate(left, axis=1)
        return dot(left, factor_ref[0, :tokens, :]).reshape(outs, slots, rank)

    def pair(own_ref, mate_ref):
        rows_ref[0] = own_ref[0, tokens:, :].astype(F32)
        rows_ref[1] = mate_ref[0, tokens:, :].astype(F32)
        own, mate = build(own_ref, 0), build(mate_ref, 1)
        even = at_ref[1] % 2 == 0
        both = [jnp.where(even, own, mate), jnp.where(even, mate, own)]
        both = jnp.concatenate(both, axis=1).astype(BF)
        for o in range(outs_col):
            col_ref[:, o * rank : (o + 1) * rank] = both[o]
        for o in range(outs_row):
            row_ref[:, o * rank : (o + 1) * rank] = both[outs_col + o]

    for part in range(parts):
        pl.when(pl.program_id(0) == part)(
            functools.partial(pair, factor_refs[part], factor_refs[parts + part])
        )


def build_grads(place, own, mate, rows, cols):
    parts = len(own)
    tiers, depth, rank = own[0].shape
    tokens = depth // 2
    slots = tokens // SEQ
    files = parts // 2
    total = 2 * parts * tiers * slots

    def grads_at(p, i, at_ref):
        z, y, x = at_ref[0] // 2, at_ref[0] % 2, at_ref[1] // 2
        from_x = lax.rem(x - p // 2 + files, files)
        from_z = lax.rem(z - i + tiers, tiers)
        return ((from_x * tiers + from_z) * 2 + (y ^ (p % 2)), 0)

    def factor_at(part, p, i, at_ref):
        return (jnp.where(p == part, i, jnp.where(p < part, 0, tiers - 1)), 0, 0)

    return pl.pallas_call(
        functools.partial(grads_kernel, parts, cols // rank, rows // rank),
        grid_spec=pltpu.PrefetchScalarGridSpec(
            num_scalar_prefetch=1,
            grid=(parts, tiers),
            in_specs=[
                pl.BlockSpec((1, depth, rank), functools.partial(factor_at, part % parts))
                for part in range(2 * parts)
            ],
            out_specs=[
                pl.BlockSpec((2 * slots, cols), grads_at),
                pl.BlockSpec((2 * slots, rows), grads_at),
            ],
            scratch_shapes=[pltpu.VMEM((2, tokens, rank), F32)],
        ),
        out_shape=[
            jax.ShapeDtypeStruct((total, cols), BF),
            jax.ShapeDtypeStruct((total, rows), BF),
        ],
        compiler_params=params(),
        cost_estimate=cost(2 * total * (rows + cols) * tokens, 2 * total * (rows + cols)),
        name="build_grads",
    )(place, *own, *mate)


def back_kernel(streams, plan_ref, *refs):
    vec_ref, gram_refs = refs[0], refs[1 : 1 + streams]
    out_ref, copy_ref = refs[-2:]
    depth = gram_refs[0].shape[0]
    total = None
    for s in range(streams):
        block = gram_refs[s][...].astype(BF)
        copy_ref[s * depth : (s + 1) * depth, :] = block
        value = dot(vec_ref[:, s * depth : (s + 1) * depth], block)
        total = value if total is None else total + value
    total = decay_rate * total.T
    if len(refs) > streams + 3:
        own = jnp.where(plan_ref[1] == 1, damping, 0.0)
        total = total + own * refs[streams + 1][...]
    out_ref[...] = total.astype(out_ref.dtype)


def back_product(plan, vec, gram, queries=None):
    count, rows = vec.shape
    width = gram.shape[1] // 2
    block = min(512, width)
    steps = width // block
    streams = 2
    depth = rows // streams

    def gram_at(s, i, plan_ref):
        return (s, plan_ref[0] * steps + i)

    in_specs = [pl.BlockSpec((count, rows), lambda i, plan_ref: (0, 0))]
    for s in range(streams):
        in_specs.append(pl.BlockSpec((depth, block), functools.partial(gram_at, s)))
    args = [vec] + [gram] * streams
    kind = BF
    if queries is not None:
        in_specs.append(pl.BlockSpec((block, count), lambda i, plan_ref: (i, 0)))
        args.append(queries)
        kind = F32
    return pl.pallas_call(
        functools.partial(back_kernel, streams),
        grid_spec=pltpu.PrefetchScalarGridSpec(
            num_scalar_prefetch=1,
            grid=(steps,),
            in_specs=in_specs,
            out_specs=[
                pl.BlockSpec((block, count), lambda i, plan_ref: (i, 0)),
                pl.BlockSpec((rows, block), lambda i, plan_ref: (0, i)),
            ],
        ),
        out_shape=[
            jax.ShapeDtypeStruct((width, count), kind),
            jax.ShapeDtypeStruct((rows, width), BF),
        ],
        compiler_params=params(),
        cost_estimate=cost(2 * rows * width * count, 4 * rows * width + 4 * width * count),
        name="back_product",
    )(plan, *args)


def gram_kernel(scale, strip, at_ref, same_ref, other_ref, left_ref, right_ref, out_ref):
    j, i = pl.program_id(0), pl.program_id(1)
    block, width = out_ref.shape
    left = left_ref[...]
    offset = at_ref[0] + i * block - (at_ref[1] ^ j) * width
    ahead = lax.broadcasted_iota(jnp.int32, (block, strip), 0)
    ahead = ahead - lax.broadcasted_iota(jnp.int32, (block, strip), 1)

    def write(old_ref):
        for s in range(width // strip):
            part = slice(s * strip, (s + 1) * strip)
            product = dot(left, right_ref[:, part], ((0,), (0,)))
            value = decay_rate * old_ref[:, part].astype(F32) + scale * product
            out_ref[:, part] = value + jnp.where(ahead == s * strip - offset, damping, 0.0)

    pl.when(j == 0)(functools.partial(write, same_ref))
    pl.when(j == 1)(functools.partial(write, other_ref))


def update_gram(at, same, other, left, right, scale):
    rows, width = same.shape
    examples = left.shape[0]
    block = min(512, rows)
    steps = rows // block
    strip = min(1024, width)
    return pl.pallas_call(
        functools.partial(gram_kernel, scale, strip),
        grid_spec=pltpu.PrefetchScalarGridSpec(
            num_scalar_prefetch=1,
            grid=(2, steps),
            in_specs=[
                pl.BlockSpec(
                    (block, width), lambda j, i, at_ref: (jnp.where(j == 0, i, steps - 1), 0)
                ),
                pl.BlockSpec((block, width), lambda j, i, at_ref: (jnp.where(j == 1, i, 0), 0)),
                pl.BlockSpec((examples, block), lambda j, i, at_ref: (0, i)),
                pl.BlockSpec((examples, width), lambda j, i, at_ref: (0, at_ref[1] ^ j)),
            ],
            out_specs=pl.BlockSpec((block, width), lambda j, i, at_ref: (i, at_ref[1] ^ j)),
        ),
        out_shape=jax.ShapeDtypeStruct((rows, 2 * width), F32),
        compiler_params=params(),
        cost_estimate=cost(4 * rows * width * examples, 8 * rows * width),
        name="update_gram",
    )(at, same, other, left, right)


def tail_kernel(scale, even, tiers, plan_ref, *refs):
    same_ref, other_ref, found_refs = refs[0], refs[1], refs[2:5]
    col_ref, row_ref, inner_ref, query_ref, old_same_ref, old_other_ref = refs[5:11]
    mapped_ref, sums_ref, vec_same_ref, vec_other_ref = refs[11:]
    _, piece, count = same_ref.shape
    depth = tiers * piece
    width = depth // 2
    inner = inner_ref[...]
    tier, y = plan_ref[0], plan_ref[1]
    source = plan_ref[6] == 1
    along, square = jnp.zeros((8, count), F32), jnp.zeros((8, count), F32)
    norm = jnp.zeros((8, count), F32)

    def fold(value):
        return jnp.sum(value.reshape(value.shape[0] // 8, 8, count), axis=0)

    for s in range(tiers):
        quarter = lax.rem(tier - s + tiers, tiers)
        rows = pl.ds(pl.multiple_of(quarter * piece, piece), piece)

        def low_rank(ref, start):
            part = ref[:, pl.ds(pl.multiple_of(start * piece, piece), piece)]
            return dot(part, inner, ((0,), (0,)))

        own = same_ref[s]
        value = own.astype(F32) + low_rank(col_ref, y * tiers + quarter)
        vec_same_ref[rows, :] = value.astype(BF)
        value = other_ref[s].astype(F32) + low_rank(col_ref, (1 - y) * tiers + quarter)
        vec_other_ref[rows, :] = value.astype(BF)
        got = found_refs[0][s].astype(F32) + found_refs[1][s].astype(F32) + found_refs[2][s].astype(F32)
        value = jnp.where(source, own.astype(F32), got) + low_rank(row_ref, quarter)
        mapped_ref[rows, :] = value
        query = query_ref[rows, :]
        norm += fold(query * query)
        along += fold(query * value)
        square += fold(value * value)

    def take(ref, quadrant):
        return ref[pl.ds(pl.multiple_of(quadrant * width, width), width), :]

    def columns(ref, k, quadrant):
        start = pl.multiple_of(quadrant * width, width)
        return ref[k * piece : (k + 1) * piece, pl.ds(start, width)]

    weight = decay_rate * plan_ref[4].astype(F32)
    sums_ref[...] = jnp.zeros_like(sums_ref)
    for k in range(tiers):
        upper = k * 2 // tiers
        quadrant = upper ^ plan_ref[2]
        total = weight * dot(columns(old_same_ref, k, quadrant), take(vec_same_ref, quadrant))
        quadrant = upper ^ plan_ref[3]
        total += 2.0 * decay_rate * dot(
            columns(old_other_ref, k, quadrant), take(vec_other_ref, quadrant)
        )
        sums_ref[3] += fold(total * mapped_ref[k * piece : (k + 1) * piece, :])

    @pl.when(plan_ref[5] == 1)
    def _():
        for k in range(tiers // 2):
            total = 2.0 * decay_rate * dot(columns(old_same_ref, k, 1), take(vec_same_ref, 1))
            sums_ref[3] += fold(total * mapped_ref[k * piece : (k + 1) * piece, :])

    here = dot(row_ref[...], mapped_ref[...].astype(BF))
    half = pl.ds(pl.multiple_of(y * depth, depth), depth)
    there = dot(col_ref[:, half], vec_same_ref[...])
    half = pl.ds(pl.multiple_of((1 - y) * depth, depth), depth)
    there += dot(col_ref[:, half], vec_other_ref[...])
    sums_ref[3] += scale * fold(here * there) + even * damping * square
    sums_ref[0] = even * norm
    sums_ref[1] = even * along
    sums_ref[2] = even * square


def tail(plan, same, other, found, grads_col, grads_row, inner, queries, old_same, old_other, scale, even):
    tiers, piece, count = same.shape
    rows = queries.shape[0]
    args = [same, other, *found, grads_col, grads_row, inner, queries, old_same, old_other]
    return pl.pallas_call(
        functools.partial(tail_kernel, scale, even, tiers),
        in_specs=[pl.BlockSpec(memory_space=pltpu.SMEM)]
        + [pl.BlockSpec(memory_space=pltpu.VMEM)] * len(args),
        out_specs=[pl.BlockSpec(memory_space=pltpu.VMEM)] * 2,
        out_shape=[
            jax.ShapeDtypeStruct((rows, count), F32),
            jax.ShapeDtypeStruct((4, 8, count), F32),
        ],
        scratch_shapes=[pltpu.VMEM((rows, count), BF), pltpu.VMEM((rows, count), BF)],
        compiler_params=params(16),
        cost_estimate=cost(4 * rows * rows * count, 4 * rows * rows),
        name="tail",
    )(plan, *args)


def combine_kernel(sums_ref, query_ref, mapped_ref, out_ref):
    norm_now, along = sums_ref[0:1, :], sums_ref[1:2, :]
    square, curve = sums_ref[2:3, :], sums_ref[3:4, :]
    step = norm_now / along
    norm_next = step * step * square - norm_now
    momentum = norm_next / norm_now
    curvature = along - 2.0 * step * square + step * step * curve
    step_next = norm_next / (curvature - momentum * norm_next / step)
    here = step + step_next * (1.0 + momentum)
    out_ref[...] = here * query_ref[...] - (step_next * step) * mapped_ref[...]


def combine(sums, queries, mapped):
    rows, count = queries.shape
    block = rows // 4
    return pl.pallas_call(
        combine_kernel,
        grid=(rows // block,),
        in_specs=[
            pl.BlockSpec(sums.shape, lambda i: (0, 0)),
            pl.BlockSpec((block, count), lambda i: (i, 0)),
            pl.BlockSpec((block, count), lambda i: (i, 0)),
        ],
        out_specs=pl.BlockSpec((block, count), lambda i: (i, 0)),
        out_shape=jax.ShapeDtypeStruct((rows, count), F32),
        compiler_params=params(),
        cost_estimate=cost(3 * rows * count, 12 * rows * count),
        name="combine",
    )(sums, queries, mapped)


def after(value, *others):
    return lax.optimization_barrier((value,) + others)[0]


def integers(*values):
    return jnp.stack([jnp.asarray(v).astype(jnp.int32) for v in values])


def shards(activations, out_grads, proj_in, proj_out, lengths, gram_old, queries):
    local_count = lengths.shape[0]
    rank = proj_in.shape[1]
    row_count = lax.axis_size("row")
    col_count = lax.axis_size("col")
    rows, cols = gram_old.shape
    count = queries.shape[1]
    tokens = local_count * SEQ
    tiers = row_count // 2
    files = col_count // 2
    piece = rows // tiers
    row = lax.axis_index("row")
    col = lax.axis_index("col")
    z, y = row // 2, row % 2
    x, core = col // 2, col % 2
    total_examples = local_count * row_count * col_count
    scale = (1.0 - decay_rate) / total_examples

    def move(value, goes):
        pairs = []
        for r in range(row_count):
            for c in range(col_count):
                to = goes(r // 2, r % 2, c // 2, c % 2)
                if to is not None:
                    pairs.append((r * col_count + c, (to[0] * 2 + to[1]) * col_count + to[2] * 2 + to[3]))
        return lax.ppermute(value, ("row", "col"), pairs)

    def swap_y(value):
        return move(value, lambda z, y, x, k: (z, 1 - y, x, k))

    def swap_core(value):
        return move(value, lambda z, y, x, k: (z, y, x, 1 - k))

    def ring_z(value, by=1):
        return move(value, lambda z, y, x, k: ((z + by) % tiers, y, x, k))

    def ring_x(value):
        return move(value, lambda z, y, x, k: (z, y, (x + 1) % files, k))

    def flip_x(value, bit):
        return move(value, lambda z, y, x, k: (z, y, x ^ bit, k))

    def spread_z(value):
        return [value] + [ring_z(value, by) for by in range(1, tiers)]

    vec = queries.astype(BF).T
    away, old_other = back_product(integers(1 - y, 0), vec, gram_old)
    come = swap_y(away)

    low_in = dot(activations, proj_in).astype(BF)
    low_out = dot(proj_out, out_grads, ((0,), (1,))).astype(BF)
    slot = jnp.arange(tokens, dtype=jnp.int32)
    valid_mask = slot % SEQ < jnp.repeat(lengths, SEQ)
    low_out = jnp.where(valid_mask[None, :], low_out, jnp.zeros((), BF))
    low_out = low_out.reshape(rank, tokens // rank, rank).transpose(1, 0, 2).reshape(tokens, rank)
    local = after(jnp.concatenate([low_in, low_out], axis=0), away)
    factors = spread_z(local)

    here, old_same = back_product(after(integers(y, z == col), local), vec, gram_old, queries)
    here = here.reshape(tiers, piece, count)
    come = come.reshape(tiers, piece, count)

    def piece_for(by):
        at = (z + by) % tiers
        one = lax.dynamic_index_in_dim(here, at, 0, keepdims=False)
        two = lax.dynamic_index_in_dim(come, at, 0, keepdims=False)
        return one + two.astype(F32)

    sends = [piece_for(by).astype(BF) for by in range(1, tiers)]
    parts = [ring_z(sends[by - 1], by) for by in range(1, tiers)]

    factors = jnp.stack(factors)
    own = []
    for dx in range(files):
        across = factors
        if dx:
            across = move(factors, lambda z, y, x, k: (z, y, (x + dx) % files, k))
        own.append(across)
        own.append(swap_y(after(across, *sends)))

    total = piece_for(0)
    for part in parts:
        total = total + part.astype(F32)
    short = total.astype(BF)
    own = lax.optimization_barrier((*own, short))[:-1]
    mate = [swap_core(f) for f in own]

    same = spread_z(short)
    grads_col, grads_row = build_grads(integers(row, col), own, mate, rows, cols)
    partial = dot(grads_row, queries.astype(BF))
    inner = (partial + swap_y(partial.astype(BF)).astype(F32)).astype(BF)
    sums = spread_z(inner)
    same = lax.optimization_barrier((*same, partial))[:-1]
    stacked = jnp.stack(same)
    other = swap_y(stacked)

    def goes_core(z, y, x, k):
        return (z, y, x, 1 - k) if 2 * x + k == z else None

    found = [move(stacked, goes_core)]
    for flip in range(2):
        got = None
        for dx in range(1, files):

            def goes(z, y, x, k):
                return (z, y, (x + dx) % files, k ^ flip) if 2 * x + k == z else None

            came = move(stacked, goes)
            got = came if got is None else got + came
        found.append(got)

    at = after(integers(row * rows - col * cols, y), stacked, inner)
    gram_new = update_gram(at, old_same, old_other, grads_row, grads_col, scale)
    inner = sum(v.astype(F32) for v in reversed(sums))
    inner = (scale * inner).astype(BF)
    plan = integers(
        z, y, row > 2 * col + y, row > 2 * col + 1 - y, jnp.where(z == col, 1, 2), z == col, z == col
    )
    mapped, sums = tail(
        after(plan, gram_new), stacked, other, found, grads_col, grads_row, inner, queries,
        old_same, old_other, scale, 1.0 / col_count,
    )
    sums = jnp.sum(sums, axis=1)
    sums = sums + swap_core(sums)
    bit = 1
    while bit < files:
        sums = sums + flip_x(sums, bit)
        bit *= 2
    sums = sums + swap_y(sums)
    around = jnp.stack(spread_z(sums))
    sums = sum(
        lax.dynamic_index_in_dim(around, (z - k) % tiers, 0, keepdims=False) for k in range(tiers)
    )
    solution = combine(sums, queries, mapped)
    return (gram_new, solution)


def solution(mesh):
    in_specs = (
        P(("row", "col"), None),
        P(("row", "col"), None),
        P(),
        P(),
        P(("row", "col")),
        P("row", "col"),
        P("row", None),
    )
    out_specs = (P("row", "col"), P("row", None))
    return jax.shard_map(shards, mesh=mesh, in_specs=in_specs, out_specs=out_specs, check_vma=False)
```

```python
import functools

import jax
import jax.numpy as jnp
from jax import lax
from jax.experimental import pallas as pl
from jax.experimental.pallas import tpu as pltpu
from jax.sharding import PartitionSpec as P

SEQ = 32

decay_rate = 0.5
damping = 1.0

BF = jnp.bfloat16
F32 = jnp.float32
VMEM_BYTES = 40 * 1024 * 1024


def dot(a, b, dims=((1,), (0,))):
    return lax.dot_general(a, b, (dims, ((), ())), preferred_element_type=F32)


def params(mebibytes=24):
    return pltpu.CompilerParams(vmem_limit_bytes=mebibytes * 1024 * 1024)


def cost(flops, moved):
    return pl.CostEstimate(flops=flops, bytes_accessed=moved, transcendentals=0)


def grads_kernel(parts, outs_col, outs_row, at_ref, *refs):
    factor_refs = refs[: 2 * parts]
    col_ref, row_ref, rows_ref = refs[2 * parts :]
    rank = factor_refs[0].shape[2]
    tokens = factor_refs[0].shape[1] // 2
    slots = tokens // SEQ
    halves = tokens // rank
    outs = outs_col + outs_row
    example = lax.broadcasted_iota(jnp.int32, (slots, rank), 0)
    token = lax.broadcasted_iota(jnp.int32, (slots, rank), 1)
    col_at = pl.multiple_of(at_ref[1] * outs_col, outs_col)
    row_at = pl.multiple_of(at_ref[0] * outs_row, outs_row)

    def build(factor_ref, k):
        left = []
        for h in range(halves):
            mask = ((token + h * rank) // SEQ == example).astype(F32)
            rows = jnp.concatenate(
                [
                    rows_ref[k, pl.ds(h * rank + col_at, outs_col), :],
                    rows_ref[k, pl.ds(h * rank + row_at, outs_row), :],
                ],
                axis=0,
            )
            spread = rows[:, None, :] * mask[None, :, :]
            left.append(spread.reshape(outs * slots, rank).astype(BF))
        left = jnp.concatenate(left, axis=1)
        return dot(left, factor_ref[0, :tokens, :]).reshape(outs, slots, rank)

    def pair(own_ref, mate_ref):
        rows_ref[0] = own_ref[0, tokens:, :].astype(F32)
        rows_ref[1] = mate_ref[0, tokens:, :].astype(F32)
        own, mate = build(own_ref, 0), build(mate_ref, 1)
        even = at_ref[1] % 2 == 0
        both = [jnp.where(even, own, mate), jnp.where(even, mate, own)]
        both = jnp.concatenate(both, axis=1).astype(BF)
        for o in range(outs_col):
            col_ref[:, o * rank : (o + 1) * rank] = both[o]
        for o in range(outs_row):
            row_ref[:, o * rank : (o + 1) * rank] = both[outs_col + o]

    for part in range(parts):
        pl.when(pl.program_id(0) == part)(
            functools.partial(pair, factor_refs[part], factor_refs[parts + part])
        )


def build_grads(place, own, mate, rows, cols):
    parts = len(own)
    tiers, depth, rank = own[0].shape
    tokens = depth // 2
    slots = tokens // SEQ
    files = parts // 2
    total = 2 * parts * tiers * slots

    def grads_at(p, i, at_ref):
        z, y, x = at_ref[0] // 2, at_ref[0] % 2, at_ref[1] // 2
        from_x = lax.rem(x - p // 2 + files, files)
        from_z = lax.rem(z - i + tiers, tiers)
        return ((from_x * tiers + from_z) * 2 + (y ^ (p % 2)), 0)

    def factor_at(part, p, i, at_ref):
        return (jnp.where(p == part, i, jnp.where(p < part, 0, tiers - 1)), 0, 0)

    return pl.pallas_call(
        functools.partial(grads_kernel, parts, cols // rank, rows // rank),
        grid_spec=pltpu.PrefetchScalarGridSpec(
            num_scalar_prefetch=1,
            grid=(parts, tiers),
            in_specs=[
                pl.BlockSpec((1, depth, rank), functools.partial(factor_at, part % parts))
                for part in range(2 * parts)
            ],
            out_specs=[
                pl.BlockSpec((2 * slots, cols), grads_at),
                pl.BlockSpec((2 * slots, rows), grads_at),
            ],
            scratch_shapes=[pltpu.VMEM((2, tokens, rank), F32)],
        ),
        out_shape=[
            jax.ShapeDtypeStruct((total, cols), BF),
            jax.ShapeDtypeStruct((total, rows), BF),
        ],
        compiler_params=params(),
        cost_estimate=cost(2 * total * (rows + cols) * tokens, 2 * total * (rows + cols)),
        name="build_grads",
    )(place, *own, *mate)


def back_kernel(streams, plan_ref, *refs):
    vec_ref, gram_refs, out_ref = refs[0], refs[1 : 1 + streams], refs[-1]
    depth = gram_refs[0].shape[0]
    total = None
    for s in range(streams):
        vec = vec_ref[:, s * depth : (s + 1) * depth]
        value = dot(vec, gram_refs[s][...].astype(BF))
        total = value if total is None else total + value
    total = decay_rate * total.T
    if len(refs) > streams + 2:
        own = jnp.where(plan_ref[1] == 1, damping, 0.0)
        total = total + own * refs[streams + 1][...]
    out_ref[...] = total.astype(out_ref.dtype)


def back_product(plan, vec, gram, queries=None):
    count, rows = vec.shape
    width = gram.shape[1] // 2
    block = min(512, width)
    steps = width // block
    streams = 2
    depth = rows // streams

    def gram_at(s, i, plan_ref):
        return (s, plan_ref[0] * steps + i)

    in_specs = [pl.BlockSpec((count, rows), lambda i, plan_ref: (0, 0))]
    for s in range(streams):
        in_specs.append(pl.BlockSpec((depth, block), functools.partial(gram_at, s)))
    args = [vec] + [gram] * streams
    kind = BF
    if queries is not None:
        in_specs.append(pl.BlockSpec((block, count), lambda i, plan_ref: (i, 0)))
        args.append(queries)
        kind = F32
    return pl.pallas_call(
        functools.partial(back_kernel, streams),
        grid_spec=pltpu.PrefetchScalarGridSpec(
            num_scalar_prefetch=1,
            grid=(steps,),
            in_specs=in_specs,
            out_specs=pl.BlockSpec((block, count), lambda i, plan_ref: (i, 0)),
        ),
        out_shape=jax.ShapeDtypeStruct((width, count), kind),
        compiler_params=params(),
        cost_estimate=cost(2 * rows * width * count, 4 * rows * width + 4 * width * count),
        name="back_product",
    )(plan, *args)


def gram_kernel(scale, block, first, at_ref, gram_ref, left_ref, right_ref, *rest):
    out_ref, copy_ref = rest[-2:]
    strip = copy_ref.shape[1] // 3
    lower = ((first + pl.program_id(0)) * block >= strip).astype(jnp.int32)
    left = left_ref[...]
    offset = at_ref[0] + (first + pl.program_id(0)) * block
    ahead = lax.broadcasted_iota(jnp.int32, (block, strip), 0)
    ahead = ahead - lax.broadcasted_iota(jnp.int32, (block, strip), 1)
    for s in range(gram_ref.shape[1] // strip):
        part = slice(s * strip, (s + 1) * strip)
        product = dot(left, right_ref[:, part], ((0,), (0,)))
        value = decay_rate * gram_ref[:, part] + scale * product
        value = value + jnp.where(ahead == s * strip - offset, damping, 0.0)
        out_ref[:, part] = value
        short = value.astype(BF)
        for k in range(3):

            @pl.when(at_ref[1 + 3 * lower + k] == s)
            def _(k=k, short=short):
                copy_ref[:, k * strip : (k + 1) * strip] = short


def update_gram(at, gram, left, right, scale, first, count, block, before):
    rows, cols = gram.shape
    examples = left.shape[0]
    width = 3 * (cols // 4)
    in_specs = [
        pl.BlockSpec((block, cols), lambda i, at_ref: (first + i, 0)),
        pl.BlockSpec((examples, block), lambda i, at_ref: (0, first + i)),
        pl.BlockSpec((examples, cols), lambda i, at_ref: (0, 0)),
    ]
    args = [gram, left, right]
    alias = {}
    if before is not None:
        in_specs.append(pl.BlockSpec(memory_space=pl.ANY))
        args.append(before)
        alias = {4: 0}
    return pl.pallas_call(
        functools.partial(gram_kernel, scale, block, first),
        grid_spec=pltpu.PrefetchScalarGridSpec(
            num_scalar_prefetch=1,
            grid=(count,),
            in_specs=in_specs,
            out_specs=[
                pl.BlockSpec((block, cols), lambda i, at_ref: (first + i, 0)),
                pl.BlockSpec((block, width), lambda i, at_ref: (i, 0)),
            ],
        ),
        out_shape=[
            jax.ShapeDtypeStruct((rows, cols), F32),
            jax.ShapeDtypeStruct((count * block, width), BF),
        ],
        input_output_aliases=alias,
        compiler_params=params(30),
        cost_estimate=cost(2 * count * block * cols * examples, 8 * count * block * cols),
        name="update_gram",
    )(at, *args)


def tail_kernel(even, pieces, plan_ref, *refs):
    same_ref, other_ref, mate_ref, came_ref, rest_ref = refs[:5]
    col_ref, row_ref, inner_ref, query_ref = refs[5:9]
    copy_refs = refs[9 : 9 + pieces]
    mapped_ref, sums_ref, vec_same_ref, vec_other_ref = refs[9 + pieces :]
    tiers, piece, count = same_ref.shape
    depth = tiers * piece
    width = depth // 2
    inner = inner_ref[...]
    tier, y = plan_ref[0], plan_ref[1]
    near, source = plan_ref[6] == 1, plan_ref[7] == 1
    along, square = jnp.zeros((8, count), F32), jnp.zeros((8, count), F32)
    norm = jnp.zeros((8, count), F32)

    def fold(value):
        return jnp.sum(value.reshape(value.shape[0] // 8, 8, count), axis=0)

    def low_rank(ref, start):
        part = ref[:, pl.ds(pl.multiple_of(start * piece, piece), piece)]
        return dot(part, inner, ((0,), (0,)))

    for s in range(tiers):
        quarter = lax.rem(tier - s + tiers, tiers)
        rows = pl.ds(pl.multiple_of(quarter * piece, piece), piece)
        own = same_ref[s].astype(F32)
        value = own + low_rank(col_ref, y * tiers + quarter)
        vec_same_ref[rows, :] = value.astype(BF)
        value = other_ref[s].astype(F32) + low_rank(col_ref, (1 - y) * tiers + quarter)
        vec_other_ref[rows, :] = value.astype(BF)
        here = plan_ref[8] == s // (tiers // 2)
        got = jnp.where(here, came_ref[s % (tiers // 2)], rest_ref[s % (tiers // 2)]).astype(F32)
        got = jnp.where(near, jnp.where(source, own, mate_ref[s].astype(F32)), got)
        value = got + low_rank(row_ref, quarter)
        mapped_ref[rows, :] = value
        query = query_ref[rows, :]
        norm += fold(query * query)
        along += fold(query * value)
        square += fold(value * value)

    def take(ref, quadrant):
        return ref[pl.ds(pl.multiple_of(quadrant * width, width), width), :]

    sums_ref[0] = even * norm
    sums_ref[1] = even * along
    sums_ref[2] = even * square
    sums_ref[3] = jnp.zeros_like(norm)
    weight = plan_ref[4].astype(F32)
    cuts = [(k, h) for k in range(pieces) for h in range(tiers // pieces)]

    def left(k, h):
        start = (k * (tiers // pieces) + h) * piece
        return mapped_ref[start : start + piece, :]

    for k, h in cuts:
        upper = (k * (tiers // pieces) + h) * 2 // tiers
        rows = slice(h * piece, (h + 1) * piece)
        total = weight * dot(copy_refs[k][rows, :width], take(vec_same_ref, upper ^ plan_ref[2]))
        total += 2.0 * dot(
            copy_refs[k][rows, width : 2 * width], take(vec_other_ref, upper ^ plan_ref[3])
        )
        sums_ref[3] += fold(total * left(k, h))

    @pl.when(plan_ref[5] == 1)
    def _():
        for k, h in cuts[: len(cuts) // 2]:
            rows = slice(h * piece, (h + 1) * piece)
            total = 2.0 * dot(copy_refs[k][rows, 2 * width :], vec_same_ref[width:, :])
            sums_ref[3] += fold(total * left(k, h))


def tail(plan, same, other, found, grads_col, grads_row, inner, queries, copies, even):
    rows, count = queries.shape
    args = [same, other, *found, grads_col, grads_row, inner, queries, *copies]
    return pl.pallas_call(
        functools.partial(tail_kernel, even, len(copies)),
        in_specs=[pl.BlockSpec(memory_space=pltpu.SMEM)]
        + [pl.BlockSpec(memory_space=pltpu.VMEM)] * len(args),
        out_specs=[pl.BlockSpec(memory_space=pltpu.VMEM)] * 2,
        out_shape=[
            jax.ShapeDtypeStruct((rows, count), F32),
            jax.ShapeDtypeStruct((4, 8, count), F32),
        ],
        scratch_shapes=[pltpu.VMEM((rows, count), BF), pltpu.VMEM((rows, count), BF)],
        compiler_params=params(16),
        cost_estimate=cost(4 * rows * rows * count, 4 * rows * rows),
        name="tail",
    )(plan, *args)


def after(value, *others):
    return lax.optimization_barrier((value,) + others)[0]


def integers(*values):
    return jnp.stack([jnp.asarray(v).astype(jnp.int32) for v in values])


def shards(activations, out_grads, proj_in, proj_out, lengths, gram_old, queries):
    local_count = lengths.shape[0]
    rank = proj_in.shape[1]
    row_count = lax.axis_size("row")
    col_count = lax.axis_size("col")
    rows, cols = gram_old.shape
    count = queries.shape[1]
    tokens = local_count * SEQ
    tiers = row_count // 2
    files = col_count // 2
    piece = rows // tiers
    row = lax.axis_index("row")
    col = lax.axis_index("col")
    z, y = row // 2, row % 2
    x, core = col // 2, col % 2
    total_examples = local_count * row_count * col_count
    scale = (1.0 - decay_rate) / total_examples

    def move(value, goes):
        pairs = []
        for r in range(row_count):
            for c in range(col_count):
                to = goes(r // 2, r % 2, c // 2, c % 2)
                if to is not None:
                    pairs.append((r * col_count + c, (to[0] * 2 + to[1]) * col_count + to[2] * 2 + to[3]))
        return lax.ppermute(value, ("row", "col"), pairs)

    def swap_y(value):
        return move(value, lambda z, y, x, k: (z, 1 - y, x, k))

    def swap_core(value):
        return move(value, lambda z, y, x, k: (z, y, x, 1 - k))

    def ring_z(value, by=1):
        return move(value, lambda z, y, x, k: ((z + by) % tiers, y, x, k))

    def ring_x(value):
        return move(value, lambda z, y, x, k: (z, y, (x + 1) % files, k))

    def flip_x(value, bit):
        return move(value, lambda z, y, x, k: (z, y, x ^ bit, k))

    def spread_z(value):
        return [value] + [ring_z(value, by) for by in range(1, tiers)]

    vec = queries.astype(BF).T
    away = back_product(integers(1 - y, 0), vec, gram_old)
    come = swap_y(away)

    low_in = dot(activations, proj_in).astype(BF)
    low_out = dot(proj_out, out_grads, ((0,), (1,))).astype(BF)
    slot = jnp.arange(tokens, dtype=jnp.int32)
    valid_mask = slot % SEQ < jnp.repeat(lengths, SEQ)
    low_out = jnp.where(valid_mask[None, :], low_out, jnp.zeros((), BF))
    low_out = low_out.reshape(rank, tokens // rank, rank).transpose(1, 0, 2).reshape(tokens, rank)
    local = after(jnp.concatenate([low_in, low_out], axis=0), away)
    factors = spread_z(local)

    here = back_product(after(integers(y, z == col), local), vec, gram_old, queries)
    here = here.reshape(tiers, piece, count)
    come = come.reshape(tiers, piece, count)

    def piece_for(by):
        at = (z + by) % tiers
        one = lax.dynamic_index_in_dim(here, at, 0, keepdims=False)
        two = lax.dynamic_index_in_dim(come, at, 0, keepdims=False)
        return one + two.astype(F32)

    sends = [piece_for(by).astype(BF) for by in range(1, tiers)]
    parts = [ring_z(sends[by - 1], by) for by in range(1, tiers)]

    factors = jnp.stack(lax.optimization_barrier((*factors, here))[:tiers])
    across = [factors]
    for dx in range(1, files):
        across.append(move(factors, lambda z, y, x, k: (z, y, (x + dx) % files, k)))
    own = []
    for one in across:
        own.append(one)
        own.append(swap_y(after(one, *sends)))

    total = piece_for(0)
    for part in parts:
        total = total + part.astype(F32)
    short = total.astype(BF)

    same = spread_z(short)
    held = lax.optimization_barrier((*own, short))[:-1]
    mate = [swap_core(f) for f in held]
    grads_col, grads_row = build_grads(integers(row, col), held, mate, rows, cols)
    partial = dot(grads_row, queries.astype(BF))
    inner = (partial + swap_y(partial.astype(BF)).astype(F32)).astype(BF)
    sums = spread_z(inner)
    same = lax.optimization_barrier((*same, partial))[:-1]
    stacked = jnp.stack(same)
    other = swap_y(stacked)

    fellow = swap_core(stacked)
    cut = tiers // 2
    half = lax.dynamic_slice_in_dim(
        jnp.where(core == z % 2, stacked, fellow), core * cut, cut, 0
    )
    came = half
    for dx in range(1, files):
        got = move(half, lambda z, y, x, k: (z, y, (x + dx) % files, k))
        came = got if files == 2 else jnp.where((x - dx) % files == z // 2, got, came)
    found = [fellow, came, swap_core(came)]

    inner = sum(v.astype(F32) for v in reversed(sums))
    inner = (scale * inner).astype(BF)

    flags = integers(row > 2 * col + y, row > 2 * col + 1 - y)
    block = min(256, rows // 4)
    at = integers(
        row * rows - col * cols,
        2 * y + flags[0],
        2 * (1 - y) + flags[1],
        jnp.where(z == col, 2 * y + 1, -1),
        2 * y + 1 - flags[0],
        2 * (1 - y) + 1 - flags[1],
        -1,
    )
    gram_new, copy = update_gram(
        after(at, half, inner), gram_old, grads_row, grads_col, scale, 0, rows // block, block, None
    )
    plan = jnp.concatenate(
        [
            integers(z, y),
            flags,
            integers(jnp.where(z == col, 1, 2), z == col, x == z // 2, core == z % 2, core),
        ]
    )
    mapped, sums = tail(
        after(plan, gram_new), stacked, other, found, grads_col, grads_row, inner, queries,
        [copy], 1.0 / col_count,
    )
    sums = jnp.sum(sums, axis=1)
    sums = sums + swap_core(sums)
    bit = 1
    while bit < files:
        sums = sums + flip_x(sums, bit)
        bit *= 2
    sums = sums + swap_y(sums)
    around = jnp.stack(spread_z(sums))
    sums = sum(
        lax.dynamic_index_in_dim(around, (z - k) % tiers, 0, keepdims=False) for k in range(tiers)
    )
    norm_now, along, square, curve = sums[0], sums[1], sums[2], sums[3]
    step = norm_now / along
    norm_next = step * step * square - norm_now
    momentum = norm_next / norm_now
    curvature = along - 2.0 * step * square + step * step * curve
    step_next = norm_next / (curvature - momentum * norm_next / step)
    solution = (step + step_next * (1.0 + momentum)) * queries - (step_next * step) * mapped
    return (gram_new, solution)


def solution(mesh):
    in_specs = (
        P(("row", "col"), None),
        P(("row", "col"), None),
        P(),
        P(),
        P(("row", "col")),
        P("row", "col"),
        P("row", None),
    )
    out_specs = (P("row", "col"), P("row", None))
    return jax.shard_map(shards, mesh=mesh, in_specs=in_specs, out_specs=out_specs, check_vma=False)
```

```python
import functools

import jax
import jax.numpy as jnp
from jax import lax
from jax.experimental import pallas as pl
from jax.experimental.pallas import tpu as pltpu
from jax.sharding import PartitionSpec as P

SEQ = 32

decay_rate = 0.5
damping = 1.0

BF = jnp.bfloat16
F32 = jnp.float32
VMEM_BYTES = 40 * 1024 * 1024


def dot(a, b, dims=((1,), (0,))):
    return lax.dot_general(a, b, (dims, ((), ())), preferred_element_type=F32)


def params(mebibytes=24):
    return pltpu.CompilerParams(vmem_limit_bytes=mebibytes * 1024 * 1024)


def cost(flops, moved):
    return pl.CostEstimate(flops=flops, bytes_accessed=moved, transcendentals=0)


def grads_kernel(parts, outs_col, outs_row, at_ref, *refs):
    factor_refs = refs[: 2 * parts]
    col_ref, row_ref, rows_ref = refs[2 * parts :]
    rank = factor_refs[0].shape[2]
    tokens = factor_refs[0].shape[1] // 2
    slots = tokens // SEQ
    halves = tokens // rank
    outs = outs_col + outs_row
    example = lax.broadcasted_iota(jnp.int32, (slots, rank), 0)
    token = lax.broadcasted_iota(jnp.int32, (slots, rank), 1)
    col_at = pl.multiple_of(at_ref[1] * outs_col, outs_col)
    row_at = pl.multiple_of(at_ref[0] * outs_row, outs_row)

    def build(factor_ref, k):
        left = []
        for h in range(halves):
            mask = ((token + h * rank) // SEQ == example).astype(F32)
            rows = jnp.concatenate(
                [
                    rows_ref[k, pl.ds(h * rank + col_at, outs_col), :],
                    rows_ref[k, pl.ds(h * rank + row_at, outs_row), :],
                ],
                axis=0,
            )
            spread = rows[:, None, :] * mask[None, :, :]
            left.append(spread.reshape(outs * slots, rank).astype(BF))
        left = jnp.concatenate(left, axis=1)
        return dot(left, factor_ref[0, :tokens, :]).reshape(outs, slots, rank)

    def pair(own_ref, mate_ref):
        rows_ref[0] = own_ref[0, tokens:, :].astype(F32)
        rows_ref[1] = mate_ref[0, tokens:, :].astype(F32)
        own, mate = build(own_ref, 0), build(mate_ref, 1)
        even = at_ref[1] % 2 == 0
        both = [jnp.where(even, own, mate), jnp.where(even, mate, own)]
        both = jnp.concatenate(both, axis=1).astype(BF)
        for o in range(outs_col):
            col_ref[:, o * rank : (o + 1) * rank] = both[o]
        for o in range(outs_row):
            row_ref[:, o * rank : (o + 1) * rank] = both[outs_col + o]

    for part in range(parts):
        pl.when(pl.program_id(0) == part)(
            functools.partial(pair, factor_refs[part], factor_refs[parts + part])
        )


def build_grads(place, own, mate, rows, cols):
    parts = len(own)
    tiers, depth, rank = own[0].shape
    tokens = depth // 2
    slots = tokens // SEQ
    files = parts // 2
    total = 2 * parts * tiers * slots

    def grads_at(p, i, at_ref):
        z, y, x = at_ref[0] // 2, at_ref[0] % 2, at_ref[1] // 2
        from_x = lax.rem(x - p // 2 + files, files)
        from_z = lax.rem(z - i + tiers, tiers)
        return ((from_x * tiers + from_z) * 2 + (y ^ (p % 2)), 0)

    def factor_at(part, p, i, at_ref):
        return (jnp.where(p == part, i, jnp.where(p < part, 0, tiers - 1)), 0, 0)

    return pl.pallas_call(
        functools.partial(grads_kernel, parts, cols // rank, rows // rank),
        grid_spec=pltpu.PrefetchScalarGridSpec(
            num_scalar_prefetch=1,
            grid=(parts, tiers),
            in_specs=[
                pl.BlockSpec((1, depth, rank), functools.partial(factor_at, part % parts))
                for part in range(2 * parts)
            ],
            out_specs=[
                pl.BlockSpec((2 * slots, cols), grads_at),
                pl.BlockSpec((2 * slots, rows), grads_at),
            ],
            scratch_shapes=[pltpu.VMEM((2, tokens, rank), F32)],
        ),
        out_shape=[
            jax.ShapeDtypeStruct((total, cols), BF),
            jax.ShapeDtypeStruct((total, rows), BF),
        ],
        compiler_params=params(),
        cost_estimate=cost(2 * total * (rows + cols) * tokens, 2 * total * (rows + cols)),
        name="build_grads",
    )(place, *own, *mate)


def back_kernel(streams, plan_ref, *refs):
    vec_ref, gram_refs, out_ref = refs[0], refs[1 : 1 + streams], refs[-1]
    depth = gram_refs[0].shape[0]
    total = None
    for s in range(streams):
        vec = vec_ref[:, s * depth : (s + 1) * depth]
        value = dot(vec, gram_refs[s][...].astype(BF))
        total = value if total is None else total + value
    total = decay_rate * total.T
    if len(refs) > streams + 2:
        own = jnp.where(plan_ref[1] == 1, damping, 0.0)
        total = total + own * refs[streams + 1][...]
    out_ref[...] = total.astype(out_ref.dtype)


def back_product(plan, vec, gram, queries=None):
    count, rows = vec.shape
    width = gram.shape[1] // 2
    block = min(512, width)
    steps = width // block
    streams = 4
    depth = rows // streams

    def gram_at(s, i, plan_ref):
        return (s, plan_ref[0] * steps + i)

    in_specs = [pl.BlockSpec((count, rows), lambda i, plan_ref: (0, 0))]
    for s in range(streams):
        in_specs.append(pl.BlockSpec((depth, block), functools.partial(gram_at, s)))
    args = [vec] + [gram] * streams
    kind = BF
    if queries is not None:
        in_specs.append(pl.BlockSpec((block, count), lambda i, plan_ref: (i, 0)))
        args.append(queries)
        kind = F32
    return pl.pallas_call(
        functools.partial(back_kernel, streams),
        grid_spec=pltpu.PrefetchScalarGridSpec(
            num_scalar_prefetch=1,
            grid=(steps,),
            in_specs=in_specs,
            out_specs=pl.BlockSpec((block, count), lambda i, plan_ref: (i, 0)),
        ),
        out_shape=jax.ShapeDtypeStruct((width, count), kind),
        compiler_params=params(),
        cost_estimate=cost(2 * rows * width * count, 4 * rows * width + 4 * width * count),
        name="back_product",
    )(plan, *args)


def gram_kernel(scale, block, first, at_ref, gram_ref, left_ref, right_ref, *rest):
    out_ref, copy_ref = rest[-2:]
    strip = copy_ref.shape[1] // 3
    left = left_ref[...]
    offset = at_ref[0] + (first + pl.program_id(0)) * block
    ahead = lax.broadcasted_iota(jnp.int32, (block, strip), 0)
    ahead = ahead - lax.broadcasted_iota(jnp.int32, (block, strip), 1)
    for s in range(gram_ref.shape[1] // strip):
        part = slice(s * strip, (s + 1) * strip)
        product = dot(left, right_ref[:, part], ((0,), (0,)))
        value = decay_rate * gram_ref[:, part] + scale * product
        value = value + jnp.where(ahead == s * strip - offset, damping, 0.0)
        out_ref[:, part] = value
        short = value.astype(BF)
        for k in range(3):

            @pl.when(at_ref[1 + k] == s)
            def _(k=k, short=short):
                copy_ref[:, k * strip : (k + 1) * strip] = short


def update_gram(at, gram, left, right, scale, first, count, block, before):
    rows, cols = gram.shape
    examples = left.shape[0]
    width = 3 * (cols // 4)
    in_specs = [
        pl.BlockSpec((block, cols), lambda i, at_ref: (first + i, 0)),
        pl.BlockSpec((examples, block), lambda i, at_ref: (0, first + i)),
        pl.BlockSpec((examples, cols), lambda i, at_ref: (0, 0)),
    ]
    args = [gram, left, right]
    alias = {}
    if before is not None:
        in_specs.append(pl.BlockSpec(memory_space=pl.ANY))
        args.append(before)
        alias = {4: 0}
    return pl.pallas_call(
        functools.partial(gram_kernel, scale, block, first),
        grid_spec=pltpu.PrefetchScalarGridSpec(
            num_scalar_prefetch=1,
            grid=(count,),
            in_specs=in_specs,
            out_specs=[
                pl.BlockSpec((block, cols), lambda i, at_ref: (first + i, 0)),
                pl.BlockSpec((block, width), lambda i, at_ref: (i, 0)),
            ],
        ),
        out_shape=[
            jax.ShapeDtypeStruct((rows, cols), F32),
            jax.ShapeDtypeStruct((count * block, width), BF),
        ],
        input_output_aliases=alias,
        compiler_params=params(30),
        cost_estimate=cost(2 * count * block * cols * examples, 8 * count * block * cols),
        name="update_gram",
    )(at, *args)


def tail_kernel(even, pieces, plan_ref, *refs):
    same_ref, other_ref, mate_ref, came_ref, rest_ref = refs[:5]
    col_ref, row_ref, inner_ref, query_ref = refs[5:9]
    copy_refs = refs[9 : 9 + pieces]
    mapped_ref, sums_ref, vec_same_ref, vec_other_ref = refs[9 + pieces :]
    tiers, piece, count = same_ref.shape
    depth = tiers * piece
    width = depth // 2
    inner = inner_ref[...]
    tier, y = plan_ref[0], plan_ref[1]
    near, source = plan_ref[6] == 1, plan_ref[7] == 1
    along, square = jnp.zeros((8, count), F32), jnp.zeros((8, count), F32)
    norm = jnp.zeros((8, count), F32)

    def fold(value):
        return jnp.sum(value.reshape(value.shape[0] // 8, 8, count), axis=0)

    def low_rank(ref, start):
        part = ref[:, pl.ds(pl.multiple_of(start * piece, piece), piece)]
        return dot(part, inner, ((0,), (0,)))

    for s in range(tiers):
        quarter = lax.rem(tier - s + tiers, tiers)
        rows = pl.ds(pl.multiple_of(quarter * piece, piece), piece)
        own = same_ref[s].astype(F32)
        value = own + low_rank(col_ref, y * tiers + quarter)
        vec_same_ref[rows, :] = value.astype(BF)
        value = other_ref[s].astype(F32) + low_rank(col_ref, (1 - y) * tiers + quarter)
        vec_other_ref[rows, :] = value.astype(BF)
        here = plan_ref[8] == s // (tiers // 2)
        got = jnp.where(here, came_ref[s % (tiers // 2)], rest_ref[s % (tiers // 2)]).astype(F32)
        got = jnp.where(near, jnp.where(source, own, mate_ref[s].astype(F32)), got)
        value = got + low_rank(row_ref, quarter)
        mapped_ref[rows, :] = value
        query = query_ref[rows, :]
        norm += fold(query * query)
        along += fold(query * value)
        square += fold(value * value)

    def take(ref, quadrant):
        return ref[pl.ds(pl.multiple_of(quadrant * width, width), width), :]

    sums_ref[0] = even * norm
    sums_ref[1] = even * along
    sums_ref[2] = even * square
    sums_ref[3] = jnp.zeros_like(norm)
    weight = plan_ref[4].astype(F32)
    cuts = [(k, h) for k in range(pieces) for h in range(tiers // pieces)]

    def left(k, h):
        start = (k * (tiers // pieces) + h) * piece
        return mapped_ref[start : start + piece, :]

    for k, h in cuts:
        upper = (k * (tiers // pieces) + h) * 2 // tiers
        rows = slice(h * piece, (h + 1) * piece)
        total = weight * dot(copy_refs[k][rows, :width], take(vec_same_ref, upper ^ plan_ref[2]))
        total += 2.0 * dot(
            copy_refs[k][rows, width : 2 * width], take(vec_other_ref, upper ^ plan_ref[3])
        )
        sums_ref[3] += fold(total * left(k, h))

    @pl.when(plan_ref[5] == 1)
    def _():
        for k, h in cuts[: len(cuts) // 2]:
            rows = slice(h * piece, (h + 1) * piece)
            total = 2.0 * dot(copy_refs[k][rows, 2 * width :], vec_same_ref[width:, :])
            sums_ref[3] += fold(total * left(k, h))


def tail(plan, same, other, found, grads_col, grads_row, inner, queries, copies, even):
    rows, count = queries.shape
    args = [same, other, *found, grads_col, grads_row, inner, queries, *copies]
    return pl.pallas_call(
        functools.partial(tail_kernel, even, len(copies)),
        in_specs=[pl.BlockSpec(memory_space=pltpu.SMEM)]
        + [pl.BlockSpec(memory_space=pltpu.VMEM)] * len(args),
        out_specs=[pl.BlockSpec(memory_space=pltpu.VMEM)] * 2,
        out_shape=[
            jax.ShapeDtypeStruct((rows, count), F32),
            jax.ShapeDtypeStruct((4, 8, count), F32),
        ],
        scratch_shapes=[pltpu.VMEM((rows, count), BF), pltpu.VMEM((rows, count), BF)],
        compiler_params=params(16),
        cost_estimate=cost(4 * rows * rows * count, 4 * rows * rows),
        name="tail",
    )(plan, *args)


def after(value, *others):
    return lax.optimization_barrier((value,) + others)[0]


def integers(*values):
    return jnp.stack([jnp.asarray(v).astype(jnp.int32) for v in values])


def shards(activations, out_grads, proj_in, proj_out, lengths, gram_old, queries):
    local_count = lengths.shape[0]
    rank = proj_in.shape[1]
    row_count = lax.axis_size("row")
    col_count = lax.axis_size("col")
    rows, cols = gram_old.shape
    count = queries.shape[1]
    tokens = local_count * SEQ
    tiers = row_count // 2
    files = col_count // 2
    piece = rows // tiers
    row = lax.axis_index("row")
    col = lax.axis_index("col")
    z, y = row // 2, row % 2
    x, core = col // 2, col % 2
    total_examples = local_count * row_count * col_count
    scale = (1.0 - decay_rate) / total_examples

    def move(value, goes):
        pairs = []
        for r in range(row_count):
            for c in range(col_count):
                to = goes(r // 2, r % 2, c // 2, c % 2)
                if to is not None:
                    pairs.append((r * col_count + c, (to[0] * 2 + to[1]) * col_count + to[2] * 2 + to[3]))
        return lax.ppermute(value, ("row", "col"), pairs)

    def swap_y(value):
        return move(value, lambda z, y, x, k: (z, 1 - y, x, k))

    def swap_core(value):
        return move(value, lambda z, y, x, k: (z, y, x, 1 - k))

    def ring_z(value, by=1):
        return move(value, lambda z, y, x, k: ((z + by) % tiers, y, x, k))

    def ring_x(value):
        return move(value, lambda z, y, x, k: (z, y, (x + 1) % files, k))

    def flip_x(value, bit):
        return move(value, lambda z, y, x, k: (z, y, x ^ bit, k))

    def spread_z(value):
        return [value] + [ring_z(value, by) for by in range(1, tiers)]

    vec = queries.astype(BF).T
    away = back_product(integers(1 - y, 0), vec, gram_old)
    come = swap_y(away)

    low_in = dot(activations, proj_in).astype(BF)
    low_out = dot(proj_out, out_grads, ((0,), (1,))).astype(BF)
    slot = jnp.arange(tokens, dtype=jnp.int32)
    valid_mask = slot % SEQ < jnp.repeat(lengths, SEQ)
    low_out = jnp.where(valid_mask[None, :], low_out, jnp.zeros((), BF))
    low_out = low_out.reshape(rank, tokens // rank, rank).transpose(1, 0, 2).reshape(tokens, rank)
    local = after(jnp.concatenate([low_in, low_out], axis=0), away)
    factors = spread_z(local)

    here = back_product(after(integers(y, z == col), local), vec, gram_old, queries)
    here = here.reshape(tiers, piece, count)
    come = come.reshape(tiers, piece, count)

    def piece_for(by):
        at = (z + by) % tiers
        one = lax.dynamic_index_in_dim(here, at, 0, keepdims=False)
        two = lax.dynamic_index_in_dim(come, at, 0, keepdims=False)
        return one + two.astype(F32)

    sends = [piece_for(by).astype(BF) for by in range(1, tiers)]
    parts = [ring_z(sends[by - 1], by) for by in range(1, tiers)]

    factors = jnp.stack(lax.optimization_barrier((*factors, here))[:tiers])
    across = [factors]
    for dx in range(1, files):
        across.append(move(factors, lambda z, y, x, k: (z, y, (x + dx) % files, k)))
    own = []
    for one in across:
        own.append(one)
        own.append(swap_y(after(one, *sends)))

    total = piece_for(0)
    for part in parts:
        total = total + part.astype(F32)
    short = total.astype(BF)

    same = spread_z(short)
    held = lax.optimization_barrier((*own, short))[:-1]
    mate = [swap_core(f) for f in held]
    grads_col, grads_row = build_grads(integers(row, col), held, mate, rows, cols)
    partial = dot(grads_row, queries.astype(BF))
    fetched = swap_y(partial.astype(BF))
    flags = integers(row > 2 * col + y, row > 2 * col + 1 - y)
    block = min(256, rows // 4)
    blocks = rows // block // 2
    copies = []

    def update(k, before, *wait):
        at = integers(
            row * rows - col * cols,
            2 * y + (k ^ flags[0]),
            2 * (1 - y) + (k ^ flags[1]),
            jnp.where(z == col, 2 * y + 1, -1) if k == 0 else -1,
        )
        gram, copy = update_gram(
            after(at, *wait), gram_old, grads_row, grads_col, scale, k * blocks, blocks, block, before
        )
        copies.append(copy)
        return gram

    gram_new = update(0, None, partial)
    same = lax.optimization_barrier((*same, fetched, gram_new))[:-1]
    fetched = same[-1]
    stacked = jnp.stack(same[:-1])
    inner = (partial + fetched.astype(F32)).astype(BF)
    sums = spread_z(inner)
    other = swap_y(stacked)

    fellow = swap_core(stacked)
    cut = tiers // 2
    half = lax.dynamic_slice_in_dim(
        jnp.where(core == z % 2, stacked, fellow), core * cut, cut, 0
    )
    came = half
    for dx in range(1, files):
        got = move(half, lambda z, y, x, k: (z, y, (x + dx) % files, k))
        came = got if files == 2 else jnp.where((x - dx) % files == z // 2, got, came)
    gram_new = update(1, gram_new, half)
    came, *sums = lax.optimization_barrier((came, *sums, gram_new))[:-1]
    found = [fellow, came, swap_core(came)]
    inner = sum(v.astype(F32) for v in reversed(sums))
    inner = (scale * inner).astype(BF)
    plan = jnp.concatenate(
        [
            integers(z, y),
            flags,
            integers(jnp.where(z == col, 1, 2), z == col, x == z // 2, core == z % 2, core),
        ]
    )
    mapped, sums = tail(
        after(plan, gram_new), stacked, other, found, grads_col, grads_row, inner, queries,
        copies, 1.0 / col_count,
    )
    sums = jnp.sum(sums, axis=1)
    sums = sums + swap_core(sums)
    bit = 1
    while bit < files:
        sums = sums + flip_x(sums, bit)
        bit *= 2
    sums = sums + swap_y(sums)
    around = jnp.stack(spread_z(sums))
    sums = sum(
        lax.dynamic_index_in_dim(around, (z - k) % tiers, 0, keepdims=False) for k in range(tiers)
    )
    norm_now, along, square, curve = sums[0], sums[1], sums[2], sums[3]
    step = norm_now / along
    norm_next = step * step * square - norm_now
    momentum = norm_next / norm_now
    curvature = along - 2.0 * step * square + step * step * curve
    step_next = norm_next / (curvature - momentum * norm_next / step)
    solution = (step + step_next * (1.0 + momentum)) * queries - (step_next * step) * mapped
    return (gram_new, solution)


def solution(mesh):
    in_specs = (
        P(("row", "col"), None),
        P(("row", "col"), None),
        P(),
        P(),
        P(("row", "col")),
        P("row", "col"),
        P("row", None),
    )
    out_specs = (P("row", "col"), P("row", None))
    return jax.shard_map(shards, mesh=mesh, in_specs=in_specs, out_specs=out_specs, check_vma=False)
```

```python
import functools

import jax
import jax.numpy as jnp
from jax import lax
from jax.experimental import pallas as pl
from jax.experimental.pallas import tpu as pltpu
from jax.sharding import PartitionSpec as P

SEQ = 32

decay_rate = 0.5
damping = 1.0

BF = jnp.bfloat16
F32 = jnp.float32
VMEM_BYTES = 40 * 1024 * 1024


def dot(a, b, dims=((1,), (0,))):
    return lax.dot_general(a, b, (dims, ((), ())), preferred_element_type=F32)


def params(mebibytes=24):
    return pltpu.CompilerParams(vmem_limit_bytes=mebibytes * 1024 * 1024)


def cost(flops, moved):
    return pl.CostEstimate(flops=flops, bytes_accessed=moved, transcendentals=0)


def grads_kernel(parts, outs_col, outs_row, at_ref, *refs):
    factor_refs = refs[: 2 * parts]
    col_ref, row_ref, rows_ref, picked_ref = refs[2 * parts :]
    rank = factor_refs[0].shape[2]
    tokens = factor_refs[0].shape[1] // 2
    slots = tokens // SEQ
    halves = tokens // rank
    outs = outs_col + outs_row
    example = lax.broadcasted_iota(jnp.int32, (slots, rank), 0)
    token = lax.broadcasted_iota(jnp.int32, (slots, rank), 1)
    col_at = pl.multiple_of(at_ref[1] * outs_col, outs_col)
    row_at = pl.multiple_of(at_ref[0] * outs_row, outs_row)

    masks = [((token + h * rank) // SEQ == example).astype(F32) for h in range(halves)]

    def build(k, low_in):
        left = []
        for h in range(halves):
            picked_ref[k, h, :outs_col, :] = rows_ref[k, pl.ds(h * rank + col_at, outs_col), :]
            picked_ref[k, h, outs_col:, :] = rows_ref[k, pl.ds(h * rank + row_at, outs_row), :]
        for h in range(halves):
            rows = picked_ref[k, h]
            spread = rows[:, None, :] * masks[h][None, :, :]
            left.append(spread.reshape(outs * slots, rank).astype(BF))
        left = jnp.concatenate(left, axis=1)
        return dot(left, low_in).reshape(outs, slots, rank)

    def pair(own_ref, mate_ref):
        even = at_ref[1] % 2 == 0
        rows_ref[0] = jnp.where(even, own_ref[0, tokens:, :], mate_ref[0, tokens:, :]).astype(F32)
        rows_ref[1] = jnp.where(even, mate_ref[0, tokens:, :], own_ref[0, tokens:, :]).astype(F32)
        first = jnp.where(even, own_ref[0, :tokens, :], mate_ref[0, :tokens, :])
        second = jnp.where(even, mate_ref[0, :tokens, :], own_ref[0, :tokens, :])
        both = jnp.concatenate([build(0, first), build(1, second)], axis=1).astype(BF)
        for o in range(outs_col):
            col_ref[:, o * rank : (o + 1) * rank] = both[o]
        for o in range(outs_row):
            row_ref[:, o * rank : (o + 1) * rank] = both[outs_col + o]

    for part in range(parts):
        pl.when(pl.program_id(0) == part)(
            functools.partial(pair, factor_refs[part], factor_refs[parts + part])
        )


def build_grads(place, own, mate, rows, cols):
    parts = len(own)
    tiers, depth, rank = own[0].shape
    tokens = depth // 2
    slots = tokens // SEQ
    files = parts // 2
    total = 2 * parts * tiers * slots

    def grads_at(p, i, at_ref):
        z, y, x = at_ref[0] // 2, at_ref[0] % 2, at_ref[1] // 2
        from_x = lax.rem(x - p // 2 + files, files)
        from_z = lax.rem(z - i + tiers, tiers)
        return ((from_x * tiers + from_z) * 2 + (y ^ (p % 2)), 0)

    def factor_at(part, p, i, at_ref):
        return (jnp.where(p == part, i, jnp.where(p < part, 0, tiers - 1)), 0, 0)

    return pl.pallas_call(
        functools.partial(grads_kernel, parts, cols // rank, rows // rank),
        grid_spec=pltpu.PrefetchScalarGridSpec(
            num_scalar_prefetch=1,
            grid=(parts, tiers),
            in_specs=[
                pl.BlockSpec((1, depth, rank), functools.partial(factor_at, part % parts))
                for part in range(2 * parts)
            ],
            out_specs=[
                pl.BlockSpec((2 * slots, cols), grads_at),
                pl.BlockSpec((2 * slots, rows), grads_at),
            ],
            scratch_shapes=[
                pltpu.VMEM((2, tokens, rank), F32),
                pltpu.VMEM((2, tokens // rank, (cols + rows) // rank, rank), F32),
            ],
        ),
        out_shape=[
            jax.ShapeDtypeStruct((total, cols), BF),
            jax.ShapeDtypeStruct((total, rows), BF),
        ],
        compiler_params=params(12),
        cost_estimate=cost(2 * total * (rows + cols) * tokens, 2 * total * (rows + cols)),
        name="build_grads",
    )(place, *own, *mate)


def back_kernel(streams, plan_ref, *refs):
    vec_ref, gram_refs, out_ref = refs[0], refs[1 : 1 + streams], refs[-1]
    depth = gram_refs[0].shape[0]
    total = None
    for s in range(streams):
        vec = vec_ref[:, s * depth : (s + 1) * depth]
        value = dot(vec, gram_refs[s][...].astype(BF))
        total = value if total is None else total + value
    total = decay_rate * total.T
    if len(refs) > streams + 2:
        own = jnp.where(plan_ref[1] == 1, damping, 0.0)
        total = total + own * refs[streams + 1][...]
    out_ref[...] = total.astype(out_ref.dtype)


def back_product(plan, vec, gram, queries=None):
    count, rows = vec.shape
    width = gram.shape[1] // 2
    block = min(512, width)
    steps = width // block
    streams = 2
    depth = rows // streams

    def gram_at(s, i, plan_ref):
        return (s, plan_ref[0] * steps + i)

    in_specs = [pl.BlockSpec((count, rows), lambda i, plan_ref: (0, 0))]
    for s in range(streams):
        in_specs.append(pl.BlockSpec((depth, block), functools.partial(gram_at, s)))
    args = [vec] + [gram] * streams
    kind = BF
    if queries is not None:
        in_specs.append(pl.BlockSpec((block, count), lambda i, plan_ref: (i, 0)))
        args.append(queries)
        kind = F32
    return pl.pallas_call(
        functools.partial(back_kernel, streams),
        grid_spec=pltpu.PrefetchScalarGridSpec(
            num_scalar_prefetch=1,
            grid=(steps,),
            in_specs=in_specs,
            out_specs=pl.BlockSpec((block, count), lambda i, plan_ref: (i, 0)),
        ),
        out_shape=jax.ShapeDtypeStruct((width, count), kind),
        compiler_params=params(16),
        cost_estimate=cost(2 * rows * width * count, 4 * rows * width + 4 * width * count),
        name="back_product",
    )(plan, *args)


def gram_kernel(scale, block, first, at_ref, gram_ref, left_ref, right_ref, *rest):
    out_ref, copy_ref = rest[-2:]
    strip = copy_ref.shape[1] // 3
    lower = ((first + pl.program_id(0)) * block >= strip).astype(jnp.int32)
    left = left_ref[...]
    offset = at_ref[0] + (first + pl.program_id(0)) * block
    ahead = lax.broadcasted_iota(jnp.int32, (block, strip), 0)
    ahead = ahead - lax.broadcasted_iota(jnp.int32, (block, strip), 1)
    for s in range(gram_ref.shape[1] // strip):
        part = slice(s * strip, (s + 1) * strip)
        product = dot(left, right_ref[:, part], ((0,), (0,)))
        value = decay_rate * gram_ref[:, part] + scale * product
        value = value + jnp.where(ahead == s * strip - offset, damping, 0.0)
        out_ref[:, part] = value
        short = value.astype(BF)
        for k in range(3):

            @pl.when(at_ref[1 + 3 * lower + k] == s)
            def _(k=k, short=short):
                copy_ref[:, k * strip : (k + 1) * strip] = short


def update_gram(at, gram, left, right, scale, first, count, block, before):
    rows, cols = gram.shape
    examples = left.shape[0]
    width = 3 * (cols // 4)
    in_specs = [
        pl.BlockSpec((block, cols), lambda i, at_ref: (first + i, 0)),
        pl.BlockSpec((examples, block), lambda i, at_ref: (0, first + i)),
        pl.BlockSpec((examples, cols), lambda i, at_ref: (0, 0)),
    ]
    args = [gram, left, right]
    alias = {}
    if before is not None:
        in_specs.append(pl.BlockSpec(memory_space=pl.ANY))
        args.append(before)
        alias = {4: 0}
    return pl.pallas_call(
        functools.partial(gram_kernel, scale, block, first),
        grid_spec=pltpu.PrefetchScalarGridSpec(
            num_scalar_prefetch=1,
            grid=(count,),
            in_specs=in_specs,
            out_specs=[
                pl.BlockSpec((block, cols), lambda i, at_ref: (first + i, 0)),
                pl.BlockSpec((block, width), lambda i, at_ref: (i, 0)),
            ],
        ),
        out_shape=[
            jax.ShapeDtypeStruct((rows, cols), F32),
            jax.ShapeDtypeStruct((count * block, width), BF),
        ],
        input_output_aliases=alias,
        compiler_params=params(30),
        cost_estimate=cost(2 * count * block * cols * examples, 8 * count * block * cols),
        name="update_gram",
    )(at, *args)


def tail_kernel(even, pieces, plan_ref, *refs):
    same_ref, other_ref, mate_ref, came_ref, rest_ref = refs[:5]
    col_ref, row_ref, inner_ref, query_ref = refs[5:9]
    copy_refs = refs[9 : 9 + pieces]
    mapped_ref, sums_ref, vec_same_ref, vec_other_ref = refs[9 + pieces :]
    tiers, piece, count = same_ref.shape
    depth = tiers * piece
    width = depth // 2
    inner = inner_ref[...]
    tier, y = plan_ref[0], plan_ref[1]
    near, source = plan_ref[6] == 1, plan_ref[7] == 1
    along, square = jnp.zeros((8, count), F32), jnp.zeros((8, count), F32)
    norm = jnp.zeros((8, count), F32)

    def fold(value):
        return jnp.sum(value.reshape(value.shape[0] // 8, 8, count), axis=0)

    def low_rank(ref, start):
        part = ref[:, pl.ds(pl.multiple_of(start * piece, piece), piece)]
        return dot(part, inner, ((0,), (0,)))

    for s in range(tiers):
        quarter = lax.rem(tier - s + tiers, tiers)
        rows = pl.ds(pl.multiple_of(quarter * piece, piece), piece)
        own = same_ref[s].astype(F32)
        value = own + low_rank(col_ref, y * tiers + quarter)
        vec_same_ref[rows, :] = value.astype(BF)
        value = other_ref[s].astype(F32) + low_rank(col_ref, (1 - y) * tiers + quarter)
        vec_other_ref[rows, :] = value.astype(BF)
        here = plan_ref[8] == s // (tiers // 2)
        got = jnp.where(here, came_ref[s % (tiers // 2)], rest_ref[s % (tiers // 2)]).astype(F32)
        got = jnp.where(near, jnp.where(source, own, mate_ref[s].astype(F32)), got)
        value = got + low_rank(row_ref, quarter)
        mapped_ref[rows, :] = value
        query = query_ref[rows, :]
        norm += fold(query * query)
        along += fold(query * value)
        square += fold(value * value)

    def take(ref, quadrant):
        return ref[pl.ds(pl.multiple_of(quadrant * width, width), width), :]

    sums_ref[0] = even * norm
    sums_ref[1] = even * along
    sums_ref[2] = even * square
    sums_ref[3] = jnp.zeros_like(norm)
    weight = plan_ref[4].astype(F32)
    cuts = [(k, h) for k in range(pieces) for h in range(tiers // pieces)]

    def left(k, h):
        start = (k * (tiers // pieces) + h) * piece
        return mapped_ref[start : start + piece, :]

    for k, h in cuts:
        upper = (k * (tiers // pieces) + h) * 2 // tiers
        rows = slice(h * piece, (h + 1) * piece)
        total = weight * dot(copy_refs[k][rows, :width], take(vec_same_ref, upper ^ plan_ref[2]))
        total += 2.0 * dot(
            copy_refs[k][rows, width : 2 * width], take(vec_other_ref, upper ^ plan_ref[3])
        )
        sums_ref[3] += fold(total * left(k, h))

    @pl.when(plan_ref[5] == 1)
    def _():
        for k, h in cuts[: len(cuts) // 2]:
            rows = slice(h * piece, (h + 1) * piece)
            total = 2.0 * dot(copy_refs[k][rows, 2 * width :], vec_same_ref[width:, :])
            sums_ref[3] += fold(total * left(k, h))


def tail(plan, same, other, found, grads_col, grads_row, inner, queries, copies, even):
    rows, count = queries.shape
    args = [same, other, *found, grads_col, grads_row, inner, queries, *copies]
    return pl.pallas_call(
        functools.partial(tail_kernel, even, len(copies)),
        in_specs=[pl.BlockSpec(memory_space=pltpu.SMEM)]
        + [pl.BlockSpec(memory_space=pltpu.VMEM)] * len(args),
        out_specs=[pl.BlockSpec(memory_space=pltpu.VMEM)] * 2,
        out_shape=[
            jax.ShapeDtypeStruct((rows, count), F32),
            jax.ShapeDtypeStruct((4, 8, count), F32),
        ],
        scratch_shapes=[pltpu.VMEM((rows, count), BF), pltpu.VMEM((rows, count), BF)],
        compiler_params=params(16),
        cost_estimate=cost(4 * rows * rows * count, 4 * rows * rows),
        name="tail",
    )(plan, *args)


def after(value, *others):
    return lax.optimization_barrier((value,) + others)[0]


def integers(*values):
    return jnp.stack([jnp.asarray(v).astype(jnp.int32) for v in values])


def shards(activations, out_grads, proj_in, proj_out, lengths, gram_old, queries):
    local_count = lengths.shape[0]
    rank = proj_in.shape[1]
    row_count = lax.axis_size("row")
    col_count = lax.axis_size("col")
    rows, cols = gram_old.shape
    count = queries.shape[1]
    tokens = local_count * SEQ
    tiers = row_count // 2
    files = col_count // 2
    piece = rows // tiers
    row = lax.axis_index("row")
    col = lax.axis_index("col")
    z, y = row // 2, row % 2
    x, core = col // 2, col % 2
    total_examples = local_count * row_count * col_count
    scale = (1.0 - decay_rate) / total_examples

    def move(value, goes):
        pairs = []
        for r in range(row_count):
            for c in range(col_count):
                to = goes(r // 2, r % 2, c // 2, c % 2)
                if to is not None:
                    pairs.append((r * col_count + c, (to[0] * 2 + to[1]) * col_count + to[2] * 2 + to[3]))
        return lax.ppermute(value, ("row", "col"), pairs)

    def swap_y(value):
        return move(value, lambda z, y, x, k: (z, 1 - y, x, k))

    def swap_core(value):
        return move(value, lambda z, y, x, k: (z, y, x, 1 - k))

    def ring_z(value, by=1):
        return move(value, lambda z, y, x, k: ((z + by) % tiers, y, x, k))

    def ring_x(value):
        return move(value, lambda z, y, x, k: (z, y, (x + 1) % files, k))

    def flip_x(value, bit):
        return move(value, lambda z, y, x, k: (z, y, x ^ bit, k))

    def spread_z(value):
        return [value] + [ring_z(value, by) for by in range(1, tiers)]

    vec = queries.astype(BF).T
    away = back_product(integers(1 - y, 0), vec, gram_old)
    come = swap_y(away)

    low_in = dot(activations, proj_in).astype(BF)
    low_out = dot(proj_out, out_grads, ((0,), (1,))).astype(BF)
    slot = jnp.arange(tokens, dtype=jnp.int32)
    valid_mask = slot % SEQ < jnp.repeat(lengths, SEQ)
    low_out = jnp.where(valid_mask[None, :], low_out, jnp.zeros((), BF))
    low_out = low_out.reshape(rank, tokens // rank, rank).transpose(1, 0, 2).reshape(tokens, rank)
    local = after(jnp.concatenate([low_in, low_out], axis=0), away)
    factors = spread_z(local)

    here = back_product(after(integers(y, z == col), local), vec, gram_old, queries)
    here = here.reshape(tiers, piece, count)
    come = come.reshape(tiers, piece, count)

    def piece_for(by):
        at = (z + by) % tiers
        one = lax.dynamic_index_in_dim(here, at, 0, keepdims=False)
        two = lax.dynamic_index_in_dim(come, at, 0, keepdims=False)
        return one + two.astype(F32)

    sends = [piece_for(by).astype(BF) for by in range(1, tiers)]
    parts = [ring_z(sends[by - 1], by) for by in range(1, tiers)]

    factors = jnp.stack(lax.optimization_barrier((*factors, here))[:tiers])
    across = [factors]
    for dx in range(1, files):
        across.append(move(factors, lambda z, y, x, k: (z, y, (x + dx) % files, k)))
    own = []
    for one in across:
        own.append(one)
        own.append(swap_y(after(one, *sends)))

    total = piece_for(0)
    for part in parts:
        total = total + part.astype(F32)
    short = total.astype(BF)

    same = spread_z(short)
    held = lax.optimization_barrier((*own, short))[:-1]
    mate = [swap_core(f) for f in held]
    grads_col, grads_row = build_grads(integers(row, col), held, mate, rows, cols)
    partial = dot(grads_row, queries.astype(BF))
    fetched = swap_y(partial.astype(BF))
    same = lax.optimization_barrier((*same, fetched, partial))[:-1]
    fetched = same[-1]
    stacked = jnp.stack(same[:-1])
    inner = (partial + fetched.astype(F32)).astype(BF)
    sums = spread_z(inner)
    other = swap_y(stacked)

    fellow = swap_core(stacked)
    cut = tiers // 2
    half = lax.dynamic_slice_in_dim(
        jnp.where(core == z % 2, stacked, fellow), core * cut, cut, 0
    )
    came = half
    for dx in range(1, files):
        got = move(half, lambda z, y, x, k: (z, y, (x + dx) % files, k))
        came = got if files == 2 else jnp.where((x - dx) % files == z // 2, got, came)
    flags = integers(row > 2 * col + y, row > 2 * col + 1 - y)
    block = min(256, rows // 4)
    at = integers(
        row * rows - col * cols,
        2 * y + flags[0],
        2 * (1 - y) + flags[1],
        jnp.where(z == col, 2 * y + 1, -1),
        2 * y + 1 - flags[0],
        2 * (1 - y) + 1 - flags[1],
        -1,
    )
    gram_new, copy = update_gram(
        after(at, half), gram_old, grads_row, grads_col, scale, 0, rows // block, block, None
    )
    came, *sums = lax.optimization_barrier((came, *sums, gram_new))[:-1]
    found = [fellow, came, swap_core(came)]
    inner = sum(v.astype(F32) for v in reversed(sums))
    inner = (scale * inner).astype(BF)
    plan = jnp.concatenate(
        [
            integers(z, y),
            flags,
            integers(jnp.where(z == col, 1, 2), z == col, x == z // 2, core == z % 2, core),
        ]
    )
    mapped, sums = tail(
        after(plan, gram_new), stacked, other, found, grads_col, grads_row, inner, queries,
        [copy], 1.0 / col_count,
    )
    sums = jnp.sum(sums, axis=1)
    sums = sums + swap_core(sums)
    bit = 1
    while bit < files:
        sums = sums + flip_x(sums, bit)
        bit *= 2
    sums = sums + swap_y(sums)
    around = jnp.stack(spread_z(sums))
    sums = sum(
        lax.dynamic_index_in_dim(around, (z - k) % tiers, 0, keepdims=False) for k in range(tiers)
    )
    norm_now, along, square, curve = sums[0], sums[1], sums[2], sums[3]
    step = norm_now / along
    norm_next = step * step * square - norm_now
    momentum = norm_next / norm_now
    curvature = along - 2.0 * step * square + step * step * curve
    step_next = norm_next / (curvature - momentum * norm_next / step)
    solution = (step + step_next * (1.0 + momentum)) * queries - (step_next * step) * mapped
    return (gram_new, solution)


def solution(mesh):
    in_specs = (
        P(("row", "col"), None),
        P(("row", "col"), None),
        P(),
        P(),
        P(("row", "col")),
        P("row", "col"),
        P("row", None),
    )
    out_specs = (P("row", "col"), P("row", None))
    return jax.shard_map(shards, mesh=mesh, in_specs=in_specs, out_specs=out_specs, check_vma=False)
```

```python
import functools

import jax
import jax.numpy as jnp
from jax import lax
from jax.experimental import pallas as pl
from jax.experimental.pallas import tpu as pltpu
from jax.sharding import PartitionSpec as P

SEQ = 32

decay_rate = 0.5
damping = 1.0

BF = jnp.bfloat16
F32 = jnp.float32
VMEM_BYTES = 40 * 1024 * 1024


def dot(a, b, dims=((1,), (0,))):
    return lax.dot_general(a, b, (dims, ((), ())), preferred_element_type=F32)


def params(mebibytes=24):
    return pltpu.CompilerParams(vmem_limit_bytes=mebibytes * 1024 * 1024)


def cost(flops, moved):
    return pl.CostEstimate(flops=flops, bytes_accessed=moved, transcendentals=0)


def grads_kernel(parts, outs_col, outs_row, at_ref, *refs):
    own_refs, mate_refs = refs[:parts], refs[parts : 2 * parts]
    col_ref, row_ref, rows_ref, picked_ref = refs[2 * parts :]
    tiers, depth, rank = own_refs[0].shape
    tokens = depth // 2
    slots = tokens // SEQ
    halves = tokens // rank
    outs = outs_col + outs_row
    files = parts // 2
    z, y, x = at_ref[0] // 2, at_ref[0] % 2, at_ref[1] // 2
    even = at_ref[1] % 2 == 0
    example = lax.broadcasted_iota(jnp.int32, (slots, rank), 0)
    token = lax.broadcasted_iota(jnp.int32, (slots, rank), 1)
    masks = [((token + h * rank) // SEQ == example).astype(F32) for h in range(halves)]
    col_at = pl.multiple_of(at_ref[1] * outs_col, outs_col)
    row_at = pl.multiple_of(at_ref[0] * outs_row, outs_row)

    def build(k, low_in):
        left = []
        for h in range(halves):
            picked_ref[k, h, :outs_col, :] = rows_ref[k, pl.ds(h * rank + col_at, outs_col), :]
            picked_ref[k, h, outs_col:, :] = rows_ref[k, pl.ds(h * rank + row_at, outs_row), :]
        for h in range(halves):
            rows = picked_ref[k, h]
            spread = rows[:, None, :] * masks[h][None, :, :]
            left.append(spread.reshape(outs * slots, rank).astype(BF))
        left = jnp.concatenate(left, axis=1)
        return dot(left, low_in).reshape(outs, slots, rank)

    for part in range(parts):
        from_x = lax.rem(x - part // 2 + files, files)

        def chunk(i, carry, part=part, from_x=from_x):
            own, mate = own_refs[part][i], mate_refs[part][i]
            rows_ref[0] = jnp.where(even, own[tokens:, :], mate[tokens:, :]).astype(F32)
            rows_ref[1] = jnp.where(even, mate[tokens:, :], own[tokens:, :]).astype(F32)
            first = jnp.where(even, own[:tokens, :], mate[:tokens, :])
            second = jnp.where(even, mate[:tokens, :], own[:tokens, :])
            both = jnp.concatenate([build(0, first), build(1, second)], axis=1).astype(BF)
            from_z = lax.rem(z - i + tiers, tiers)
            place = ((from_x * tiers + from_z) * 2 + (y ^ (part % 2))) * (2 * slots)
            place = pl.ds(pl.multiple_of(place, 2 * slots), 2 * slots)
            for o in range(outs_col):
                col_ref[place, o * rank : (o + 1) * rank] = both[o]
            for o in range(outs_row):
                row_ref[place, o * rank : (o + 1) * rank] = both[outs_col + o]
            return carry

        lax.fori_loop(0, tiers, chunk, 0)


def build_grads(place, own, mate, rows, cols):
    parts = len(own)
    tiers, depth, rank = own[0].shape
    tokens = depth // 2
    total = 2 * parts * tiers * tokens // SEQ
    return pl.pallas_call(
        functools.partial(grads_kernel, parts, cols // rank, rows // rank),
        in_specs=[pl.BlockSpec(memory_space=pltpu.SMEM)]
        + [pl.BlockSpec(memory_space=pltpu.VMEM)] * (2 * parts),
        out_specs=[pl.BlockSpec(memory_space=pltpu.VMEM)] * 2,
        out_shape=[
            jax.ShapeDtypeStruct((total, cols), BF),
            jax.ShapeDtypeStruct((total, rows), BF),
        ],
        scratch_shapes=[
            pltpu.VMEM((2, tokens, rank), F32),
            pltpu.VMEM((2, tokens // rank, (cols + rows) // rank, rank), F32),
        ],
        compiler_params=params(16),
        cost_estimate=cost(2 * total * (rows + cols) * tokens, 2 * total * (rows + cols)),
        name="build_grads",
    )(place, *own, *mate)


def back_kernel(streams, plan_ref, *refs):
    vec_ref, gram_refs, out_ref = refs[0], refs[1 : 1 + streams], refs[-1]
    depth = gram_refs[0].shape[0]
    total = None
    for s in range(streams):
        vec = vec_ref[:, s * depth : (s + 1) * depth]
        value = dot(vec, gram_refs[s][...].astype(BF))
        total = value if total is None else total + value
    total = decay_rate * total.T
    if len(refs) > streams + 2:
        own = jnp.where(plan_ref[1] == 1, damping, 0.0)
        total = total + own * refs[streams + 1][...]
    out_ref[...] = total.astype(out_ref.dtype)


def back_product(plan, vec, gram, queries=None):
    count, rows = vec.shape
    width = gram.shape[1] // 2
    block = min(512, width)
    steps = width // block
    streams = 2
    depth = rows // streams

    def gram_at(s, i, plan_ref):
        return (s, plan_ref[0] * steps + i)

    in_specs = [pl.BlockSpec((count, rows), lambda i, plan_ref: (0, 0))]
    for s in range(streams):
        in_specs.append(pl.BlockSpec((depth, block), functools.partial(gram_at, s)))
    args = [vec] + [gram] * streams
    kind = BF
    if queries is not None:
        in_specs.append(pl.BlockSpec((block, count), lambda i, plan_ref: (i, 0)))
        args.append(queries)
        kind = F32
    return pl.pallas_call(
        functools.partial(back_kernel, streams),
        grid_spec=pltpu.PrefetchScalarGridSpec(
            num_scalar_prefetch=1,
            grid=(steps,),
            in_specs=in_specs,
            out_specs=pl.BlockSpec((block, count), lambda i, plan_ref: (i, 0)),
        ),
        out_shape=jax.ShapeDtypeStruct((width, count), kind),
        compiler_params=params(),
        cost_estimate=cost(2 * rows * width * count, 4 * rows * width + 4 * width * count),
        name="back_product",
    )(plan, *args)


def gram_kernel(scale, block, first, at_ref, gram_ref, left_ref, right_ref, *rest):
    out_ref, copy_ref = rest[-2:]
    strip = copy_ref.shape[1] // 3
    lower = ((first + pl.program_id(0)) * block >= strip).astype(jnp.int32)
    left = left_ref[...]
    offset = at_ref[0] + (first + pl.program_id(0)) * block
    ahead = lax.broadcasted_iota(jnp.int32, (block, strip), 0)
    ahead = ahead - lax.broadcasted_iota(jnp.int32, (block, strip), 1)
    for s in range(gram_ref.shape[1] // strip):
        part = slice(s * strip, (s + 1) * strip)
        product = dot(left, right_ref[:, part], ((0,), (0,)))
        value = decay_rate * gram_ref[:, part] + scale * product
        value = value + jnp.where(ahead == s * strip - offset, damping, 0.0)
        out_ref[:, part] = value
        short = value.astype(BF)
        for k in range(3):

            @pl.when(at_ref[1 + 3 * lower + k] == s)
            def _(k=k, short=short):
                copy_ref[:, k * strip : (k + 1) * strip] = short


def update_gram(at, gram, left, right, scale, first, count, block, before):
    rows, cols = gram.shape
    examples = left.shape[0]
    width = 3 * (cols // 4)
    in_specs = [
        pl.BlockSpec((block, cols), lambda i, at_ref: (first + i, 0)),
        pl.BlockSpec((examples, block), lambda i, at_ref: (0, first + i)),
        pl.BlockSpec((examples, cols), lambda i, at_ref: (0, 0)),
    ]
    args = [gram, left, right]
    alias = {}
    if before is not None:
        in_specs.append(pl.BlockSpec(memory_space=pl.ANY))
        args.append(before)
        alias = {4: 0}
    return pl.pallas_call(
        functools.partial(gram_kernel, scale, block, first),
        grid_spec=pltpu.PrefetchScalarGridSpec(
            num_scalar_prefetch=1,
            grid=(count,),
            in_specs=in_specs,
            out_specs=[
                pl.BlockSpec((block, cols), lambda i, at_ref: (first + i, 0)),
                pl.BlockSpec((block, width), lambda i, at_ref: (i, 0)),
            ],
        ),
        out_shape=[
            jax.ShapeDtypeStruct((rows, cols), F32),
            jax.ShapeDtypeStruct((count * block, width), BF),
        ],
        input_output_aliases=alias,
        compiler_params=params(30),
        cost_estimate=cost(2 * count * block * cols * examples, 8 * count * block * cols),
        name="update_gram",
    )(at, *args)


def tail_kernel(scale, even, pieces, plan_ref, *refs):
    same_ref, other_ref, mate_ref, came_ref, rest_ref = refs[:5]
    tiers, piece, count = same_ref.shape
    depth = tiers * piece
    width = depth // 2
    col_ref, row_ref, query_ref = refs[5:8]
    copy_refs, inner_refs = refs[8 : 8 + pieces], refs[8 + pieces : 8 + pieces + tiers]
    mapped_ref, sums_ref, vec_same_ref, vec_other_ref = refs[8 + pieces + tiers :]
    inner = sum(ref[...].astype(F32) for ref in reversed(inner_refs))
    inner = (scale * inner).astype(BF)
    tier, y = plan_ref[0], plan_ref[1]
    near, source = plan_ref[6] == 1, plan_ref[7] == 1
    along, square = jnp.zeros((8, count), F32), jnp.zeros((8, count), F32)
    norm = jnp.zeros((8, count), F32)

    def fold(value):
        return jnp.sum(value.reshape(value.shape[0] // 8, 8, count), axis=0)

    def low_rank(ref, start):
        part = ref[:, pl.ds(pl.multiple_of(start * piece, piece), piece)]
        return dot(part, inner, ((0,), (0,)))

    for s in range(tiers):
        quarter = lax.rem(tier - s + tiers, tiers)
        rows = pl.ds(pl.multiple_of(quarter * piece, piece), piece)
        own = same_ref[s].astype(F32)
        value = own + low_rank(col_ref, y * tiers + quarter)
        vec_same_ref[rows, :] = value.astype(BF)
        value = other_ref[s].astype(F32) + low_rank(col_ref, (1 - y) * tiers + quarter)
        vec_other_ref[rows, :] = value.astype(BF)
        here = plan_ref[8] == s // (tiers // 2)
        got = jnp.where(here, came_ref[s % (tiers // 2)], rest_ref[s % (tiers // 2)]).astype(F32)
        got = jnp.where(near, jnp.where(source, own, mate_ref[s].astype(F32)), got)
        value = got + low_rank(row_ref, quarter)
        mapped_ref[rows, :] = value
        query = query_ref[rows, :]
        norm += fold(query * query)
        along += fold(query * value)
        square += fold(value * value)

    def take(ref, quadrant):
        return ref[pl.ds(pl.multiple_of(quadrant * width, width), width), :]

    sums_ref[0] = even * norm
    sums_ref[1] = even * along
    sums_ref[2] = even * square
    sums_ref[3] = jnp.zeros_like(norm)
    weight = plan_ref[4].astype(F32)
    cuts = [(k, h) for k in range(pieces) for h in range(tiers // pieces)]

    def left(k, h):
        start = (k * (tiers // pieces) + h) * piece
        return mapped_ref[start : start + piece, :]

    for k, h in cuts:
        upper = (k * (tiers // pieces) + h) * 2 // tiers
        rows = slice(h * piece, (h + 1) * piece)
        total = weight * dot(copy_refs[k][rows, :width], take(vec_same_ref, upper ^ plan_ref[2]))
        total += 2.0 * dot(
            copy_refs[k][rows, width : 2 * width], take(vec_other_ref, upper ^ plan_ref[3])
        )
        sums_ref[3] += fold(total * left(k, h))

    @pl.when(plan_ref[5] == 1)
    def _():
        for k, h in cuts[: len(cuts) // 2]:
            rows = slice(h * piece, (h + 1) * piece)
            total = 2.0 * dot(copy_refs[k][rows, 2 * width :], vec_same_ref[width:, :])
            sums_ref[3] += fold(total * left(k, h))


def tail(plan, same, other, found, grads_col, grads_row, inner, queries, copies, scale, even):
    rows, count = queries.shape
    args = [same, other, *found, grads_col, grads_row, queries, *copies, *inner]
    return pl.pallas_call(
        functools.partial(tail_kernel, scale, even, len(copies)),
        in_specs=[pl.BlockSpec(memory_space=pltpu.SMEM)]
        + [pl.BlockSpec(memory_space=pltpu.VMEM)] * len(args),
        out_specs=[pl.BlockSpec(memory_space=pltpu.VMEM)] * 2,
        out_shape=[
            jax.ShapeDtypeStruct((rows, count), F32),
            jax.ShapeDtypeStruct((4, 8, count), F32),
        ],
        scratch_shapes=[pltpu.VMEM((rows, count), BF), pltpu.VMEM((rows, count), BF)],
        compiler_params=params(16),
        cost_estimate=cost(4 * rows * rows * count, 4 * rows * rows),
        name="tail",
    )(plan, *args)


def after(value, *others):
    return lax.optimization_barrier((value,) + others)[0]


def integers(*values):
    return jnp.stack([jnp.asarray(v).astype(jnp.int32) for v in values])


def shards(activations, out_grads, proj_in, proj_out, lengths, gram_old, queries):
    local_count = lengths.shape[0]
    rank = proj_in.shape[1]
    row_count = lax.axis_size("row")
    col_count = lax.axis_size("col")
    rows, cols = gram_old.shape
    count = queries.shape[1]
    tokens = local_count * SEQ
    tiers = row_count // 2
    files = col_count // 2
    piece = rows // tiers
    row = lax.axis_index("row")
    col = lax.axis_index("col")
    z, y = row // 2, row % 2
    x, core = col // 2, col % 2
    total_examples = local_count * row_count * col_count
    scale = (1.0 - decay_rate) / total_examples

    def move(value, goes):
        pairs = []
        for r in range(row_count):
            for c in range(col_count):
                to = goes(r // 2, r % 2, c // 2, c % 2)
                if to is not None:
                    pairs.append((r * col_count + c, (to[0] * 2 + to[1]) * col_count + to[2] * 2 + to[3]))
        return lax.ppermute(value, ("row", "col"), pairs)

    def swap_y(value):
        return move(value, lambda z, y, x, k: (z, 1 - y, x, k))

    def swap_core(value):
        return move(value, lambda z, y, x, k: (z, y, x, 1 - k))

    def ring_z(value, by=1):
        return move(value, lambda z, y, x, k: ((z + by) % tiers, y, x, k))

    def ring_x(value):
        return move(value, lambda z, y, x, k: (z, y, (x + 1) % files, k))

    def flip_x(value, bit):
        return move(value, lambda z, y, x, k: (z, y, x ^ bit, k))

    def spread_z(value):
        return [value] + [ring_z(value, by) for by in range(1, tiers)]

    vec = queries.astype(BF).T
    away = back_product(integers(1 - y, 0), vec, gram_old)
    come = swap_y(away)

    low_in = dot(activations, proj_in).astype(BF)
    low_out = dot(proj_out, out_grads, ((0,), (1,))).astype(BF)
    slot = jnp.arange(tokens, dtype=jnp.int32)
    valid_mask = slot % SEQ < jnp.repeat(lengths, SEQ)
    low_out = jnp.where(valid_mask[None, :], low_out, jnp.zeros((), BF))
    low_out = low_out.reshape(rank, tokens // rank, rank).transpose(1, 0, 2).reshape(tokens, rank)
    local = after(jnp.concatenate([low_in, low_out], axis=0), away)
    factors = spread_z(local)

    here = back_product(after(integers(y, z == col), local), vec, gram_old, queries)
    here = here.reshape(tiers, piece, count)
    come = come.reshape(tiers, piece, count)

    def piece_for(by):
        at = (z + by) % tiers
        one = lax.dynamic_index_in_dim(here, at, 0, keepdims=False)
        two = lax.dynamic_index_in_dim(come, at, 0, keepdims=False)
        return one + two.astype(F32)

    sends = [piece_for(by).astype(BF) for by in range(1, tiers)]
    parts = [ring_z(sends[by - 1], by) for by in range(1, tiers)]

    factors = jnp.stack(lax.optimization_barrier((*factors, here))[:tiers])
    across = [factors]
    for dx in range(1, files):
        across.append(move(factors, lambda z, y, x, k: (z, y, (x + dx) % files, k)))
    own = []
    for one in across:
        own.append(one)
        own.append(swap_y(after(one, *sends)))

    total = piece_for(0)
    for part in parts:
        total = total + part.astype(F32)
    short = total.astype(BF)

    same = spread_z(short)
    held = lax.optimization_barrier((*own, short))[:-1]
    mate = [swap_core(f) for f in held]
    grads_col, grads_row = build_grads(integers(row, col), held, mate, rows, cols)
    partial = dot(grads_row, queries.astype(BF))
    fetched = swap_y(partial.astype(BF))
    same = lax.optimization_barrier((*same, fetched, partial))[:-1]
    fetched = same[-1]
    stacked = jnp.stack(same[:-1])
    inner = (partial + fetched.astype(F32)).astype(BF)
    sums = spread_z(inner)
    other = swap_y(stacked)

    fellow = swap_core(stacked)
    cut = tiers // 2
    half = lax.dynamic_slice_in_dim(
        jnp.where(core == z % 2, stacked, fellow), core * cut, cut, 0
    )
    came = half
    for dx in range(1, files):
        got = move(half, lambda z, y, x, k: (z, y, (x + dx) % files, k))
        came = got if files == 2 else jnp.where((x - dx) % files == z // 2, got, came)
    flags = integers(row > 2 * col + y, row > 2 * col + 1 - y)
    block = min(256, rows // 4)
    at = integers(
        row * rows - col * cols,
        2 * y + flags[0],
        2 * (1 - y) + flags[1],
        jnp.where(z == col, 2 * y + 1, -1),
        2 * y + 1 - flags[0],
        2 * (1 - y) + 1 - flags[1],
        -1,
    )
    gram_new, copy = update_gram(
        after(at, half), gram_old, grads_row, grads_col, scale, 0, rows // block, block, None
    )
    came, *sums = lax.optimization_barrier((came, *sums, gram_new))[:-1]
    found = [fellow, came, swap_core(came)]
    plan = jnp.concatenate(
        [
            integers(z, y),
            flags,
            integers(jnp.where(z == col, 1, 2), z == col, x == z // 2, core == z % 2, core),
        ]
    )
    mapped, sums = tail(
        after(plan, gram_new), stacked, other, found, grads_col, grads_row, sums, queries,
        [copy], scale, 1.0 / col_count,
    )
    sums = jnp.sum(sums, axis=1)
    sums = sums + swap_core(sums)
    bit = 1
    while bit < files:
        sums = sums + flip_x(sums, bit)
        bit *= 2
    sums = sums + swap_y(sums)
    around = jnp.stack(spread_z(sums))
    sums = sum(
        lax.dynamic_index_in_dim(around, (z - k) % tiers, 0, keepdims=False) for k in range(tiers)
    )
    norm_now, along, square, curve = sums[0], sums[1], sums[2], sums[3]
    step = norm_now / along
    norm_next = step * step * square - norm_now
    momentum = norm_next / norm_now
    curvature = along - 2.0 * step * square + step * step * curve
    step_next = norm_next / (curvature - momentum * norm_next / step)
    solution = (step + step_next * (1.0 + momentum)) * queries - (step_next * step) * mapped
    return (gram_new, solution)


def solution(mesh):
    in_specs = (
        P(("row", "col"), None),
        P(("row", "col"), None),
        P(),
        P(),
        P(("row", "col")),
        P("row", "col"),
        P("row", None),
    )
    out_specs = (P("row", "col"), P("row", None))
    return jax.shard_map(shards, mesh=mesh, in_specs=in_specs, out_specs=out_specs, check_vma=False)
```

```python
import functools

import jax
import jax.numpy as jnp
from jax import lax
from jax.experimental import pallas as pl
from jax.experimental.pallas import tpu as pltpu
from jax.sharding import PartitionSpec as P

SEQ = 32

decay_rate = 0.5
damping = 1.0

BF = jnp.bfloat16
F32 = jnp.float32
VMEM_BYTES = 40 * 1024 * 1024


def dot(a, b, dims=((1,), (0,))):
    return lax.dot_general(a, b, (dims, ((), ())), preferred_element_type=F32)


def params(mebibytes=24):
    return pltpu.CompilerParams(vmem_limit_bytes=mebibytes * 1024 * 1024)


def cost(flops, moved):
    return pl.CostEstimate(flops=flops, bytes_accessed=moved, transcendentals=0)


def grads_kernel(parts, outs_col, outs_row, at_ref, *refs):
    own_refs, mate_refs = refs[:parts], refs[parts : 2 * parts]
    col_ref, row_ref, rows_ref, picked_ref = refs[2 * parts :]
    tiers, depth, rank = own_refs[0].shape
    tokens = depth // 2
    slots = tokens // SEQ
    halves = tokens // rank
    outs = outs_col + outs_row
    files = parts // 2
    z, y, x = at_ref[0] // 2, at_ref[0] % 2, at_ref[1] // 2
    even = at_ref[1] % 2 == 0
    example = lax.broadcasted_iota(jnp.int32, (slots, rank), 0)
    token = lax.broadcasted_iota(jnp.int32, (slots, rank), 1)
    masks = [((token + h * rank) // SEQ == example).astype(F32) for h in range(halves)]
    col_at = pl.multiple_of(at_ref[1] * outs_col, outs_col)
    row_at = pl.multiple_of(at_ref[0] * outs_row, outs_row)

    def build(k, low_in):
        left = []
        for h in range(halves):
            picked_ref[k, h, :outs_col, :] = rows_ref[k, pl.ds(h * rank + col_at, outs_col), :]
            picked_ref[k, h, outs_col:, :] = rows_ref[k, pl.ds(h * rank + row_at, outs_row), :]
        for h in range(halves):
            rows = picked_ref[k, h]
            spread = rows[:, None, :] * masks[h][None, :, :]
            left.append(spread.reshape(outs * slots, rank).astype(BF))
        left = jnp.concatenate(left, axis=1)
        return dot(left, low_in).reshape(outs, slots, rank)

    for part in range(parts):
        from_x = lax.rem(x - part // 2 + files, files)

        def chunk(i, carry, part=part, from_x=from_x):
            own, mate = own_refs[part][i], mate_refs[part][i]
            rows_ref[0] = jnp.where(even, own[tokens:, :], mate[tokens:, :]).astype(F32)
            rows_ref[1] = jnp.where(even, mate[tokens:, :], own[tokens:, :]).astype(F32)
            first = jnp.where(even, own[:tokens, :], mate[:tokens, :])
            second = jnp.where(even, mate[:tokens, :], own[:tokens, :])
            both = jnp.concatenate([build(0, first), build(1, second)], axis=1).astype(BF)
            from_z = lax.rem(z - i + tiers, tiers)
            place = ((from_x * tiers + from_z) * 2 + (y ^ (part % 2))) * (2 * slots)
            place = pl.ds(pl.multiple_of(place, 2 * slots), 2 * slots)
            for o in range(outs_col):
                col_ref[place, o * rank : (o + 1) * rank] = both[o]
            for o in range(outs_row):
                row_ref[place, o * rank : (o + 1) * rank] = both[outs_col + o]
            return carry

        lax.fori_loop(0, tiers, chunk, 0)


def build_grads(place, own, mate, rows, cols):
    parts = len(own)
    tiers, depth, rank = own[0].shape
    tokens = depth // 2
    total = 2 * parts * tiers * tokens // SEQ
    return pl.pallas_call(
        functools.partial(grads_kernel, parts, cols // rank, rows // rank),
        in_specs=[pl.BlockSpec(memory_space=pltpu.SMEM)]
        + [pl.BlockSpec(memory_space=pltpu.VMEM)] * (2 * parts),
        out_specs=[pl.BlockSpec(memory_space=pltpu.VMEM)] * 2,
        out_shape=[
            jax.ShapeDtypeStruct((total, cols), BF),
            jax.ShapeDtypeStruct((total, rows), BF),
        ],
        scratch_shapes=[
            pltpu.VMEM((2, tokens, rank), F32),
            pltpu.VMEM((2, tokens // rank, (cols + rows) // rank, rank), F32),
        ],
        compiler_params=params(16),
        cost_estimate=cost(2 * total * (rows + cols) * tokens, 2 * total * (rows + cols)),
        name="build_grads",
    )(place, *own, *mate)


def back_kernel(streams, plan_ref, *refs):
    vec_ref, gram_refs, out_ref = refs[0], refs[1 : 1 + streams], refs[-1]
    depth = gram_refs[0].shape[0]
    total = None
    for s in range(streams):
        vec = vec_ref[:, s * depth : (s + 1) * depth]
        value = dot(vec, gram_refs[s][...].astype(BF))
        total = value if total is None else total + value
    total = decay_rate * total.T
    if len(refs) > streams + 2:
        own = jnp.where(plan_ref[1] == 1, damping, 0.0)
        total = total + own * refs[streams + 1][...]
    out_ref[...] = total.astype(out_ref.dtype)


def back_product(plan, vec, gram, queries=None):
    count, rows = vec.shape
    width = gram.shape[1] // 2
    block = min(512, width)
    steps = width // block
    streams = 2
    depth = rows // streams

    def gram_at(s, i, plan_ref):
        return (s, plan_ref[0] * steps + i)

    in_specs = [pl.BlockSpec((count, rows), lambda i, plan_ref: (0, 0))]
    for s in range(streams):
        in_specs.append(pl.BlockSpec((depth, block), functools.partial(gram_at, s)))
    args = [vec] + [gram] * streams
    kind = BF
    if queries is not None:
        in_specs.append(pl.BlockSpec((block, count), lambda i, plan_ref: (i, 0)))
        args.append(queries)
        kind = F32
    return pl.pallas_call(
        functools.partial(back_kernel, streams),
        grid_spec=pltpu.PrefetchScalarGridSpec(
            num_scalar_prefetch=1,
            grid=(steps,),
            in_specs=in_specs,
            out_specs=pl.BlockSpec((block, count), lambda i, plan_ref: (i, 0)),
        ),
        out_shape=jax.ShapeDtypeStruct((width, count), kind),
        compiler_params=params(),
        cost_estimate=cost(2 * rows * width * count, 4 * rows * width + 4 * width * count),
        name="back_product",
    )(plan, *args)


def gram_kernel(scale, block, first, at_ref, gram_ref, left_ref, right_ref, *rest):
    out_ref, copy_ref = rest[-2:]
    strip = copy_ref.shape[1] // 3
    lower = ((first + pl.program_id(0)) * block >= strip).astype(jnp.int32)
    left = left_ref[...]
    offset = at_ref[0] + (first + pl.program_id(0)) * block
    ahead = lax.broadcasted_iota(jnp.int32, (block, strip), 0)
    ahead = ahead - lax.broadcasted_iota(jnp.int32, (block, strip), 1)
    for s in range(gram_ref.shape[1] // strip):
        part = slice(s * strip, (s + 1) * strip)
        product = dot(left, right_ref[:, part], ((0,), (0,)))
        value = decay_rate * gram_ref[:, part] + scale * product
        value = value + jnp.where(ahead == s * strip - offset, damping, 0.0)
        out_ref[:, part] = value
        short = value.astype(BF)
        for k in range(3):

            @pl.when(at_ref[1 + 3 * lower + k] == s)
            def _(k=k, short=short):
                copy_ref[:, k * strip : (k + 1) * strip] = short


def update_gram(at, gram, left, right, scale, first, count, block, before):
    rows, cols = gram.shape
    examples = left.shape[0]
    width = 3 * (cols // 4)
    in_specs = [
        pl.BlockSpec((block, cols), lambda i, at_ref: (first + i, 0)),
        pl.BlockSpec((examples, block), lambda i, at_ref: (0, first + i)),
        pl.BlockSpec((examples, cols), lambda i, at_ref: (0, 0)),
    ]
    args = [gram, left, right]
    alias = {}
    if before is not None:
        in_specs.append(pl.BlockSpec(memory_space=pl.ANY))
        args.append(before)
        alias = {4: 0}
    return pl.pallas_call(
        functools.partial(gram_kernel, scale, block, first),
        grid_spec=pltpu.PrefetchScalarGridSpec(
            num_scalar_prefetch=1,
            grid=(count,),
            in_specs=in_specs,
            out_specs=[
                pl.BlockSpec((block, cols), lambda i, at_ref: (first + i, 0)),
                pl.BlockSpec((block, width), lambda i, at_ref: (i, 0)),
            ],
        ),
        out_shape=[
            jax.ShapeDtypeStruct((rows, cols), F32),
            jax.ShapeDtypeStruct((count * block, width), BF),
        ],
        input_output_aliases=alias,
        compiler_params=params(30),
        cost_estimate=cost(2 * count * block * cols * examples, 8 * count * block * cols),
        name="update_gram",
    )(at, *args)


def tail_kernel(scale, even, pieces, plan_ref, *refs):
    same_ref, other_ref, mate_ref, came_ref, rest_ref = refs[:5]
    tiers, piece, count = same_ref.shape
    depth = tiers * piece
    width = depth // 2
    col_ref, row_ref, query_ref = refs[5:8]
    copy_refs, inner_refs = refs[8 : 8 + pieces], refs[8 + pieces : 8 + pieces + tiers]
    mapped_ref, total_ref, vec_same_ref, vec_other_ref, sums_ref = refs[8 + pieces + tiers :]
    inner = sum(ref[...].astype(F32) for ref in reversed(inner_refs))
    inner = (scale * inner).astype(BF)
    tier, y = plan_ref[0], plan_ref[1]
    near, source = plan_ref[6] == 1, plan_ref[7] == 1
    along, square = jnp.zeros((8, count), F32), jnp.zeros((8, count), F32)
    norm = jnp.zeros((8, count), F32)

    def fold(value):
        return jnp.sum(value.reshape(value.shape[0] // 8, 8, count), axis=0)

    def low_rank(ref, start):
        part = ref[:, pl.ds(pl.multiple_of(start * piece, piece), piece)]
        return dot(part, inner, ((0,), (0,)))

    for s in range(tiers):
        quarter = lax.rem(tier - s + tiers, tiers)
        rows = pl.ds(pl.multiple_of(quarter * piece, piece), piece)
        own = same_ref[s].astype(F32)
        value = own + low_rank(col_ref, y * tiers + quarter)
        vec_same_ref[rows, :] = value.astype(BF)
        value = other_ref[s].astype(F32) + low_rank(col_ref, (1 - y) * tiers + quarter)
        vec_other_ref[rows, :] = value.astype(BF)
        here = plan_ref[8] == s // (tiers // 2)
        got = jnp.where(here, came_ref[s % (tiers // 2)], rest_ref[s % (tiers // 2)]).astype(F32)
        got = jnp.where(near, jnp.where(source, own, mate_ref[s].astype(F32)), got)
        value = got + low_rank(row_ref, quarter)
        mapped_ref[rows, :] = value
        query = query_ref[rows, :]
        norm += fold(query * query)
        along += fold(query * value)
        square += fold(value * value)

    def take(ref, quadrant):
        return ref[pl.ds(pl.multiple_of(quadrant * width, width), width), :]

    sums_ref[0] = even * norm
    sums_ref[1] = even * along
    sums_ref[2] = even * square
    sums_ref[3] = jnp.zeros_like(norm)
    weight = plan_ref[4].astype(F32)
    cuts = [(k, h) for k in range(pieces) for h in range(tiers // pieces)]

    def left(k, h):
        start = (k * (tiers // pieces) + h) * piece
        return mapped_ref[start : start + piece, :]

    for k, h in cuts:
        upper = (k * (tiers // pieces) + h) * 2 // tiers
        rows = slice(h * piece, (h + 1) * piece)
        total = weight * dot(copy_refs[k][rows, :width], take(vec_same_ref, upper ^ plan_ref[2]))
        total += 2.0 * dot(
            copy_refs[k][rows, width : 2 * width], take(vec_other_ref, upper ^ plan_ref[3])
        )
        sums_ref[3] += fold(total * left(k, h))

    @pl.when(plan_ref[5] == 1)
    def _():
        for k, h in cuts[: len(cuts) // 2]:
            rows = slice(h * piece, (h + 1) * piece)
            total = 2.0 * dot(copy_refs[k][rows, 2 * width :], vec_same_ref[width:, :])
            sums_ref[3] += fold(total * left(k, h))

    total_ref[...] = jnp.sum(sums_ref[...], axis=1)


def tail(plan, same, other, found, grads_col, grads_row, inner, queries, copies, scale, even):
    rows, count = queries.shape
    args = [same, other, *found, grads_col, grads_row, queries, *copies, *inner]
    return pl.pallas_call(
        functools.partial(tail_kernel, scale, even, len(copies)),
        in_specs=[pl.BlockSpec(memory_space=pltpu.SMEM)]
        + [pl.BlockSpec(memory_space=pltpu.VMEM)] * len(args),
        out_specs=[pl.BlockSpec(memory_space=pltpu.VMEM)] * 2,
        out_shape=[
            jax.ShapeDtypeStruct((rows, count), F32),
            jax.ShapeDtypeStruct((4, count), F32),
        ],
        scratch_shapes=[
            pltpu.VMEM((rows, count), BF),
            pltpu.VMEM((rows, count), BF),
            pltpu.VMEM((4, 8, count), F32),
        ],
        compiler_params=params(16),
        cost_estimate=cost(4 * rows * rows * count, 4 * rows * rows),
        name="tail",
    )(plan, *args)


def after(value, *others):
    return lax.optimization_barrier((value,) + others)[0]


def integers(*values):
    return jnp.stack([jnp.asarray(v).astype(jnp.int32) for v in values])


def shards(activations, out_grads, proj_in, proj_out, lengths, gram_old, queries):
    local_count = lengths.shape[0]
    rank = proj_in.shape[1]
    row_count = lax.axis_size("row")
    col_count = lax.axis_size("col")
    rows, cols = gram_old.shape
    count = queries.shape[1]
    tokens = local_count * SEQ
    tiers = row_count // 2
    files = col_count // 2
    piece = rows // tiers
    row = lax.axis_index("row")
    col = lax.axis_index("col")
    z, y = row // 2, row % 2
    x, core = col // 2, col % 2
    total_examples = local_count * row_count * col_count
    scale = (1.0 - decay_rate) / total_examples

    def move(value, goes):
        pairs = []
        for r in range(row_count):
            for c in range(col_count):
                to = goes(r // 2, r % 2, c // 2, c % 2)
                if to is not None:
                    pairs.append((r * col_count + c, (to[0] * 2 + to[1]) * col_count + to[2] * 2 + to[3]))
        return lax.ppermute(value, ("row", "col"), pairs)

    def swap_y(value):
        return move(value, lambda z, y, x, k: (z, 1 - y, x, k))

    def swap_core(value):
        return move(value, lambda z, y, x, k: (z, y, x, 1 - k))

    def ring_z(value, by=1):
        return move(value, lambda z, y, x, k: ((z + by) % tiers, y, x, k))

    def ring_x(value):
        return move(value, lambda z, y, x, k: (z, y, (x + 1) % files, k))

    def flip_x(value, bit):
        return move(value, lambda z, y, x, k: (z, y, x ^ bit, k))

    def spread_z(value):
        return [value] + [ring_z(value, by) for by in range(1, tiers)]

    vec = queries.astype(BF).T
    away = back_product(integers(1 - y, 0), vec, gram_old)
    come = swap_y(away)

    low_in = dot(activations, proj_in).astype(BF)
    low_out = dot(proj_out, out_grads, ((0,), (1,))).astype(BF)
    slot = jnp.arange(tokens, dtype=jnp.int32)
    valid_mask = slot % SEQ < jnp.repeat(lengths, SEQ)
    low_out = jnp.where(valid_mask[None, :], low_out, jnp.zeros((), BF))
    low_out = low_out.reshape(rank, tokens // rank, rank).transpose(1, 0, 2).reshape(tokens, rank)
    local = after(jnp.concatenate([low_in, low_out], axis=0), away)
    factors = spread_z(local)

    here = back_product(after(integers(y, z == col), local), vec, gram_old, queries)
    here = here.reshape(tiers, piece, count)
    come = come.reshape(tiers, piece, count)

    def piece_for(by):
        at = (z + by) % tiers
        one = lax.dynamic_index_in_dim(here, at, 0, keepdims=False)
        two = lax.dynamic_index_in_dim(come, at, 0, keepdims=False)
        return one + two.astype(F32)

    sends = [piece_for(by).astype(BF) for by in range(1, tiers)]
    parts = [ring_z(sends[by - 1], by) for by in range(1, tiers)]

    factors = jnp.stack(lax.optimization_barrier((*factors, here))[:tiers])
    across = [factors]
    for dx in range(1, files):
        across.append(move(factors, lambda z, y, x, k: (z, y, (x + dx) % files, k)))
    own = []
    for one in across:
        own.append(one)
        own.append(swap_y(after(one, *sends)))

    total = piece_for(0)
    for part in parts:
        total = total + part.astype(F32)
    short = total.astype(BF)

    same = spread_z(short)
    held = lax.optimization_barrier((*own, short))[:-1]
    mate = [swap_core(f) for f in held]
    grads_col, grads_row = build_grads(integers(row, col), held, mate, rows, cols)
    partial = dot(grads_row, queries.astype(BF))
    fetched = swap_y(partial.astype(BF))
    same = lax.optimization_barrier((*same, fetched, partial))[:-1]
    fetched = same[-1]
    stacked = jnp.stack(same[:-1])
    inner = (partial + fetched.astype(F32)).astype(BF)
    sums = spread_z(inner)
    other = swap_y(stacked)

    fellow = swap_core(stacked)
    cut = tiers // 2
    half = lax.dynamic_slice_in_dim(
        jnp.where(core == z % 2, stacked, fellow), core * cut, cut, 0
    )
    found = [fellow]
    for flip in range(2):
        came = half
        for dx in range(1, files):
            got = move(half, lambda z, y, x, k: (z, y, (x + dx) % files, k ^ flip))
            came = got if files == 2 else jnp.where((x - dx) % files == z // 2, got, came)
        found.append(came)

    flags = integers(row > 2 * col + y, row > 2 * col + 1 - y)
    block = min(256, rows // 4)
    at = integers(
        row * rows - col * cols,
        2 * y + flags[0],
        2 * (1 - y) + flags[1],
        jnp.where(z == col, 2 * y + 1, -1),
        2 * y + 1 - flags[0],
        2 * (1 - y) + 1 - flags[1],
        -1,
    )
    gram_new, copy = update_gram(
        after(at, half), gram_old, grads_row, grads_col, scale, 0, rows // block, block, None
    )
    held = lax.optimization_barrier((*found[1:], *sums, gram_new))
    found, sums = [fellow, *held[:2]], held[2:-1]
    plan = jnp.concatenate(
        [
            integers(z, y),
            flags,
            integers(jnp.where(z == col, 1, 2), z == col, x == z // 2, core == z % 2, core),
        ]
    )
    mapped, sums = tail(
        after(plan, gram_new), stacked, other, found, grads_col, grads_row, sums, queries,
        [copy], scale, 1.0 / col_count,
    )
    sums = sums + swap_core(sums)
    bit = 1
    while bit < files:
        sums = sums + flip_x(sums, bit)
        bit *= 2
    sums = sums + swap_y(sums)
    around = jnp.stack(spread_z(sums))
    sums = sum(
        lax.dynamic_index_in_dim(around, (z - k) % tiers, 0, keepdims=False) for k in range(tiers)
    )
    norm_now, along, square, curve = sums[0], sums[1], sums[2], sums[3]
    step = norm_now / along
    norm_next = step * step * square - norm_now
    momentum = norm_next / norm_now
    curvature = along - 2.0 * step * square + step * step * curve
    step_next = norm_next / (curvature - momentum * norm_next / step)
    solution = (step + step_next * (1.0 + momentum)) * queries - (step_next * step) * mapped
    return (gram_new, solution)


def solution(mesh):
    in_specs = (
        P(("row", "col"), None),
        P(("row", "col"), None),
        P(),
        P(),
        P(("row", "col")),
        P("row", "col"),
        P("row", None),
    )
    out_specs = (P("row", "col"), P("row", None))
    return jax.shard_map(shards, mesh=mesh, in_specs=in_specs, out_specs=out_specs, check_vma=False)
```

```python
import functools

import jax
import jax.numpy as jnp
from jax import lax
from jax.experimental import pallas as pl
from jax.experimental.pallas import tpu as pltpu
from jax.sharding import PartitionSpec as P

SEQ = 32

decay_rate = 0.5
damping = 1.0

BF = jnp.bfloat16
F32 = jnp.float32
VMEM_BYTES = 40 * 1024 * 1024


def dot(a, b, dims=((1,), (0,))):
    return lax.dot_general(a, b, (dims, ((), ())), preferred_element_type=F32)


def params(mebibytes=24):
    return pltpu.CompilerParams(vmem_limit_bytes=mebibytes * 1024 * 1024)


def cost(flops, moved):
    return pl.CostEstimate(flops=flops, bytes_accessed=moved, transcendentals=0)


def grads_kernel(parts, outs_col, outs_row, at_ref, *refs):
    own_refs, mate_refs = refs[:parts], refs[parts : 2 * parts]
    col_ref, row_ref, rows_ref, picked_ref = refs[2 * parts :]
    tiers, depth, rank = own_refs[0].shape
    tokens = depth // 2
    slots = tokens // SEQ
    halves = tokens // rank
    outs = outs_col + outs_row
    files = parts // 2
    z, y, x = at_ref[0] // 2, at_ref[0] % 2, at_ref[1] // 2
    even = at_ref[1] % 2 == 0
    example = lax.broadcasted_iota(jnp.int32, (slots, rank), 0)
    token = lax.broadcasted_iota(jnp.int32, (slots, rank), 1)
    masks = [((token + h * rank) // SEQ == example).astype(F32) for h in range(halves)]
    col_at = pl.multiple_of(at_ref[1] * outs_col, outs_col)
    row_at = pl.multiple_of(at_ref[0] * outs_row, outs_row)

    def build(k, low_in):
        left = []
        for h in range(halves):
            picked_ref[k, h, :outs_col, :] = rows_ref[k, pl.ds(h * rank + col_at, outs_col), :]
            picked_ref[k, h, outs_col:, :] = rows_ref[k, pl.ds(h * rank + row_at, outs_row), :]
        for h in range(halves):
            rows = picked_ref[k, h]
            spread = rows[:, None, :] * masks[h][None, :, :]
            left.append(spread.reshape(outs * slots, rank).astype(BF))
        left = jnp.concatenate(left, axis=1)
        return dot(left, low_in).reshape(outs, slots, rank)

    for part in range(parts):
        from_x = lax.rem(x - part // 2 + files, files)

        def chunk(i, carry, part=part, from_x=from_x):
            own, mate = own_refs[part][i], mate_refs[part][i]
            rows_ref[0] = jnp.where(even, own[tokens:, :], mate[tokens:, :]).astype(F32)
            rows_ref[1] = jnp.where(even, mate[tokens:, :], own[tokens:, :]).astype(F32)
            first = jnp.where(even, own[:tokens, :], mate[:tokens, :])
            second = jnp.where(even, mate[:tokens, :], own[:tokens, :])
            both = jnp.concatenate([build(0, first), build(1, second)], axis=1).astype(BF)
            from_z = lax.rem(z - i + tiers, tiers)
            place = ((from_x * tiers + from_z) * 2 + (y ^ (part % 2))) * (2 * slots)
            place = pl.ds(pl.multiple_of(place, 2 * slots), 2 * slots)
            for o in range(outs_col):
                col_ref[place, o * rank : (o + 1) * rank] = both[o]
            for o in range(outs_row):
                row_ref[place, o * rank : (o + 1) * rank] = both[outs_col + o]
            return carry

        lax.fori_loop(0, tiers, chunk, 0)


def build_grads(place, own, mate, rows, cols):
    parts = len(own)
    tiers, depth, rank = own[0].shape
    tokens = depth // 2
    total = 2 * parts * tiers * tokens // SEQ
    return pl.pallas_call(
        functools.partial(grads_kernel, parts, cols // rank, rows // rank),
        in_specs=[pl.BlockSpec(memory_space=pltpu.SMEM)]
        + [pl.BlockSpec(memory_space=pltpu.VMEM)] * (2 * parts),
        out_specs=[pl.BlockSpec(memory_space=pltpu.VMEM)] * 2,
        out_shape=[
            jax.ShapeDtypeStruct((total, cols), BF),
            jax.ShapeDtypeStruct((total, rows), BF),
        ],
        scratch_shapes=[
            pltpu.VMEM((2, tokens, rank), F32),
            pltpu.VMEM((2, tokens // rank, (cols + rows) // rank, rank), F32),
        ],
        compiler_params=params(16),
        cost_estimate=cost(2 * total * (rows + cols) * tokens, 2 * total * (rows + cols)),
        name="build_grads",
    )(place, *own, *mate)


def back_kernel(streams, plan_ref, *refs):
    vec_ref, gram_refs, out_ref = refs[0], refs[1 : 1 + streams], refs[-1]
    depth = gram_refs[0].shape[0]
    total = None
    for s in range(streams):
        vec = vec_ref[:, s * depth : (s + 1) * depth]
        value = dot(vec, gram_refs[s][...].astype(BF))
        total = value if total is None else total + value
    total = decay_rate * total.T
    if len(refs) > streams + 2:
        own = jnp.where(plan_ref[1] == 1, damping, 0.0)
        total = total + own * refs[streams + 1][...]
    out_ref[...] = total.astype(out_ref.dtype)


def back_product(plan, vec, gram, queries=None):
    count, rows = vec.shape
    width = gram.shape[1] // 2
    block = min(512, width)
    steps = width // block
    streams = 2
    depth = rows // streams

    def gram_at(s, i, plan_ref):
        return (s, plan_ref[0] * steps + i)

    in_specs = [pl.BlockSpec((count, rows), lambda i, plan_ref: (0, 0))]
    for s in range(streams):
        in_specs.append(pl.BlockSpec((depth, block), functools.partial(gram_at, s)))
    args = [vec] + [gram] * streams
    kind = BF
    if queries is not None:
        in_specs.append(pl.BlockSpec((block, count), lambda i, plan_ref: (i, 0)))
        args.append(queries)
        kind = F32
    return pl.pallas_call(
        functools.partial(back_kernel, streams),
        grid_spec=pltpu.PrefetchScalarGridSpec(
            num_scalar_prefetch=1,
            grid=(steps,),
            in_specs=in_specs,
            out_specs=pl.BlockSpec((block, count), lambda i, plan_ref: (i, 0)),
        ),
        out_shape=jax.ShapeDtypeStruct((width, count), kind),
        compiler_params=params(),
        cost_estimate=cost(2 * rows * width * count, 4 * rows * width + 4 * width * count),
        name="back_product",
    )(plan, *args)


def gram_kernel(scale, block, first, at_ref, gram_ref, left_ref, right_ref, *rest):
    out_ref, copy_ref = rest[-2:]
    strip = copy_ref.shape[1] // 3
    cols = gram_ref.shape[1]
    lower = ((first + pl.program_id(0)) * block >= strip).astype(jnp.int32)
    left = left_ref[...]
    for s in range(cols // strip):
        part = slice(s * strip, (s + 1) * strip)
        product = dot(left, right_ref[:, part], ((0,), (0,)))
        out_ref[:, part] = decay_rate * gram_ref[:, part] + scale * product

    start = at_ref[0] + (first + pl.program_id(0)) * block

    @pl.when((start >= 0) & (start < cols))
    def _():
        here = lax.broadcasted_iota(jnp.int32, (block, block), 0)
        here = here == lax.broadcasted_iota(jnp.int32, (block, block), 1)
        place = pl.ds(pl.multiple_of(start, block), block)
        out_ref[:, place] = out_ref[:, place] + jnp.where(here, damping, 0.0)

    for k in range(3):
        wanted = at_ref[1 + 3 * lower + k]

        @pl.when(wanted >= 0)
        def _(k=k, wanted=wanted):
            place = pl.ds(pl.multiple_of(wanted * strip, strip), strip)
            copy_ref[:, k * strip : (k + 1) * strip] = out_ref[:, place].astype(BF)


def update_gram(at, gram, left, right, scale, first, count, block, before):
    rows, cols = gram.shape
    examples = left.shape[0]
    width = 3 * (cols // 4)
    in_specs = [
        pl.BlockSpec((block, cols), lambda i, at_ref: (first + i, 0)),
        pl.BlockSpec((examples, block), lambda i, at_ref: (0, first + i)),
        pl.BlockSpec((examples, cols), lambda i, at_ref: (0, 0)),
    ]
    args = [gram, left, right]
    alias = {}
    if before is not None:
        in_specs.append(pl.BlockSpec(memory_space=pl.ANY))
        args.append(before)
        alias = {4: 0}
    return pl.pallas_call(
        functools.partial(gram_kernel, scale, block, first),
        grid_spec=pltpu.PrefetchScalarGridSpec(
            num_scalar_prefetch=1,
            grid=(count,),
            in_specs=in_specs,
            out_specs=[
                pl.BlockSpec((block, cols), lambda i, at_ref: (first + i, 0)),
                pl.BlockSpec((block, width), lambda i, at_ref: (i, 0)),
            ],
        ),
        out_shape=[
            jax.ShapeDtypeStruct((rows, cols), F32),
            jax.ShapeDtypeStruct((count * block, width), BF),
        ],
        input_output_aliases=alias,
        compiler_params=params(30),
        cost_estimate=cost(2 * count * block * cols * examples, 8 * count * block * cols),
        name="update_gram",
    )(at, *args)


def tail_kernel(scale, even, pieces, plan_ref, *refs):
    same_ref, other_ref, mate_ref, came_ref, rest_ref = refs[:5]
    tiers, piece, count = same_ref.shape
    depth = tiers * piece
    width = depth // 2
    col_ref, row_ref, query_ref = refs[5:8]
    copy_refs, inner_refs = refs[8 : 8 + pieces], refs[8 + pieces : 8 + pieces + tiers]
    mapped_ref, total_ref, vec_same_ref, vec_other_ref, sums_ref = refs[8 + pieces + tiers :]
    inner = sum(ref[...].astype(F32) for ref in reversed(inner_refs))
    inner = (scale * inner).astype(BF)
    tier, y = plan_ref[0], plan_ref[1]
    near, source = plan_ref[6] == 1, plan_ref[7] == 1
    along, square = jnp.zeros((8, count), F32), jnp.zeros((8, count), F32)
    norm = jnp.zeros((8, count), F32)

    def fold(value):
        return jnp.sum(value.reshape(value.shape[0] // 8, 8, count), axis=0)

    def low_rank(ref, start):
        part = ref[:, pl.ds(pl.multiple_of(start * piece, piece), piece)]
        return dot(part, inner, ((0,), (0,)))

    for s in range(tiers):
        quarter = lax.rem(tier - s + tiers, tiers)
        rows = pl.ds(pl.multiple_of(quarter * piece, piece), piece)
        own = same_ref[s].astype(F32)
        value = own + low_rank(col_ref, y * tiers + quarter)
        vec_same_ref[rows, :] = value.astype(BF)
        value = other_ref[s].astype(F32) + low_rank(col_ref, (1 - y) * tiers + quarter)
        vec_other_ref[rows, :] = value.astype(BF)
        here = plan_ref[8] == s // (tiers // 2)
        got = jnp.where(here, came_ref[s % (tiers // 2)], rest_ref[s % (tiers // 2)]).astype(F32)
        got = jnp.where(near, jnp.where(source, own, mate_ref[s].astype(F32)), got)
        value = got + low_rank(row_ref, quarter)
        mapped_ref[rows, :] = value
        query = query_ref[rows, :]
        norm += fold(query * query)
        along += fold(query * value)
        square += fold(value * value)

    def take(ref, quadrant):
        return ref[pl.ds(pl.multiple_of(quadrant * width, width), width), :]

    sums_ref[0] = even * norm
    sums_ref[1] = even * along
    sums_ref[2] = even * square
    sums_ref[3] = jnp.zeros_like(norm)
    weight = plan_ref[4].astype(F32)
    cuts = [(k, h) for k in range(pieces) for h in range(tiers // pieces)]

    def left(k, h):
        start = (k * (tiers // pieces) + h) * piece
        return mapped_ref[start : start + piece, :]

    for k, h in cuts:
        upper = (k * (tiers // pieces) + h) * 2 // tiers
        rows = slice(h * piece, (h + 1) * piece)
        total = weight * dot(copy_refs[k][rows, :width], take(vec_same_ref, upper ^ plan_ref[2]))
        total += 2.0 * dot(
            copy_refs[k][rows, width : 2 * width], take(vec_other_ref, upper ^ plan_ref[3])
        )
        sums_ref[3] += fold(total * left(k, h))

    @pl.when(plan_ref[5] == 1)
    def _():
        for k, h in cuts[: len(cuts) // 2]:
            rows = slice(h * piece, (h + 1) * piece)
            total = 2.0 * dot(copy_refs[k][rows, 2 * width :], vec_same_ref[width:, :])
            sums_ref[3] += fold(total * left(k, h))

    total_ref[...] = jnp.sum(sums_ref[...], axis=1)


def tail(plan, same, other, found, grads_col, grads_row, inner, queries, copies, scale, even):
    rows, count = queries.shape
    args = [same, other, *found, grads_col, grads_row, queries, *copies, *inner]
    return pl.pallas_call(
        functools.partial(tail_kernel, scale, even, len(copies)),
        in_specs=[pl.BlockSpec(memory_space=pltpu.SMEM)]
        + [pl.BlockSpec(memory_space=pltpu.VMEM)] * len(args),
        out_specs=[pl.BlockSpec(memory_space=pltpu.VMEM)] * 2,
        out_shape=[
            jax.ShapeDtypeStruct((rows, count), F32),
            jax.ShapeDtypeStruct((4, count), F32),
        ],
        scratch_shapes=[
            pltpu.VMEM((rows, count), BF),
            pltpu.VMEM((rows, count), BF),
            pltpu.VMEM((4, 8, count), F32),
        ],
        compiler_params=params(16),
        cost_estimate=cost(4 * rows * rows * count, 4 * rows * rows),
        name="tail",
    )(plan, *args)


def after(value, *others):
    return lax.optimization_barrier((value,) + others)[0]


def integers(*values):
    return jnp.stack([jnp.asarray(v).astype(jnp.int32) for v in values])


def shards(activations, out_grads, proj_in, proj_out, lengths, gram_old, queries):
    local_count = lengths.shape[0]
    rank = proj_in.shape[1]
    row_count = lax.axis_size("row")
    col_count = lax.axis_size("col")
    rows, cols = gram_old.shape
    count = queries.shape[1]
    tokens = local_count * SEQ
    tiers = row_count // 2
    files = col_count // 2
    piece = rows // tiers
    row = lax.axis_index("row")
    col = lax.axis_index("col")
    z, y = row // 2, row % 2
    x, core = col // 2, col % 2
    total_examples = local_count * row_count * col_count
    scale = (1.0 - decay_rate) / total_examples

    def move(value, goes):
        pairs = []
        for r in range(row_count):
            for c in range(col_count):
                to = goes(r // 2, r % 2, c // 2, c % 2)
                if to is not None:
                    pairs.append((r * col_count + c, (to[0] * 2 + to[1]) * col_count + to[2] * 2 + to[3]))
        return lax.ppermute(value, ("row", "col"), pairs)

    def swap_y(value):
        return move(value, lambda z, y, x, k: (z, 1 - y, x, k))

    def swap_core(value):
        return move(value, lambda z, y, x, k: (z, y, x, 1 - k))

    def ring_z(value, by=1):
        return move(value, lambda z, y, x, k: ((z + by) % tiers, y, x, k))

    def ring_x(value):
        return move(value, lambda z, y, x, k: (z, y, (x + 1) % files, k))

    def flip_x(value, bit):
        return move(value, lambda z, y, x, k: (z, y, x ^ bit, k))

    def spread_z(value):
        return [value] + [ring_z(value, by) for by in range(1, tiers)]

    vec = queries.astype(BF).T
    away = back_product(integers(1 - y, 0), vec, gram_old)
    come = swap_y(away)

    low_in = dot(activations, proj_in).astype(BF)
    low_out = dot(proj_out, out_grads, ((0,), (1,))).astype(BF)
    slot = jnp.arange(tokens, dtype=jnp.int32)
    valid_mask = slot % SEQ < jnp.repeat(lengths, SEQ)
    low_out = jnp.where(valid_mask[None, :], low_out, jnp.zeros((), BF))
    low_out = low_out.reshape(rank, tokens // rank, rank).transpose(1, 0, 2).reshape(tokens, rank)
    local = after(jnp.concatenate([low_in, low_out], axis=0), away)
    factors = spread_z(local)

    here = back_product(after(integers(y, z == col), local), vec, gram_old, queries)
    here = here.reshape(tiers, piece, count)
    come = come.reshape(tiers, piece, count)

    def piece_for(by):
        at = (z + by) % tiers
        one = lax.dynamic_index_in_dim(here, at, 0, keepdims=False)
        two = lax.dynamic_index_in_dim(come, at, 0, keepdims=False)
        return one + two.astype(F32)

    sends = [piece_for(by).astype(BF) for by in range(1, tiers)]
    parts = [ring_z(sends[by - 1], by) for by in range(1, tiers)]

    factors = jnp.stack(lax.optimization_barrier((*factors, here))[:tiers])
    across = [factors]
    for dx in range(1, files):
        across.append(move(factors, lambda z, y, x, k: (z, y, (x + dx) % files, k)))
    own = []
    for one in across:
        own.append(one)
        own.append(swap_y(after(one, *sends)))

    total = piece_for(0)
    for part in parts:
        total = total + part.astype(F32)
    short = total.astype(BF)

    same = spread_z(short)
    held = lax.optimization_barrier((*own, short))[:-1]
    mate = [swap_core(f) for f in held]
    grads_col, grads_row = build_grads(integers(row, col), held, mate, rows, cols)
    partial = dot(grads_row, queries.astype(BF))
    fetched = swap_y(partial.astype(BF))
    same = lax.optimization_barrier((*same, fetched, partial))[:-1]
    fetched = same[-1]
    stacked = jnp.stack(same[:-1])
    inner = (partial + fetched.astype(F32)).astype(BF)
    sums = spread_z(inner)
    other = swap_y(stacked)

    fellow = swap_core(stacked)
    cut = tiers // 2
    half = lax.dynamic_slice_in_dim(
        jnp.where(core == z % 2, stacked, fellow), core * cut, cut, 0
    )
    found = [fellow]
    for flip in range(2):
        came = half
        for dx in range(1, files):
            got = move(half, lambda z, y, x, k: (z, y, (x + dx) % files, k ^ flip))
            came = got if files == 2 else jnp.where((x - dx) % files == z // 2, got, came)
        found.append(came)

    flags = integers(row > 2 * col + y, row > 2 * col + 1 - y)
    block = min(256, rows // 4)
    at = integers(
        row * rows - col * cols,
        2 * y + flags[0],
        2 * (1 - y) + flags[1],
        jnp.where(z == col, 2 * y + 1, -1),
        2 * y + 1 - flags[0],
        2 * (1 - y) + 1 - flags[1],
        -1,
    )
    gram_new, copy = update_gram(
        after(at, half), gram_old, grads_row, grads_col, scale, 0, rows // block, block, None
    )
    held = lax.optimization_barrier((*found[1:], *sums, gram_new))
    found, sums = [fellow, *held[:2]], held[2:-1]
    plan = jnp.concatenate(
        [
            integers(z, y),
            flags,
            integers(jnp.where(z == col, 1, 2), z == col, x == z // 2, core == z % 2, core),
        ]
    )
    mapped, sums = tail(
        after(plan, gram_new), stacked, other, found, grads_col, grads_row, sums, queries,
        [copy], scale, 1.0 / col_count,
    )
    sums = sums + swap_core(sums)
    bit = 1
    while bit < files:
        sums = sums + flip_x(sums, bit)
        bit *= 2
    sums = sums + swap_y(sums)
    around = jnp.stack(spread_z(sums))
    sums = sum(
        lax.dynamic_index_in_dim(around, (z - k) % tiers, 0, keepdims=False) for k in range(tiers)
    )
    norm_now, along, square, curve = sums[0], sums[1], sums[2], sums[3]
    step = norm_now / along
    norm_next = step * step * square - norm_now
    momentum = norm_next / norm_now
    curvature = along - 2.0 * step * square + step * step * curve
    step_next = norm_next / (curvature - momentum * norm_next / step)
    solution = (step + step_next * (1.0 + momentum)) * queries - (step_next * step) * mapped
    return (gram_new, solution)


def solution(mesh):
    in_specs = (
        P(("row", "col"), None),
        P(("row", "col"), None),
        P(),
        P(),
        P(("row", "col")),
        P("row", "col"),
        P("row", None),
    )
    out_specs = (P("row", "col"), P("row", None))
    return jax.shard_map(shards, mesh=mesh, in_specs=in_specs, out_specs=out_specs, check_vma=False)
```

```python
import functools

import jax
import jax.numpy as jnp
from jax import lax
from jax.experimental import pallas as pl
from jax.experimental.pallas import tpu as pltpu
from jax.sharding import PartitionSpec as P

SEQ = 32

decay_rate = 0.5
damping = 1.0

BF = jnp.bfloat16
F32 = jnp.float32
VMEM_BYTES = 40 * 1024 * 1024


def dot(a, b, dims=((1,), (0,))):
    return lax.dot_general(a, b, (dims, ((), ())), preferred_element_type=F32)


def params(mebibytes=24):
    return pltpu.CompilerParams(vmem_limit_bytes=mebibytes * 1024 * 1024)


def cost(flops, moved):
    return pl.CostEstimate(flops=flops, bytes_accessed=moved, transcendentals=0)


def grads_kernel(parts, outs_col, outs_row, at_ref, *refs):
    own_refs, mate_refs = refs[:parts], refs[parts : 2 * parts]
    col_ref, row_ref, rows_ref, picked_ref = refs[2 * parts :]
    tiers, depth, rank = own_refs[0].shape
    tokens = depth // 2
    slots = tokens // SEQ
    halves = tokens // rank
    outs = outs_col + outs_row
    files = parts // 2
    z, y, x = at_ref[0] // 2, at_ref[0] % 2, at_ref[1] // 2
    even = at_ref[1] % 2 == 0
    example = lax.broadcasted_iota(jnp.int32, (slots, rank), 0)
    token = lax.broadcasted_iota(jnp.int32, (slots, rank), 1)
    masks = [((token + h * rank) // SEQ == example).astype(F32) for h in range(halves)]
    col_at = pl.multiple_of(at_ref[1] * outs_col, outs_col)
    row_at = pl.multiple_of(at_ref[0] * outs_row, outs_row)

    def build(k, low_in):
        left = []
        for h in range(halves):
            picked_ref[k, h, :outs_col, :] = rows_ref[k, pl.ds(h * rank + col_at, outs_col), :]
            picked_ref[k, h, outs_col:, :] = rows_ref[k, pl.ds(h * rank + row_at, outs_row), :]
        for h in range(halves):
            rows = picked_ref[k, h]
            spread = rows[:, None, :] * masks[h][None, :, :]
            left.append(spread.reshape(outs * slots, rank).astype(BF))
        left = jnp.concatenate(left, axis=1)
        return dot(left, low_in).reshape(outs, slots, rank)

    for part in range(parts):
        from_x = lax.rem(x - part // 2 + files, files)

        def chunk(i, carry, part=part, from_x=from_x):
            own, mate = own_refs[part][i], mate_refs[part][i]
            rows_ref[0] = jnp.where(even, own[tokens:, :], mate[tokens:, :]).astype(F32)
            rows_ref[1] = jnp.where(even, mate[tokens:, :], own[tokens:, :]).astype(F32)
            first = jnp.where(even, own[:tokens, :], mate[:tokens, :])
            second = jnp.where(even, mate[:tokens, :], own[:tokens, :])
            both = jnp.concatenate([build(0, first), build(1, second)], axis=1).astype(BF)
            from_z = lax.rem(z - i + tiers, tiers)
            place = ((from_x * tiers + from_z) * 2 + (y ^ (part % 2))) * (2 * slots)
            place = pl.ds(pl.multiple_of(place, 2 * slots), 2 * slots)
            for o in range(outs_col):
                col_ref[place, o * rank : (o + 1) * rank] = both[o]
            for o in range(outs_row):
                row_ref[place, o * rank : (o + 1) * rank] = both[outs_col + o]
            return carry

        lax.fori_loop(0, tiers, chunk, 0)


def build_grads(place, own, mate, rows, cols):
    parts = len(own)
    tiers, depth, rank = own[0].shape
    tokens = depth // 2
    total = 2 * parts * tiers * tokens // SEQ
    return pl.pallas_call(
        functools.partial(grads_kernel, parts, cols // rank, rows // rank),
        in_specs=[pl.BlockSpec(memory_space=pltpu.SMEM)]
        + [pl.BlockSpec(memory_space=pltpu.VMEM)] * (2 * parts),
        out_specs=[pl.BlockSpec(memory_space=pltpu.VMEM)] * 2,
        out_shape=[
            jax.ShapeDtypeStruct((total, cols), BF),
            jax.ShapeDtypeStruct((total, rows), BF),
        ],
        scratch_shapes=[
            pltpu.VMEM((2, tokens, rank), F32),
            pltpu.VMEM((2, tokens // rank, (cols + rows) // rank, rank), F32),
        ],
        compiler_params=params(16),
        cost_estimate=cost(2 * total * (rows + cols) * tokens, 2 * total * (rows + cols)),
        name="build_grads",
    )(place, *own, *mate)


def back_kernel(streams, plan_ref, *refs):
    vec_ref, gram_refs, out_ref = refs[0], refs[1 : 1 + streams], refs[-1]
    depth = gram_refs[0].shape[0]
    total = None
    for s in range(streams):
        vec = vec_ref[:, s * depth : (s + 1) * depth]
        value = dot(vec, gram_refs[s][...].astype(BF))
        total = value if total is None else total + value
    total = decay_rate * total.T
    if len(refs) > streams + 2:
        own = jnp.where(plan_ref[1] == 1, damping, 0.0)
        total = total + own * refs[streams + 1][...]
    out_ref[...] = total.astype(out_ref.dtype)


def back_product(plan, vec, gram, queries=None):
    count, rows = vec.shape
    width = gram.shape[1] // 2
    block = min(512, width)
    steps = width // block
    streams = 2
    depth = rows // streams

    def gram_at(s, i, plan_ref):
        return (s, plan_ref[0] * steps + i)

    in_specs = [pl.BlockSpec((count, rows), lambda i, plan_ref: (0, 0))]
    for s in range(streams):
        in_specs.append(pl.BlockSpec((depth, block), functools.partial(gram_at, s)))
    args = [vec] + [gram] * streams
    kind = BF
    if queries is not None:
        in_specs.append(pl.BlockSpec((block, count), lambda i, plan_ref: (i, 0)))
        args.append(queries)
        kind = F32
    return pl.pallas_call(
        functools.partial(back_kernel, streams),
        grid_spec=pltpu.PrefetchScalarGridSpec(
            num_scalar_prefetch=1,
            grid=(steps,),
            in_specs=in_specs,
            out_specs=pl.BlockSpec((block, count), lambda i, plan_ref: (i, 0)),
        ),
        out_shape=jax.ShapeDtypeStruct((width, count), kind),
        compiler_params=params(),
        cost_estimate=cost(2 * rows * width * count, 4 * rows * width + 4 * width * count),
        name="back_product",
    )(plan, *args)


def gram_kernel(scale, block, first, at_ref, gram_ref, left_ref, right_ref, *rest):
    out_ref, copy_ref = rest[-2:]
    strip = copy_ref.shape[1] // 3
    cols = gram_ref.shape[1]
    lower = ((first + pl.program_id(0)) * block >= strip).astype(jnp.int32)
    left = left_ref[...]
    for s in range(cols // strip):
        part = slice(s * strip, (s + 1) * strip)
        product = dot(left, right_ref[:, part], ((0,), (0,)))
        out_ref[:, part] = decay_rate * gram_ref[:, part] + scale * product

    start = at_ref[0] + (first + pl.program_id(0)) * block

    @pl.when((start >= 0) & (start < cols))
    def _():
        here = lax.broadcasted_iota(jnp.int32, (block, block), 0)
        here = here == lax.broadcasted_iota(jnp.int32, (block, block), 1)
        place = pl.ds(pl.multiple_of(start, block), block)
        out_ref[:, place] = out_ref[:, place] + jnp.where(here, damping, 0.0)

    for k in range(3):
        wanted = at_ref[1 + 3 * lower + k]

        @pl.when(wanted >= 0)
        def _(k=k, wanted=wanted):
            place = pl.ds(pl.multiple_of(wanted * strip, strip), strip)
            copy_ref[:, k * strip : (k + 1) * strip] = out_ref[:, place].astype(BF)


def update_gram(at, gram, left, right, scale, first, count, block, before):
    rows, cols = gram.shape
    examples = left.shape[0]
    width = 3 * (cols // 4)
    in_specs = [
        pl.BlockSpec((block, cols), lambda i, at_ref: (first + i, 0)),
        pl.BlockSpec((examples, block), lambda i, at_ref: (0, first + i)),
        pl.BlockSpec((examples, cols), lambda i, at_ref: (0, 0)),
    ]
    args = [gram, left, right]
    alias = {}
    if before is not None:
        in_specs.append(pl.BlockSpec(memory_space=pl.ANY))
        args.append(before)
        alias = {4: 0}
    return pl.pallas_call(
        functools.partial(gram_kernel, scale, block, first),
        grid_spec=pltpu.PrefetchScalarGridSpec(
            num_scalar_prefetch=1,
            grid=(count,),
            in_specs=in_specs,
            out_specs=[
                pl.BlockSpec((block, cols), lambda i, at_ref: (first + i, 0)),
                pl.BlockSpec((block, width), lambda i, at_ref: (i, 0)),
            ],
        ),
        out_shape=[
            jax.ShapeDtypeStruct((rows, cols), F32),
            jax.ShapeDtypeStruct((count * block, width), BF),
        ],
        input_output_aliases=alias,
        compiler_params=params(30),
        cost_estimate=cost(2 * count * block * cols * examples, 8 * count * block * cols),
        name="update_gram",
    )(at, *args)


def tail_kernel(scale, even, pieces, plan_ref, *refs):
    same_ref, other_ref, mate_ref, came_ref, rest_ref = refs[:5]
    tiers, piece, count = same_ref.shape
    depth = tiers * piece
    width = depth // 2
    col_ref, row_ref, query_ref = refs[5:8]
    copy_refs, inner_refs = refs[8 : 8 + pieces], refs[8 + pieces : 8 + pieces + tiers]
    mapped_ref, total_ref, vec_same_ref, vec_other_ref, sums_ref = refs[8 + pieces + tiers :]
    inner = sum(ref[...].astype(F32) for ref in reversed(inner_refs))
    inner = (scale * inner).astype(BF)
    tier, y = plan_ref[0], plan_ref[1]
    near, source = plan_ref[6] == 1, plan_ref[7] == 1
    along, square = jnp.zeros((8, count), F32), jnp.zeros((8, count), F32)
    norm = jnp.zeros((8, count), F32)

    def fold(value):
        return jnp.sum(value.reshape(value.shape[0] // 8, 8, count), axis=0)

    def low_rank(ref, start):
        part = ref[:, pl.ds(pl.multiple_of(start * piece, piece), piece)]
        return dot(part, inner, ((0,), (0,)))

    for s in range(tiers):
        quarter = lax.rem(tier - s + tiers, tiers)
        rows = pl.ds(pl.multiple_of(quarter * piece, piece), piece)
        own = same_ref[s].astype(F32)
        value = own + low_rank(col_ref, y * tiers + quarter)
        vec_same_ref[rows, :] = value.astype(BF)
        value = other_ref[s].astype(F32) + low_rank(col_ref, (1 - y) * tiers + quarter)
        vec_other_ref[rows, :] = value.astype(BF)
        here = plan_ref[8] == s // (tiers // 2)
        got = jnp.where(here, came_ref[s % (tiers // 2)], rest_ref[s % (tiers // 2)]).astype(F32)
        got = jnp.where(near, jnp.where(source, own, mate_ref[s].astype(F32)), got)
        value = got + low_rank(row_ref, quarter)
        mapped_ref[rows, :] = value
        query = query_ref[rows, :]
        norm += fold(query * query)
        along += fold(query * value)
        square += fold(value * value)

    def take(ref, quadrant):
        return ref[pl.ds(pl.multiple_of(quadrant * width, width), width), :]

    sums_ref[0] = even * norm
    sums_ref[1] = even * along
    sums_ref[2] = even * square
    sums_ref[3] = jnp.zeros_like(norm)
    weight = plan_ref[4].astype(F32)
    cuts = [(k, h) for k in range(pieces) for h in range(tiers // pieces)]

    def left(k, h):
        start = (k * (tiers // pieces) + h) * piece
        return mapped_ref[start : start + piece, :]

    for k, h in cuts:
        upper = (k * (tiers // pieces) + h) * 2 // tiers
        rows = slice(h * piece, (h + 1) * piece)
        total = weight * dot(copy_refs[k][rows, :width], take(vec_same_ref, upper ^ plan_ref[2]))
        total += 2.0 * dot(
            copy_refs[k][rows, width : 2 * width], take(vec_other_ref, upper ^ plan_ref[3])
        )
        sums_ref[3] += fold(total * left(k, h))

    @pl.when(plan_ref[5] == 1)
    def _():
        for k, h in cuts[: len(cuts) // 2]:
            rows = slice(h * piece, (h + 1) * piece)
            total = 2.0 * dot(copy_refs[k][rows, 2 * width :], vec_same_ref[width:, :])
            sums_ref[3] += fold(total * left(k, h))

    total_ref[...] = jnp.sum(sums_ref[...], axis=1)


def tail(plan, same, other, found, grads_col, grads_row, inner, queries, copies, scale, even):
    rows, count = queries.shape
    args = [same, other, *found, grads_col, grads_row, queries, *copies, *inner]
    return pl.pallas_call(
        functools.partial(tail_kernel, scale, even, len(copies)),
        in_specs=[pl.BlockSpec(memory_space=pltpu.SMEM)]
        + [pl.BlockSpec(memory_space=pltpu.VMEM)] * len(args),
        out_specs=[pl.BlockSpec(memory_space=pltpu.VMEM)] * 2,
        out_shape=[
            jax.ShapeDtypeStruct((rows, count), F32),
            jax.ShapeDtypeStruct((4, count), F32),
        ],
        scratch_shapes=[
            pltpu.VMEM((rows, count), BF),
            pltpu.VMEM((rows, count), BF),
            pltpu.VMEM((4, 8, count), F32),
        ],
        compiler_params=params(16),
        cost_estimate=cost(4 * rows * rows * count, 4 * rows * rows),
        name="tail",
    )(plan, *args)


def after(value, *others):
    return lax.optimization_barrier((value,) + others)[0]


def integers(*values):
    return jnp.stack([jnp.asarray(v).astype(jnp.int32) for v in values])


def shards(activations, out_grads, proj_in, proj_out, lengths, gram_old, queries):
    local_count = lengths.shape[0]
    rank = proj_in.shape[1]
    row_count = lax.axis_size("row")
    col_count = lax.axis_size("col")
    rows, cols = gram_old.shape
    count = queries.shape[1]
    tokens = local_count * SEQ
    tiers = row_count // 2
    files = col_count // 2
    piece = rows // tiers
    row = lax.axis_index("row")
    col = lax.axis_index("col")
    z, y = row // 2, row % 2
    x, core = col // 2, col % 2
    total_examples = local_count * row_count * col_count
    scale = (1.0 - decay_rate) / total_examples

    def move(value, goes):
        pairs = []
        for r in range(row_count):
            for c in range(col_count):
                to = goes(r // 2, r % 2, c // 2, c % 2)
                if to is not None:
                    pairs.append((r * col_count + c, (to[0] * 2 + to[1]) * col_count + to[2] * 2 + to[3]))
        return lax.ppermute(value, ("row", "col"), pairs)

    def swap_y(value):
        return move(value, lambda z, y, x, k: (z, 1 - y, x, k))

    def swap_core(value):
        return move(value, lambda z, y, x, k: (z, y, x, 1 - k))

    def ring_z(value, by=1):
        return move(value, lambda z, y, x, k: ((z + by) % tiers, y, x, k))

    def ring_x(value):
        return move(value, lambda z, y, x, k: (z, y, (x + 1) % files, k))

    def flip_x(value, bit):
        return move(value, lambda z, y, x, k: (z, y, x ^ bit, k))

    def spread_z(value):
        return [value] + [ring_z(value, by) for by in range(1, tiers)]

    vec = queries.astype(BF).T
    away = back_product(integers(1 - y, 0), vec, gram_old)
    come = swap_y(away)

    low_in = dot(activations, proj_in).astype(BF)
    low_out = dot(proj_out, out_grads, ((0,), (1,))).astype(BF)
    slot = jnp.arange(tokens, dtype=jnp.int32)
    valid_mask = slot % SEQ < jnp.repeat(lengths, SEQ)
    low_out = jnp.where(valid_mask[None, :], low_out, jnp.zeros((), BF))
    low_out = low_out.reshape(rank, tokens // rank, rank).transpose(1, 0, 2).reshape(tokens, rank)
    local = after(jnp.concatenate([low_in, low_out], axis=0), away)
    factors = spread_z(local)

    here = back_product(after(integers(y, z == col), local), vec, gram_old, queries)
    here = here.reshape(tiers, piece, count)
    come = come.reshape(tiers, piece, count)

    def piece_for(by):
        at = (z + by) % tiers
        one = lax.dynamic_index_in_dim(here, at, 0, keepdims=False)
        two = lax.dynamic_index_in_dim(come, at, 0, keepdims=False)
        return one + two.astype(F32)

    sends = [piece_for(by).astype(BF) for by in range(1, tiers)]
    parts = [ring_z(sends[by - 1], by) for by in range(1, tiers)]

    factors = jnp.stack(lax.optimization_barrier((*factors, here))[:tiers])
    across = [factors]
    for dx in range(1, files):
        across.append(move(factors, lambda z, y, x, k: (z, y, (x + dx) % files, k)))
    own = []
    for one in across:
        own.append(one)
        own.append(swap_y(after(one, *sends)))

    total = piece_for(0)
    for part in parts:
        total = total + part.astype(F32)
    short = total.astype(BF)

    same = spread_z(short)
    held = lax.optimization_barrier((*own, short))[:-1]
    mate = [swap_core(f) for f in held]
    grads_col, grads_row = build_grads(integers(row, col), held, mate, rows, cols)
    partial = dot(grads_row, queries.astype(BF))
    fetched = swap_y(partial.astype(BF))
    same = lax.optimization_barrier((*same, fetched, partial))[:-1]
    fetched = same[-1]
    stacked = jnp.stack(same[:-1])
    inner = (partial + fetched.astype(F32)).astype(BF)
    sums = spread_z(inner)
    other = swap_y(stacked)

    fellow = swap_core(stacked)
    cut = tiers // 2
    half = lax.dynamic_slice_in_dim(
        jnp.where(core == z % 2, stacked, fellow), core * cut, cut, 0
    )
    found = [fellow]
    for flip in range(2):
        came = half
        for dx in range(1, files):
            got = move(half, lambda z, y, x, k: (z, y, (x + dx) % files, k ^ flip))
            came = got if files == 2 else jnp.where((x - dx) % files == z // 2, got, came)
        found.append(came)

    flags = integers(row > 2 * col + y, row > 2 * col + 1 - y)
    block = min(256, rows // 4)
    at = integers(
        row * rows - col * cols,
        2 * y + flags[0],
        2 * (1 - y) + flags[1],
        jnp.where(z == col, 2 * y + 1, -1),
        2 * y + 1 - flags[0],
        2 * (1 - y) + 1 - flags[1],
        -1,
    )
    gram_new, copy = update_gram(
        after(at, half), gram_old, grads_row, grads_col, scale, 0, rows // block, block, None
    )
    held = lax.optimization_barrier((*found[1:], *sums, gram_new))
    found, sums = [fellow, *held[:2]], held[2:-1]
    plan = jnp.concatenate(
        [
            integers(z, y),
            flags,
            integers(jnp.where(z == col, 1, 2), z == col, x == z // 2, core == z % 2, core),
        ]
    )
    mapped, sums = tail(
        after(plan, gram_new), stacked, other, found, grads_col, grads_row, sums, queries,
        [copy], scale, 1.0 / col_count,
    )
    if files == 2:
        across = move(sums, lambda z, y, x, k: (z, y, x ^ 1, 1 - k))
        sums = (sums + swap_core(sums)) + (flip_x(sums, 1) + across)
    else:
        sums = sums + swap_core(sums)
        bit = 1
        while bit < files:
            sums = sums + flip_x(sums, bit)
            bit *= 2
    sums = sums + swap_y(sums)
    around = jnp.stack(spread_z(sums))
    sums = sum(
        lax.dynamic_index_in_dim(around, (z - k) % tiers, 0, keepdims=False) for k in range(tiers)
    )
    norm_now, along, square, curve = sums[0], sums[1], sums[2], sums[3]
    step = norm_now / along
    norm_next = step * step * square - norm_now
    momentum = norm_next / norm_now
    curvature = along - 2.0 * step * square + step * step * curve
    step_next = norm_next / (curvature - momentum * norm_next / step)
    solution = (step + step_next * (1.0 + momentum)) * queries - (step_next * step) * mapped
    return (gram_new, solution)


def solution(mesh):
    in_specs = (
        P(("row", "col"), None),
        P(("row", "col"), None),
        P(),
        P(),
        P(("row", "col")),
        P("row", "col"),
        P("row", None),
    )
    out_specs = (P("row", "col"), P("row", None))
    return jax.shard_map(shards, mesh=mesh, in_specs=in_specs, out_specs=out_specs, check_vma=False)
```
